512 devices in a mesh: dp: 8 (over z_lo), chan: 4 (over z_hi, core), seq: 16 (over y, x).
Axes of the slice: x: 4, y: 4, z: 16 (z_hi: 2, z_lo: 8; z = z_hi * 8 + z_lo), core: 2. Of those that a mesh axis runs over, the one named last changes fastest.
Arguments:
- query_in: bfloat16 [8, 2048, 4096], P('dp', 'seq', 'chan'), may hold values from -6 to 6
- key_in: bfloat16 [8, 2048, 4096], P('dp', 'seq', 'chan'), may hold values from -6 to 6
- value_in: bfloat16 [8, 2048, 4096], P('dp', 'seq', 'chan'), may hold values from -6 to 6
- filter_taps: bfloat16 [2048, 4096], P('seq', 'chan'), may hold values from -1 to 1
- skip_gain: float32 [4096], P('chan'), may hold values from -4 to 4
- grad_out: bfloat16 [8, 2048, 4096], P('dp', 'seq', 'chan'), may hold values from -6 to 6
Outputs:
- mixed_out: bfloat16 [8, 2048, 4096], P('dp', 'seq', 'chan')
- grad_query: bfloat16 [8, 2048, 4096], P('dp', 'seq', 'chan')
- grad_key: bfloat16 [8, 2048, 4096], P('dp', 'seq', 'chan')
- grad_value: bfloat16 [8, 2048, 4096], P('dp', 'seq', 'chan')
- grad_filter: bfloat16 [2048, 4096], P('seq', 'chan')
The draws below stay inside these ranges and needn't reach their ends.
All inputs are finite; a program needn't handle non-finite values.
Results may differ from the reference program's by a relative error of at most 0.017.
Values may be sent and summed in bfloat16 or wider, within the bound.
No kernel may reach another device: no remote copies, remote signals or barrier semaphores. Data moves between devices by JAX's collectives and lax.ppermute only.
A program may use at most 64 MiB of HBM per device.

```python
import math
import jax
import jax.numpy as jnp
from jax import lax

D = 4096
SEQ_LEN = 2048
BATCH = 8


def draw_filter_taps(key, part):
    key = jax.random.fold_in(key, 7)
    span_key, noise_key = jax.random.split(key)
    low_log = math.log(32.0)
    high_log = math.log(SEQ_LEN * 4.0)
    spans = jnp.exp(jax.random.uniform(span_key, (D,), jnp.float32, low_log, high_log))
    lags = jnp.arange(SEQ_LEN, dtype=jnp.float32)[:, None]
    noise = jnp.clip(jax.random.normal(noise_key, (SEQ_LEN, D), jnp.float32), -4.0, 4.0)
    amplitude = 1.0 / jnp.sqrt(jnp.minimum(spans * 0.5 + 1.0, SEQ_LEN * 1.0))
    taps = noise * amplitude[None, :] * jnp.exp(-lags / spans[None, :])
    return taps.astype(jnp.bfloat16)


def block_levels(rng, dims, shards, low, top_value):
    gain, own = 1.0, jax.random.fold_in(rng, 6)
    for dim, parts in shards:
        draws = jnp.exp(jax.random.uniform(jax.random.fold_in(own, dim), (parts,), jnp.float32, low / len(shards), top_value / len(shards)))
        gain = gain * jnp.repeat(draws, dims[dim] // parts).reshape([-1 if axis == dim else 1 for axis in range(len(dims))])
    return gain


def centred(stream_key, shape, scale, most, pieces=(), kind=jnp.bfloat16):
    level = block_levels(stream_key, shape, pieces, -0.22, 0.18) if pieces else 1.0
    entries = jax.random.normal(stream_key, shape, jnp.float32) * scale * level
    return jnp.minimum(jnp.maximum(entries, -most), most).astype(kind)


def setup_inputs(seed: int = 0) -> dict:
    arg_keys = jax.random.split(jax.random.key(seed), 7)
    query_in = centred(arg_keys[0], (BATCH, SEQ_LEN, D), 1.0, 6.0, ((0, 8), (1, 16), (2, 4)))
    key_in = centred(arg_keys[1], (BATCH, SEQ_LEN, D), 1.0, 6.0, ((0, 8), (1, 16), (2, 4)))
    value_in = centred(arg_keys[2], (BATCH, SEQ_LEN, D), 1.0, 6.0, ((0, 8), (1, 16), (2, 4)))
    filter_taps = draw_filter_taps(jax.random.fold_in(arg_keys[6], 71), 0)
    skip_gain = centred(arg_keys[4], (D,), 1.0, 4.0, ((0, 4),), jnp.float32)
    grad_out = centred(arg_keys[5], (BATCH, SEQ_LEN, D), 1.0, 6.0, ((0, 8), (1, 16), (2, 4)))
    return {"query_in": query_in, "key_in": key_in, "value_in": value_in, "filter_taps": filter_taps, "skip_gain": skip_gain, "grad_out": grad_out}


def rounded(values):
    return lax.optimization_barrier(values.astype(jnp.bfloat16)).astype(jnp.float32)

def reference(query_in, key_in, value_in, filter_taps, skip_gain, grad_out):
    padded_len = 2 * SEQ_LEN
    taps_spec = jnp.fft.rfft(filter_taps.astype(jnp.float32), n=padded_len, axis=0)
    factor = 1.0 / math.sqrt(BATCH * SEQ_LEN)

    def per_sequence(inputs):
        query_row, key_row, value_row, grad_row = inputs
        query_float = query_row.astype(jnp.float32)
        key_float = key_row.astype(jnp.float32)
        value_float = value_row.astype(jnp.float32)
        grad_float = grad_row.astype(jnp.float32)
        mixed_in = rounded(key_float * value_float)
        mixed_spec = jnp.fft.rfft(mixed_in, n=padded_len, axis=0)
        convolved = jnp.fft.irfft(taps_spec * mixed_spec, n=padded_len, axis=0)[:SEQ_LEN]
        hyena_state = rounded(convolved + skip_gain[None, :] * mixed_in)
        mixed_out = (query_float * hyena_state).astype(jnp.bfloat16)
        grad_query = (grad_float * hyena_state).astype(jnp.bfloat16)
        grad_state = rounded(grad_float * query_float)
        grad_spec = jnp.fft.rfft(grad_state, n=padded_len, axis=0)
        back_mixed = jnp.fft.irfft(jnp.conj(taps_spec) * grad_spec, n=padded_len, axis=0)[:SEQ_LEN]
        grad_mixed = rounded(back_mixed + skip_gain[None, :] * grad_state)
        back_taps = jnp.fft.irfft(jnp.conj(mixed_spec) * grad_spec, n=padded_len, axis=0)[:SEQ_LEN]
        taps_term = rounded(factor * back_taps)
        grad_key = (grad_mixed * value_float).astype(jnp.bfloat16)
        grad_value = (grad_mixed * key_float).astype(jnp.bfloat16)
        return (mixed_out, grad_query, grad_key, grad_value, taps_term)
    results = lax.map(per_sequence, (query_in, key_in, value_in, grad_out))
    grad_filter = lax.optimization_barrier(jnp.sum(results[4], axis=0)).astype(jnp.bfloat16)
    return (results[0], results[1], results[2], results[3], grad_filter)
```

```python
import math

import jax
import jax.numpy as jnp
import numpy as np
from jax import lax
from jax.experimental import pallas as pl
from jax.experimental.pallas import tpu as pltpu
from jax.sharding import Mesh
from jax.sharding import PartitionSpec as P

F32 = jnp.float32
BF16 = jnp.bfloat16
LANES = 128
ROWS = 16
FREQS = 2 * ROWS
HALF = ROWS + 1
CHUNK = 16
VMEM_LIMIT = 48 * 1024 * 1024


def unit(numer, denom):
    angle = 2.0 * math.pi * numer / denom
    return (math.cos(angle), math.sin(angle))


def times_unit(value, numer, denom):
    re, im = value
    numer = numer % denom
    if 4 * numer % denom == 0:
        return ((re, im), (-im, re), (-re, -im), (im, -re))[4 * numer // denom]
    if 8 * numer % denom == 0:
        root = math.sqrt(0.5)
        summed, apart = (re + im) * root, (re - im) * root
        return {1: (apart, summed), 3: (-summed, apart), 5: (-apart, -summed), 7: (summed, -apart)}[
            8 * numer // denom
        ]
    cos, sin = unit(numer, denom)
    return (re * cos - im * sin, re * sin + im * cos)


def add(a, b):
    return (a[0] + b[0], a[1] + b[1])


def sub(a, b):
    return (a[0] - b[0], a[1] - b[1])


def conj(a):
    return (a[0], -a[1])


def complex_dft(values, sign):
    count = len(values)
    if count == 1:
        return list(values)
    even = complex_dft(values[0::2], sign)
    odd = complex_dft(values[1::2], sign)
    turned = [times_unit(v, sign * j, count) for j, v in enumerate(odd)]
    return [add(e, t) for e, t in zip(even, turned)] + [sub(e, t) for e, t in zip(even, turned)]


def odd_freqs(first, second, count):
    turned = [
        times_unit((a, -b), -r, count) for r, (a, b) in enumerate(zip(first, second))
    ]
    return {4 * j + 1: v for j, v in enumerate(complex_dft(turned, -1))}


def real_dft(values, count):
    half, quarter = count // 2, count // 4
    if count == 2:
        return [(values[0] + values[1], None), (values[0] - values[1], None)]
    if len(values) == half:
        folded, apart = values, values
    else:
        folded = [values[r] + values[r + half] for r in range(half)]
        apart = [values[r] - values[r + half] for r in range(half)]
    out = [None] * (half + 1)
    out[0::2] = real_dft(folded, half)
    for freq, value in odd_freqs(apart[:quarter], apart[quarter:], count).items():
        if freq <= half:
            out[freq] = value
        else:
            out[count - freq] = conj(value)
    return out


def real_inverse(freqs, count, keep_half):
    half, quarter = count // 2, count // 4
    if count == 2:
        first, last = freqs[0][0], freqs[1][0]
        return [first + last, first - last]
    even = real_inverse(freqs[0::2], half, False)
    picked = [
        freqs[4 * j + 1] if 4 * j + 1 <= half else conj(freqs[count - 4 * j - 1])
        for j in range(quarter)
    ]
    turned = [times_unit(v, r, count) for r, v in enumerate(complex_dft(picked, 1))]
    odd = [re for re, _ in turned] + [-im for _, im in turned]
    low = [e + o for e, o in zip(even, odd)]
    if keep_half:
        return low
    return low + [e - o for e, o in zip(even, odd)]


def split_table(table):
    high = table.astype(np.float32).astype(BF16)
    low = (table - high.astype(np.float64)).astype(BF16)
    return np.stack([high, low])


def lane_tables():
    idx = np.arange(LANES)
    angle = 2.0 * np.pi / LANES * (idx[:, None] * idx[None, :] % LANES)
    cos, sin = np.cos(angle), np.sin(angle)
    forward = np.block([[cos, -sin], [sin, cos]])
    inverse = np.block([[cos, sin], [-sin, cos]])
    return split_table(forward), split_table(inverse)


def twist_tables(factor):
    padded = FREQS * LANES
    angle = 2.0 * np.pi / padded * (np.arange(HALF)[:, None] * np.arange(LANES)[None, :])
    weight = np.full((HALF, 1), 2.0)
    weight[0] = weight[-1] = 1.0
    weight = weight / padded * factor
    cos, sin = np.cos(angle), np.sin(angle)
    return np.stack([cos, sin, cos * weight, sin * weight], axis=1).astype(np.float32)


def split_value(value):
    high = value.astype(BF16)
    return high, (value - high.astype(F32)).astype(BF16)


def store_parts(high_ref, low_ref, k, chans, first, base, re, im):
    for col, value in ((0, re), (LANES, im)):
        high, low = split_value(value)
        rows = pl.ds(pl.multiple_of(base + k * chans + first, CHUNK), CHUNK)
        high_ref[rows, pl.ds(col, LANES)] = high
        low_ref[rows, pl.ds(col, LANES)] = low


def rows_to_parts(get_row, twist_ref, high_ref, low_ref, chans, first, base):
    freqs = real_dft([get_row(r) for r in range(ROWS)], FREQS)
    for k, (re, im) in enumerate(freqs):
        cos, sin = twist_ref[k, 0:1, :], twist_ref[k, 1:2, :]
        if im is None:
            store_parts(high_ref, low_ref, k, chans, first, base, re * cos, -re * sin)
        else:
            store_parts(
                high_ref, low_ref, k, chans, first, base, re * cos + im * sin, im * cos - re * sin
            )


def lane_transform(high_ref, low_ref, table_ref, out_ref, total, step):
    def body(i, carry):
        rows = pl.ds(pl.multiple_of(i * step, CHUNK), step)
        high, low = high_ref[rows, :], low_ref[rows, :]
        out = jnp.dot(high, table_ref[0], preferred_element_type=F32)
        out += jnp.dot(low, table_ref[0], preferred_element_type=F32)
        out += jnp.dot(high, table_ref[1], preferred_element_type=F32)
        out_ref[rows, :] = out
        return carry

    lax.fori_loop(0, total // step, body, 0)


def correlate_parts(first_ref, second_ref, high_ref, low_ref, first_base, second_base, base, total, sign):
    def body(i, carry):
        start = i * CHUNK
        one = pl.ds(pl.multiple_of(first_base + start, CHUNK), CHUNK)
        two = pl.ds(pl.multiple_of(second_base + start, CHUNK), CHUNK)
        out = pl.ds(pl.multiple_of(base + start, CHUNK), CHUNK)
        are, aim = first_ref[one, 0:LANES], first_ref[one, LANES : 2 * LANES]
        bre, bim = second_ref[two, 0:LANES], second_ref[two, LANES : 2 * LANES]
        if sign > 0:
            re, im = are * bre + aim * bim, are * bim - aim * bre
        else:
            re, im = are * bre - aim * bim, are * bim + aim * bre
        for col, value in ((0, re), (LANES, im)):
            high, low = split_value(value)
            high_ref[out, pl.ds(col, LANES)] = high
            low_ref[out, pl.ds(col, LANES)] = low
        return carry

    lax.fori_loop(0, total // CHUNK, body, 0, unroll=4)


def parts_to_rows(back_ref, twist_ref, chans, first, base):
    freqs = []
    for k in range(HALF):
        rows = pl.ds(pl.multiple_of(base + k * chans + first, CHUNK), CHUNK)
        re, im = back_ref[rows, 0:LANES], back_ref[rows, LANES : 2 * LANES]
        cos, sin = twist_ref[k, 2:3, :], twist_ref[k, 3:4, :]
        if k in (0, ROWS):
            freqs.append((re * cos - im * sin, None))
        else:
            freqs.append((re * cos - im * sin, im * cos + re * sin))
    return real_inverse(freqs, FREQS, True)


def gate_kernel(query, key, value, grad, taps, out):
    own = out.shape[1] // 3
    for pair in range(out.shape[0] // 2):
        cols = pl.ds(pair * LANES, LANES)
        mixed = (key[:, cols].astype(F32) * value[:, cols].astype(F32)).astype(BF16)
        state = (grad[:, cols].astype(F32) * query[:, cols].astype(F32)).astype(BF16)
        for place, block in enumerate((mixed, state, taps[:, cols])):
            turned = block.T
            rows = pl.ds(place * own, own)
            out[2 * pair, rows, :] = turned[:own]
            out[2 * pair + 1, rows, :] = turned[own:]


def taps_grad_kernel(signals, lane_ref, back_lane_ref, twist_ref, spec_ref, out, high, low, back):
    chans = signals.shape[1] // 3
    total = HALF * chans

    def forward(i, carry):
        first = i * CHUNK
        for which in range(2):
            rows = pl.ds(pl.multiple_of(which * chans + first, CHUNK), CHUNK)
            rows_to_parts(
                lambda r: signals[r, rows, :].astype(F32),
                twist_ref, high, low, chans, first, which * total,
            )
        return carry

    lax.fori_loop(0, chans // CHUNK, forward, 0)
    lane_transform(high, low, lane_ref, spec_ref, 2 * total, total // 4)
    correlate_parts(spec_ref, spec_ref, high, low, 0, total, 0, total, 1)
    lane_transform(high, low, back_lane_ref, back, total, total // 4)

    def inverse(i, carry):
        rows = parts_to_rows(back, twist_ref, chans, i * CHUNK, 0)
        for r in range(ROWS):
            out[i, r] = rows[r].astype(BF16)
        return carry

    lax.fori_loop(0, chans // CHUNK, inverse, 0)


def state_kernel(signals, spec_ref, skip_ref, lane_ref, back_lane_ref, twist_ref, out, high, low, taps_spec, back):
    chans = signals.shape[1] // 3
    total = HALF * chans

    def forward(i, carry):
        first = i * CHUNK
        rows = pl.ds(pl.multiple_of(2 * chans + first, CHUNK), CHUNK)
        rows_to_parts(
            lambda r: signals[r, rows, :].astype(F32), twist_ref, high, low, chans, first, 0
        )
        return carry

    lax.fori_loop(0, chans // CHUNK, forward, 0)
    lane_transform(high, low, lane_ref, taps_spec, total, total // 4)
    correlate_parts(taps_spec, spec_ref, high, low, 0, 0, 0, total, -1)
    correlate_parts(taps_spec, spec_ref, high, low, 0, total, total, total, 1)
    lane_transform(high, low, back_lane_ref, back, 2 * total, total // 4)

    def inverse(i, carry):
        first = i * CHUNK
        skip = skip_ref[pl.ds(pl.multiple_of(first, CHUNK), CHUNK), :]
        for which in range(2):
            place = pl.ds(pl.multiple_of(which * chans + first, CHUNK), CHUNK)
            rows = parts_to_rows(back, twist_ref, chans, first, which * total)
            for r in range(ROWS):
                own = signals[r, place, :].astype(F32)
                out[r, place, :] = (rows[r] + skip * own).astype(BF16)
        return carry

    lax.fori_loop(0, chans // CHUNK, inverse, 0)


def output_kernel(back, query, key, value, grad, mixed_out, grad_query, grad_key, grad_value):
    own = back.shape[1] // 2
    for pair in range(back.shape[0] // 2):
        cols = pl.ds(pair * LANES, LANES)
        state, dmixed = (
            jnp.concatenate(
                [back[2 * pair + i, pl.ds(which * own, own), :] for i in range(2)], axis=0
            ).T.astype(F32)
            for which in range(2)
        )
        mixed_out[:, cols] = (query[:, cols].astype(F32) * state).astype(BF16)
        grad_query[:, cols] = (grad[:, cols].astype(F32) * state).astype(BF16)
        grad_key[:, cols] = (dmixed * value[:, cols].astype(F32)).astype(BF16)
        grad_value[:, cols] = (dmixed * key[:, cols].astype(F32)).astype(BF16)


def filter_kernel(blocks, out):
    shares = blocks.shape[0]
    for pair in range(blocks.shape[1] // 2):
        rows = [blocks[i, 2 * pair + s] for s in range(2) for i in range(shares)]
        out[:, pl.ds(pair * LANES, LANES)] = jnp.concatenate(rows, axis=0).T


def call(kernel, shapes, args, scratch=(), flops=0, moved=2 << 20):
    return pl.pallas_call(
        kernel,
        out_shape=shapes,
        in_specs=[pl.BlockSpec(memory_space=pltpu.VMEM)] * len(args),
        out_specs=jax.tree.map(lambda _: pl.BlockSpec(memory_space=pltpu.VMEM), shapes),
        scratch_shapes=list(scratch),
        compiler_params=pltpu.CompilerParams(vmem_limit_bytes=VMEM_LIMIT),
        cost_estimate=pl.CostEstimate(flops=flops, bytes_accessed=moved, transcendentals=0),
    )(*args)


def on_device(query_in, key_in, value_in, filter_taps, skip_gain, grad_out):
    seq_count = lax.axis_size("seq")
    shares = lax.axis_size("dl")
    rows_dev, chan_dev = query_in.shape[1:]
    own = chan_dev // seq_count
    total = HALF * own
    batch = query_in.shape[0] * lax.axis_size("dh") * shares
    factor = 1.0 / math.sqrt(batch * seq_count * rows_dev)
    shape = jax.ShapeDtypeStruct
    forward_lane, inverse_lane = lane_tables()
    query, key, value, grad = query_in[0], key_in[0], value_in[0], grad_out[0]
    skip_own = lax.dynamic_slice_in_dim(skip_gain, lax.axis_index("seq") * own, own)
    skip_own = jnp.broadcast_to(skip_own[:, None], (own, LANES))

    gated = call(
        gate_kernel,
        shape((seq_count, 3 * own, rows_dev), BF16),
        (query, key, value, grad, filter_taps),
    )
    signals = lax.all_to_all(gated, "seq", split_axis=0, concat_axis=0, tiled=True)

    parts = pltpu.VMEM((2 * total, 2 * LANES), BF16)
    spectra, taps_term = call(
        taps_grad_kernel,
        (
            shape((2 * total, 2 * LANES), F32),
            shape((own // CHUNK, seq_count, CHUNK, LANES), BF16),
        ),
        (signals, forward_lane, inverse_lane, twist_tables(factor)),
        (parts, parts, pltpu.VMEM((total, 2 * LANES), F32)),
        flops=10**9,
    )

    terms = taps_term.reshape(shares * seq_count, own // shares, LANES)
    terms = lax.all_to_all(terms, ("dl", "seq"), split_axis=0, concat_axis=0, tiled=True)
    part = terms.reshape(shares, seq_count, own // shares, LANES).astype(F32).sum(0).astype(BF16)
    other = lax.ppermute(part, "dh", [(0, 1), (1, 0)])
    summed = (part.astype(F32) + other.astype(F32)).astype(BF16)
    copies = jnp.broadcast_to(summed[None], (shares,) + summed.shape)
    gathered = lax.all_to_all(copies, "dl", split_axis=0, concat_axis=0, tiled=True)
    grad_filter = call(filter_kernel, shape((rows_dev, chan_dev), BF16), (gathered,))

    results = call(
        state_kernel,
        shape((seq_count, 2 * own, LANES), BF16),
        (signals, spectra, skip_own, forward_lane, inverse_lane, twist_tables(1.0)),
        (
            parts,
            parts,
            pltpu.VMEM((total, 2 * LANES), F32),
            pltpu.VMEM((2 * total, 2 * LANES), F32),
        ),
        flops=10**9,
    )
    back = lax.all_to_all(results, "seq", split_axis=0, concat_axis=0, tiled=True)
    block = shape((rows_dev, chan_dev), BF16)
    outs = call(output_kernel, (block,) * 4, (back, query, key, value, grad))
    return tuple(out[None] for out in outs) + (grad_filter,)


def solution(mesh):
    dp, chan, seq = (mesh.shape[name] for name in ("dp", "chan", "seq"))
    shares = 4
    split_mesh = Mesh(
        mesh.devices.reshape(dp // shares, shares, chan, seq), ("dh", "dl", "chan", "seq")
    )
    rows = P(("dh", "dl"), "seq", "chan")
    taps = P("seq", "chan")
    return jax.shard_map(
        on_device,
        mesh=split_mesh,
        in_specs=(rows, rows, rows, taps, P("chan"), rows),
        out_specs=(rows, rows, rows, rows, taps),
        check_vma=False,
    )
```

```python
import math

import jax
import jax.numpy as jnp
import numpy as np
from jax import lax
from jax.experimental import pallas as pl
from jax.experimental.pallas import tpu as pltpu
from jax.sharding import Mesh
from jax.sharding import PartitionSpec as P

F32 = jnp.float32
BF16 = jnp.bfloat16
LANES = 128
ROWS = 16
FREQS = 2 * ROWS
HALF = ROWS + 1
CHUNK = 16


def unit(numer, denom):
    angle = 2.0 * math.pi * numer / denom
    return (math.cos(angle), math.sin(angle))


def times_unit(value, numer, denom):
    re, im = value
    numer = numer % denom
    if 4 * numer % denom == 0:
        return ((re, im), (-im, re), (-re, -im), (im, -re))[4 * numer // denom]
    if 8 * numer % denom == 0:
        root = math.sqrt(0.5)
        summed, apart = (re + im) * root, (re - im) * root
        return {1: (apart, summed), 3: (-summed, apart), 5: (-apart, -summed), 7: (summed, -apart)}[
            8 * numer // denom
        ]
    cos, sin = unit(numer, denom)
    return (re * cos - im * sin, re * sin + im * cos)


def add(a, b):
    return (a[0] + b[0], a[1] + b[1])


def sub(a, b):
    return (a[0] - b[0], a[1] - b[1])


def conj(a):
    return (a[0], -a[1])


def complex_dft(values, sign):
    count = len(values)
    if count == 1:
        return list(values)
    even = complex_dft(values[0::2], sign)
    odd = complex_dft(values[1::2], sign)
    turned = [times_unit(v, sign * j, count) for j, v in enumerate(odd)]
    return [add(e, t) for e, t in zip(even, turned)] + [sub(e, t) for e, t in zip(even, turned)]


def odd_freqs(first, second, count):
    turned = [
        times_unit((a, -b), -r, count) for r, (a, b) in enumerate(zip(first, second))
    ]
    return {4 * j + 1: v for j, v in enumerate(complex_dft(turned, -1))}


def real_dft(values, count):
    half, quarter = count // 2, count // 4
    if count == 2:
        return [(values[0] + values[1], None), (values[0] - values[1], None)]
    if len(values) == half:
        folded, apart = values, values
    else:
        folded = [values[r] + values[r + half] for r in range(half)]
        apart = [values[r] - values[r + half] for r in range(half)]
    out = [None] * (half + 1)
    out[0::2] = real_dft(folded, half)
    for freq, value in odd_freqs(apart[:quarter], apart[quarter:], count).items():
        if freq <= half:
            out[freq] = value
        else:
            out[count - freq] = conj(value)
    return out


def real_inverse(freqs, count, keep_half):
    half, quarter = count // 2, count // 4
    if count == 2:
        first, last = freqs[0][0], freqs[1][0]
        return [first + last, first - last]
    even = real_inverse(freqs[0::2], half, False)
    picked = [
        freqs[4 * j + 1] if 4 * j + 1 <= half else conj(freqs[count - 4 * j - 1])
        for j in range(quarter)
    ]
    turned = [times_unit(v, r, count) for r, v in enumerate(complex_dft(picked, 1))]
    odd = [re for re, _ in turned] + [-im for _, im in turned]
    low = [e + o for e, o in zip(even, odd)]
    if keep_half:
        return low
    return low + [e - o for e, o in zip(even, odd)]


def split_table(table):
    high = table.astype(np.float32).astype(BF16)
    low = (table - high.astype(np.float64)).astype(BF16)
    return np.stack([high, low])


def lane_tables():
    idx = np.arange(LANES)
    angle = 2.0 * np.pi / LANES * (idx[:, None] * idx[None, :] % LANES)
    cos, sin = np.cos(angle), np.sin(angle)
    forward = np.block([[cos, -sin], [sin, cos]])
    inverse = np.block([[cos, sin], [-sin, cos]])
    return split_table(forward), split_table(inverse)


def twist_tables(factor):
    padded = FREQS * LANES
    angle = 2.0 * np.pi / padded * (np.arange(HALF)[:, None] * np.arange(LANES)[None, :])
    weight = np.full((HALF, 1), 2.0)
    weight[0] = weight[-1] = 1.0
    weight = weight / padded * factor
    cos, sin = np.cos(angle), np.sin(angle)
    return np.stack([cos, sin, cos * weight, sin * weight], axis=1).astype(np.float32)


def split_value(value):
    high = value.astype(BF16)
    return high, (value - high.astype(F32)).astype(BF16)


def store_parts(high_ref, low_ref, k, chans, first, base, re, im):
    for col, value in ((0, re), (LANES, im)):
        high, low = split_value(value)
        rows = pl.ds(pl.multiple_of(base + k * chans + first, CHUNK), CHUNK)
        high_ref[rows, pl.ds(col, LANES)] = high
        low_ref[rows, pl.ds(col, LANES)] = low


def rows_to_parts(get_row, twist_ref, high_ref, low_ref, chans, first, base):
    freqs = real_dft([get_row(r) for r in range(ROWS)], FREQS)
    for k, (re, im) in enumerate(freqs):
        cos, sin = twist_ref[k, 0:1, :], twist_ref[k, 1:2, :]
        if im is None:
            store_parts(high_ref, low_ref, k, chans, first, base, re * cos, -re * sin)
        else:
            store_parts(
                high_ref, low_ref, k, chans, first, base, re * cos + im * sin, im * cos - re * sin
            )


def lane_transform(high_ref, low_ref, table_ref, out_ref, total, step):
    def body(i, carry):
        rows = pl.ds(pl.multiple_of(i * step, CHUNK), step)
        high, low = high_ref[rows, :], low_ref[rows, :]
        out = jnp.dot(high, table_ref[0], preferred_element_type=F32)
        out += jnp.dot(low, table_ref[0], preferred_element_type=F32)
        out += jnp.dot(high, table_ref[1], preferred_element_type=F32)
        out_ref[rows, :] = out
        return carry

    lax.fori_loop(0, total // step, body, 0)


def multiply_parts(first_ref, second_ref, high_ref, low_ref, first_bases, second_bases, base, total, sign):
    def body(i, carry):
        start = i * CHUNK
        out = pl.ds(pl.multiple_of(base + start, CHUNK), CHUNK)
        terms = []
        for first_base, second_base in zip(first_bases, second_bases):
            one = pl.ds(pl.multiple_of(first_base + start, CHUNK), CHUNK)
            two = pl.ds(pl.multiple_of(second_base + start, CHUNK), CHUNK)
            are, aim = first_ref[one, 0:LANES], first_ref[one, LANES : 2 * LANES]
            bre, bim = second_ref[two, 0:LANES], second_ref[two, LANES : 2 * LANES]
            if sign > 0:
                terms.append((are * bre + aim * bim, are * bim - aim * bre))
            else:
                terms.append((are * bre - aim * bim, are * bim + aim * bre))
        re, im = terms[0]
        for more in terms[1:]:
            re, im = re + more[0], im + more[1]
        for col, value in ((0, re), (LANES, im)):
            high, low = split_value(value)
            high_ref[out, pl.ds(col, LANES)] = high
            low_ref[out, pl.ds(col, LANES)] = low
        return carry

    lax.fori_loop(0, total // CHUNK, body, 0, unroll=2)


def parts_to_rows(back_ref, twist_ref, chans, first, base):
    freqs = []
    for k in range(HALF):
        rows = pl.ds(pl.multiple_of(base + k * chans + first, CHUNK), CHUNK)
        re, im = back_ref[rows, 0:LANES], back_ref[rows, LANES : 2 * LANES]
        cos, sin = twist_ref[k, 2:3, :], twist_ref[k, 3:4, :]
        if k in (0, ROWS):
            freqs.append((re * cos - im * sin, None))
        else:
            freqs.append((re * cos - im * sin, im * cos + re * sin))
    return real_inverse(freqs, FREQS, True)


def start_copies(pairs, sems):
    copies = [pltpu.make_async_copy(a, b, sems.at[i]) for i, (a, b) in enumerate(pairs)]
    for copy in copies:
        copy.start()
    return copies


def gate_kernel(query, key, value, grad, taps, out, query_v, key_v, value_v, grad_v, taps_v, out_v, sems, out_sem):
    peers = out.shape[0]
    own = taps.shape[1] // peers
    share = out.shape[1] - 2 * own
    pieces = LANES // own
    begin = lax.axis_index("pl") * share
    held = ((key, key_v), (value, value_v), (grad, grad_v), (query, query_v), (taps, taps_v))
    copies = start_copies(held, sems)
    for copy in copies:
        copy.wait()
    sent = []
    for tile in range(peers // pieces):
        cols = pl.ds(tile * LANES, LANES)
        mixed = (key_v[:, cols].astype(F32) * value_v[:, cols].astype(F32)).astype(BF16)
        state = (grad_v[:, cols].astype(F32) * query_v[:, cols].astype(F32)).astype(BF16)
        for place, block in enumerate((mixed, state)):
            turned = block.T
            for i in range(pieces):
                out_v[tile * pieces + i, pl.ds(place * own, own), :] = turned[i * own : (i + 1) * own]
        turned = taps_v[:, cols].T
        for i in range(pieces):
            low = turned[i * own : i * own + share]
            high = turned[i * own + share : (i + 1) * own]
            out_v[tile * pieces + i, pl.ds(2 * own, share), :] = jnp.where(begin == 0, low, high)
        rows = pl.ds(tile * pieces, pieces)
        copy = pltpu.make_async_copy(out_v.at[rows], out.at[rows], out_sem.at[tile])
        copy.start()
        sent.append(copy)
    for copy in sent:
        copy.wait()


def taps_grad_kernel(signals, lane_ref, back_lane_ref, twist_ref, spec_ref, out, high, low, back):
    batch = signals.shape[0] // ROWS
    chans = out.shape[0] * CHUNK
    total = HALF * chans

    def forward(i, carry):
        first = i * CHUNK
        for which in range(2):
            rows = pl.ds(pl.multiple_of(which * chans + first, CHUNK), CHUNK)
            for b in range(batch):
                rows_to_parts(
                    lambda r: signals[b * ROWS + r, rows, :].astype(F32),
                    twist_ref, high, low, chans, first, (which * batch + b) * total,
                )
        return carry

    lax.fori_loop(0, chans // CHUNK, forward, 0)
    lane_transform(high, low, lane_ref, spec_ref, 2 * batch * total, total // 2)
    multiply_parts(
        spec_ref, spec_ref, high, low,
        [b * total for b in range(batch)], [(batch + b) * total for b in range(batch)], 0, total, 1,
    )
    lane_transform(high, low, back_lane_ref, back, total, total // 2)

    def inverse(i, carry):
        rows = parts_to_rows(back, twist_ref, chans, i * CHUNK, 0)
        for r in range(ROWS):
            out[i, r] = rows[r].astype(BF16)
        return carry

    lax.fori_loop(0, chans // CHUNK, inverse, 0)


def state_kernel(signals, spec_ref, skip_ref, lane_ref, back_lane_ref, twist_ref, out, high, low, taps_spec, back):
    batch = signals.shape[0] // ROWS
    chans = out.shape[1] // 2
    share = signals.shape[1] - 2 * chans
    total = HALF * chans

    for b in range(batch):
        for first in range(0, share, CHUNK):
            rows = pl.ds(2 * chans + first, CHUNK)
            rows_to_parts(
                lambda r: signals[b * ROWS + r, rows, :].astype(F32),
                twist_ref, high, low, chans, b * share + first, 0,
            )
    lane_transform(high, low, lane_ref, taps_spec, total, total // 2)
    for which in range(2):
        for b in range(batch):
            base = (which * batch + b) * total
            multiply_parts(
                taps_spec, spec_ref, high, low, [0], [base], base, total, 1 if which else -1
            )
    lane_transform(high, low, back_lane_ref, back, 2 * batch * total, total // 2)

    def inverse(i, carry):
        first = i * CHUNK
        skip = skip_ref[pl.ds(pl.multiple_of(first, CHUNK), CHUNK), :]
        for which in range(2):
            place = pl.ds(pl.multiple_of(which * chans + first, CHUNK), CHUNK)
            for b in range(batch):
                rows = parts_to_rows(back, twist_ref, chans, first, (which * batch + b) * total)
                for r in range(ROWS):
                    own = signals[b * ROWS + r, place, :].astype(F32)
                    out[b * ROWS + r, place, :] = (rows[r] + skip * own).astype(BF16)
        return carry

    lax.fori_loop(0, chans // CHUNK, inverse, 0)


def output_kernel(back, query, key, value, grad, mixed_out, grad_query, grad_key, grad_value):
    own = back.shape[1] // 2
    pieces = LANES // own
    for tile in range(back.shape[0] // pieces):
        cols = pl.ds(tile * LANES, LANES)
        state, dmixed = (
            jnp.concatenate(
                [back[tile * pieces + i, pl.ds(which * own, own), :] for i in range(pieces)], axis=0
            ).T.astype(F32)
            for which in range(2)
        )
        mixed_out[:, cols] = (query[:, cols].astype(F32) * state).astype(BF16)
        grad_query[:, cols] = (grad[:, cols].astype(F32) * state).astype(BF16)
        grad_key[:, cols] = (dmixed * value[:, cols].astype(F32)).astype(BF16)
        grad_value[:, cols] = (dmixed * key[:, cols].astype(F32)).astype(BF16)


def filter_kernel(blocks, out):
    shares, owners, depth = blocks.shape[:3]
    pieces = LANES // (shares * depth)
    for tile in range(owners // pieces):
        rows = [blocks[i, tile * pieces + s] for s in range(pieces) for i in range(shares)]
        out[:, pl.ds(tile * LANES, LANES)] = jnp.concatenate(rows, axis=0).T


def call(kernel, shapes, args, scratch=(), in_hbm=False, out_hbm=False, flops=0, moved=2 << 20, limit=24):
    place = lambda hbm: pl.BlockSpec(memory_space=pltpu.HBM if hbm else pltpu.VMEM)
    return pl.pallas_call(
        kernel,
        out_shape=shapes,
        in_specs=[place(in_hbm)] * len(args),
        out_specs=jax.tree.map(lambda _: place(out_hbm), shapes),
        scratch_shapes=list(scratch),
        compiler_params=pltpu.CompilerParams(vmem_limit_bytes=limit << 20),
        cost_estimate=pl.CostEstimate(flops=flops, bytes_accessed=moved, transcendentals=0),
    )(*args)


def gate(query, key, value, grad, taps, peers):
    rows_dev, chan_dev = query.shape
    own = chan_dev // peers
    out_shape = (peers, 2 * own + own // 2, rows_dev)
    return call(
        gate_kernel,
        jax.ShapeDtypeStruct(out_shape, BF16),
        (query, key, value, grad, taps),
        [pltpu.VMEM((rows_dev, chan_dev), BF16)] * 5
        + [
            pltpu.VMEM(out_shape, BF16),
            pltpu.SemaphoreType.DMA((5,)),
            pltpu.SemaphoreType.DMA((chan_dev // LANES,)),
        ],
        in_hbm=True,
        out_hbm=True,
    )


def taps_grad(signals, own, factor):
    total = HALF * own
    batch = signals.shape[0] // ROWS
    forward_lane, inverse_lane = lane_tables()
    shape = jax.ShapeDtypeStruct
    parts = pltpu.VMEM((2 * batch * total, 2 * LANES), BF16)
    return call(
        taps_grad_kernel,
        (
            shape((2 * batch * total, 2 * LANES), F32),
            shape((own // CHUNK, ROWS, CHUNK, LANES), BF16),
        ),
        (signals, forward_lane, inverse_lane, twist_tables(factor)),
        (parts, parts, pltpu.VMEM((total, 2 * LANES), F32)),
        flops=10**9,
    )


def states(signals, spectra, skip_own, own):
    total = HALF * own
    batch = signals.shape[0] // ROWS
    forward_lane, inverse_lane = lane_tables()
    parts = pltpu.VMEM((2 * batch * total, 2 * LANES), BF16)
    return call(
        state_kernel,
        jax.ShapeDtypeStruct((batch * ROWS, 2 * own, LANES), BF16),
        (signals, spectra, skip_own, forward_lane, inverse_lane, twist_tables(1.0)),
        (
            parts,
            parts,
            pltpu.VMEM((total, 2 * LANES), F32),
            pltpu.VMEM((2 * batch * total, 2 * LANES), F32),
        ),
        flops=10**9,
    )


def outputs(back, query, key, value, grad):
    block = jax.ShapeDtypeStruct(query.shape, BF16)
    return call(output_kernel, (block,) * 4, (back, query, key, value, grad))


def on_device(query_in, key_in, value_in, filter_taps, skip_gain, grad_out):
    seq_count, pair = lax.axis_size("seq"), lax.axis_size("pl")
    peers = seq_count * pair
    rows_dev, chan_dev = query_in.shape[1:]
    own = chan_dev // peers
    batch = query_in.shape[0] * lax.axis_size("dh") * lax.axis_size("dm") * pair
    factor = 1.0 / math.sqrt(batch * seq_count * rows_dev)
    query, key, value, grad = query_in[0], key_in[0], value_in[0], grad_out[0]
    place = lax.axis_index("pl") * seq_count + lax.axis_index("seq")
    skip_own = lax.dynamic_slice_in_dim(skip_gain, place * own, own)
    skip_own = jnp.broadcast_to(skip_own[:, None], (own, LANES))

    def swap(values, axes):
        return lax.all_to_all(values, axes, split_axis=0, concat_axis=0, tiled=True)

    signals = swap(gate(query, key, value, grad, filter_taps, peers), ("pl", "seq"))
    spectra, taps_term = taps_grad(signals, own, factor)

    groups = own // CHUNK
    terms = swap(taps_term.reshape(groups * seq_count, CHUNK, LANES), ("dm", "seq"))
    part = terms.reshape(groups, seq_count, CHUNK, LANES).astype(F32).sum(0).astype(BF16)
    other = lax.ppermute(part, "dh", [(0, 1), (1, 0)])
    summed = (part.astype(F32) + other.astype(F32)).astype(BF16)
    copies = jnp.broadcast_to(summed[None], (groups * pair,) + summed.shape)
    gathered = swap(copies, ("dm", "pl")).reshape(groups, peers, CHUNK, LANES)
    grad_filter = call(
        filter_kernel, jax.ShapeDtypeStruct((rows_dev, chan_dev), BF16), (gathered,)
    )

    back = swap(states(signals, spectra, skip_own, own), ("pl", "seq"))
    outs = outputs(back, query, key, value, grad)
    return tuple(out[None] for out in outs) + (grad_filter,)


def solution(mesh):
    dp, chan, seq = (mesh.shape[name] for name in ("dp", "chan", "seq"))
    split_mesh = Mesh(
        mesh.devices.reshape(dp // 4, 2, 2, chan, seq), ("dh", "dm", "pl", "chan", "seq")
    )
    rows = P(("dh", "dm", "pl"), "seq", "chan")
    taps = P("seq", "chan")
    return jax.shard_map(
        on_device,
        mesh=split_mesh,
        in_specs=(rows, rows, rows, taps, P("chan"), rows),
        out_specs=(rows, rows, rows, rows, taps),
        check_vma=False,
    )
```

```python
import math

import jax
import jax.numpy as jnp
import numpy as np
from jax import lax
from jax.experimental import pallas as pl
from jax.experimental.pallas import tpu as pltpu
from jax.sharding import Mesh
from jax.sharding import PartitionSpec as P

F32 = jnp.float32
BF16 = jnp.bfloat16
LANES = 128
ROWS = 16
FREQS = 2 * ROWS
HALF = ROWS + 1
CHUNK = 16


def unit(numer, denom):
    angle = 2.0 * math.pi * numer / denom
    return (math.cos(angle), math.sin(angle))


def times_unit(value, numer, denom):
    re, im = value
    numer = numer % denom
    if 4 * numer % denom == 0:
        return ((re, im), (-im, re), (-re, -im), (im, -re))[4 * numer // denom]
    if 8 * numer % denom == 0:
        root = math.sqrt(0.5)
        summed, apart = (re + im) * root, (re - im) * root
        return {1: (apart, summed), 3: (-summed, apart), 5: (-apart, -summed), 7: (summed, -apart)}[
            8 * numer // denom
        ]
    cos, sin = unit(numer, denom)
    return (re * cos - im * sin, re * sin + im * cos)


def add(a, b):
    return (a[0] + b[0], a[1] + b[1])


def sub(a, b):
    return (a[0] - b[0], a[1] - b[1])


def conj(a):
    return (a[0], -a[1])


def complex_dft(values, sign):
    count = len(values)
    if count == 1:
        return list(values)
    even = complex_dft(values[0::2], sign)
    odd = complex_dft(values[1::2], sign)
    turned = [times_unit(v, sign * j, count) for j, v in enumerate(odd)]
    return [add(e, t) for e, t in zip(even, turned)] + [sub(e, t) for e, t in zip(even, turned)]


def odd_freqs(first, second, count):
    turned = [
        times_unit((a, -b), -r, count) for r, (a, b) in enumerate(zip(first, second))
    ]
    return {4 * j + 1: v for j, v in enumerate(complex_dft(turned, -1))}


def real_dft(values, count):
    half, quarter = count // 2, count // 4
    if count == 2:
        return [(values[0] + values[1], None), (values[0] - values[1], None)]
    if len(values) == half:
        folded, apart = values, values
    else:
        folded = [values[r] + values[r + half] for r in range(half)]
        apart = [values[r] - values[r + half] for r in range(half)]
    out = [None] * (half + 1)
    out[0::2] = real_dft(folded, half)
    for freq, value in odd_freqs(apart[:quarter], apart[quarter:], count).items():
        if freq <= half:
            out[freq] = value
        else:
            out[count - freq] = conj(value)
    return out


def real_inverse(freqs, count, keep_half):
    half, quarter = count // 2, count // 4
    if count == 2:
        first, last = freqs[0][0], freqs[1][0]
        return [first + last, first - last]
    even = real_inverse(freqs[0::2], half, False)
    picked = [
        freqs[4 * j + 1] if 4 * j + 1 <= half else conj(freqs[count - 4 * j - 1])
        for j in range(quarter)
    ]
    turned = [times_unit(v, r, count) for r, v in enumerate(complex_dft(picked, 1))]
    odd = [re for re, _ in turned] + [-im for _, im in turned]
    low = [e + o for e, o in zip(even, odd)]
    if keep_half:
        return low
    return low + [e - o for e, o in zip(even, odd)]


def split_table(table):
    high = table.astype(np.float32).astype(BF16)
    low = (table - high.astype(np.float64)).astype(BF16)
    return np.stack([high, low])


def lane_tables():
    idx = np.arange(LANES)
    angle = 2.0 * np.pi / LANES * (idx[:, None] * idx[None, :] % LANES)
    cos, sin = np.cos(angle), np.sin(angle)
    forward = np.block([[cos, -sin], [sin, cos]])
    inverse = np.block([[cos, sin], [-sin, cos]])
    return split_table(forward), split_table(inverse)


def twist_tables(factor):
    padded = FREQS * LANES
    angle = 2.0 * np.pi / padded * (np.arange(HALF)[:, None] * np.arange(LANES)[None, :])
    weight = np.full((HALF, 1), 2.0)
    weight[0] = weight[-1] = 1.0
    weight = weight / padded * factor
    cos, sin = np.cos(angle), np.sin(angle)
    return np.stack([cos, sin, cos * weight, sin * weight], axis=1).astype(np.float32)


def split_value(value):
    high = value.astype(BF16)
    return high, (value - high.astype(F32)).astype(BF16)


def store_parts(high_ref, low_ref, k, chans, first, base, re, im):
    for col, value in ((0, re), (LANES, im)):
        high, low = split_value(value)
        rows = pl.ds(pl.multiple_of(base + k * chans + first, CHUNK), CHUNK)
        high_ref[rows, pl.ds(col, LANES)] = high
        low_ref[rows, pl.ds(col, LANES)] = low


def rows_to_parts(get_row, twist_ref, high_ref, low_ref, chans, first, base):
    freqs = real_dft([get_row(r) for r in range(ROWS)], FREQS)
    for k, (re, im) in enumerate(freqs):
        cos, sin = twist_ref[k, 0:1, :], twist_ref[k, 1:2, :]
        if im is None:
            store_parts(high_ref, low_ref, k, chans, first, base, re * cos, -re * sin)
        else:
            store_parts(
                high_ref, low_ref, k, chans, first, base, re * cos + im * sin, im * cos - re * sin
            )


def lane_transform(high_ref, low_ref, table_ref, out_ref, total, step):
    def body(i, carry):
        rows = pl.ds(pl.multiple_of(i * step, CHUNK), step)
        high, low = high_ref[rows, :], low_ref[rows, :]
        out = jnp.dot(high, table_ref[0], preferred_element_type=F32)
        out += jnp.dot(low, table_ref[0], preferred_element_type=F32)
        out += jnp.dot(high, table_ref[1], preferred_element_type=F32)
        out_ref[rows, :] = out
        return carry

    lax.fori_loop(0, total // step, body, 0)


def multiply_parts(first_ref, second_ref, high_ref, low_ref, first_bases, second_bases, base, total, sign):
    def body(i, carry):
        start = i * CHUNK
        out = pl.ds(pl.multiple_of(base + start, CHUNK), CHUNK)
        terms = []
        for first_base, second_base in zip(first_bases, second_bases):
            one = pl.ds(pl.multiple_of(first_base + start, CHUNK), CHUNK)
            two = pl.ds(pl.multiple_of(second_base + start, CHUNK), CHUNK)
            are, aim = first_ref[one, 0:LANES], first_ref[one, LANES : 2 * LANES]
            bre, bim = second_ref[two, 0:LANES], second_ref[two, LANES : 2 * LANES]
            if sign > 0:
                terms.append((are * bre + aim * bim, are * bim - aim * bre))
            else:
                terms.append((are * bre - aim * bim, are * bim + aim * bre))
        re, im = terms[0]
        for more in terms[1:]:
            re, im = re + more[0], im + more[1]
        for col, value in ((0, re), (LANES, im)):
            high, low = split_value(value)
            high_ref[out, pl.ds(col, LANES)] = high
            low_ref[out, pl.ds(col, LANES)] = low
        return carry

    lax.fori_loop(0, total // CHUNK, body, 0, unroll=2)


def parts_to_rows(back_ref, twist_ref, chans, first, base):
    freqs = []
    for k in range(HALF):
        rows = pl.ds(pl.multiple_of(base + k * chans + first, CHUNK), CHUNK)
        re, im = back_ref[rows, 0:LANES], back_ref[rows, LANES : 2 * LANES]
        cos, sin = twist_ref[k, 2:3, :], twist_ref[k, 3:4, :]
        if k in (0, ROWS):
            freqs.append((re * cos - im * sin, None))
        else:
            freqs.append((re * cos - im * sin, im * cos + re * sin))
    return real_inverse(freqs, FREQS, True)


def start_copies(pairs, sems):
    copies = [pltpu.make_async_copy(a, b, sems.at[i]) for i, (a, b) in enumerate(pairs)]
    for copy in copies:
        copy.start()
    return copies


def gate_kernel(query, key, value, grad, taps, out, query_v, key_v, value_v, grad_v, taps_v, out_v, sems, out_sem):
    peers = out.shape[0]
    own = taps.shape[1] // peers
    share = out.shape[1] - 2 * own
    pieces = LANES // own
    begin = lax.axis_index("pl") * share
    held = ((key, key_v), (value, value_v), (grad, grad_v), (query, query_v), (taps, taps_v))
    copies = start_copies(held, sems)
    for copy in copies:
        copy.wait()
    sent = []
    for tile in range(peers // pieces):
        cols = pl.ds(tile * LANES, LANES)
        mixed = (key_v[:, cols].astype(F32) * value_v[:, cols].astype(F32)).astype(BF16)
        state = (grad_v[:, cols].astype(F32) * query_v[:, cols].astype(F32)).astype(BF16)
        for place, block in enumerate((mixed, state)):
            turned = block.T
            for i in range(pieces):
                out_v[tile * pieces + i, pl.ds(place * own, own), :] = turned[i * own : (i + 1) * own]
        turned = taps_v[:, cols].T
        for i in range(pieces):
            low = turned[i * own : i * own + share]
            high = turned[i * own + share : (i + 1) * own]
            out_v[tile * pieces + i, pl.ds(2 * own, share), :] = jnp.where(begin == 0, low, high)
        rows = pl.ds(tile * pieces, pieces)
        copy = pltpu.make_async_copy(out_v.at[rows], out.at[rows], out_sem.at[tile])
        copy.start()
        sent.append(copy)
    for copy in sent:
        copy.wait()


def taps_grad_kernel(signals, lane_ref, back_lane_ref, twist_ref, spec_ref, out, high, low, back):
    batch = signals.shape[0] // ROWS
    chans = out.shape[1]
    total = HALF * chans

    def forward(i, carry):
        first = i * CHUNK
        for which in range(2):
            rows = pl.ds(pl.multiple_of(which * chans + first, CHUNK), CHUNK)
            for b in range(batch):
                rows_to_parts(
                    lambda r: signals[b * ROWS + r, rows, :].astype(F32),
                    twist_ref, high, low, chans, first, (which * batch + b) * total,
                )
        return carry

    lax.fori_loop(0, chans // CHUNK, forward, 0)
    lane_transform(high, low, lane_ref, spec_ref, 2 * batch * total, total // 2)
    multiply_parts(
        spec_ref, spec_ref, high, low,
        [b * total for b in range(batch)], [(batch + b) * total for b in range(batch)], 0, total, 1,
    )
    lane_transform(high, low, back_lane_ref, back, total, total // 2)

    for first in range(0, chans, CHUNK):
        rows = parts_to_rows(back, twist_ref, chans, first, 0)
        for r in range(ROWS):
            out[r, pl.ds(first, CHUNK), :] = rows[r].astype(BF16)


def state_kernel(signals, spec_ref, skip_ref, lane_ref, back_lane_ref, twist_ref, out, high, low, taps_spec, back):
    batch = signals.shape[0] // ROWS
    chans = out.shape[1] // 2
    share = signals.shape[1] - 2 * chans
    total = HALF * chans

    for b in range(batch):
        for first in range(0, share, CHUNK):
            rows = pl.ds(2 * chans + first, CHUNK)
            rows_to_parts(
                lambda r: signals[b * ROWS + r, rows, :].astype(F32),
                twist_ref, high, low, chans, b * share + first, 0,
            )
    lane_transform(high, low, lane_ref, taps_spec, total, total // 2)
    for which in range(2):
        for b in range(batch):
            base = (which * batch + b) * total
            multiply_parts(
                taps_spec, spec_ref, high, low, [0], [base], base, total, 1 if which else -1
            )
    lane_transform(high, low, back_lane_ref, back, 2 * batch * total, total // 2)

    def inverse(i, carry):
        first = i * CHUNK
        skip = skip_ref[pl.ds(pl.multiple_of(first, CHUNK), CHUNK), :]
        for which in range(2):
            place = pl.ds(pl.multiple_of(which * chans + first, CHUNK), CHUNK)
            for b in range(batch):
                rows = parts_to_rows(back, twist_ref, chans, first, (which * batch + b) * total)
                for r in range(ROWS):
                    own = signals[b * ROWS + r, place, :].astype(F32)
                    out[b * ROWS + r, place, :] = (rows[r] + skip * own).astype(BF16)
        return carry

    lax.fori_loop(0, chans // CHUNK, inverse, 0)


def output_kernel(back, query, key, value, grad, mixed_out, grad_query, grad_key, grad_value, grad_filter):
    own = back.shape[1] // 3
    pieces = LANES // own
    for tile in range(back.shape[0] // pieces):
        cols = pl.ds(tile * LANES, LANES)
        state, dmixed, term = (
            jnp.concatenate(
                [back[tile * pieces + i, pl.ds(which * own, own), :] for i in range(pieces)], axis=0
            ).T
            for which in range(3)
        )
        state, dmixed = state.astype(F32), dmixed.astype(F32)
        mixed_out[:, cols] = (query[:, cols].astype(F32) * state).astype(BF16)
        grad_query[:, cols] = (grad[:, cols].astype(F32) * state).astype(BF16)
        grad_key[:, cols] = (dmixed * value[:, cols].astype(F32)).astype(BF16)
        grad_value[:, cols] = (dmixed * key[:, cols].astype(F32)).astype(BF16)
        grad_filter[:, cols] = term


def call(kernel, shapes, args, scratch=(), in_hbm=False, out_hbm=False, flops=0, moved=2 << 20, limit=24):
    place = lambda hbm: pl.BlockSpec(memory_space=pltpu.HBM if hbm else pltpu.VMEM)
    return pl.pallas_call(
        kernel,
        out_shape=shapes,
        in_specs=[place(in_hbm)] * len(args),
        out_specs=jax.tree.map(lambda _: place(out_hbm), shapes),
        scratch_shapes=list(scratch),
        compiler_params=pltpu.CompilerParams(vmem_limit_bytes=limit << 20),
        cost_estimate=pl.CostEstimate(flops=flops, bytes_accessed=moved, transcendentals=0),
    )(*[pltpu.with_memory_space_constraint(a, pltpu.HBM) for a in args] if in_hbm else args)


def gate(query, key, value, grad, taps, peers):
    rows_dev, chan_dev = query.shape
    own = chan_dev // peers
    out_shape = (peers, 2 * own + own // 2, rows_dev)
    return call(
        gate_kernel,
        jax.ShapeDtypeStruct(out_shape, BF16),
        (query, key, value, grad, taps),
        [pltpu.VMEM((rows_dev, chan_dev), BF16)] * 5
        + [
            pltpu.VMEM(out_shape, BF16),
            pltpu.SemaphoreType.DMA((5,)),
            pltpu.SemaphoreType.DMA((chan_dev // LANES,)),
        ],
        in_hbm=True,
        out_hbm=True,
    )


def taps_grad(signals, own, factor):
    total = HALF * own
    batch = signals.shape[0] // ROWS
    forward_lane, inverse_lane = lane_tables()
    shape = jax.ShapeDtypeStruct
    parts = pltpu.VMEM((2 * batch * total, 2 * LANES), BF16)
    return call(
        taps_grad_kernel,
        (
            shape((2 * batch * total, 2 * LANES), F32),
            shape((ROWS, own, LANES), BF16),
        ),
        (signals, forward_lane, inverse_lane, twist_tables(factor)),
        (parts, parts, pltpu.VMEM((total, 2 * LANES), F32)),
        flops=5 * 10**9,
    )


def states(signals, spectra, skip_own, own):
    total = HALF * own
    batch = signals.shape[0] // ROWS
    forward_lane, inverse_lane = lane_tables()
    parts = pltpu.VMEM((2 * batch * total, 2 * LANES), BF16)
    return call(
        state_kernel,
        jax.ShapeDtypeStruct((batch * ROWS, 2 * own, LANES), BF16),
        (signals, spectra, skip_own, forward_lane, inverse_lane, twist_tables(1.0)),
        (
            parts,
            parts,
            pltpu.VMEM((total, 2 * LANES), F32),
            pltpu.VMEM((2 * batch * total, 2 * LANES), F32),
        ),
        flops=5 * 10**9,
    )


def outputs(back, query, key, value, grad):
    block = jax.ShapeDtypeStruct(query.shape, BF16)
    return call(output_kernel, (block,) * 5, (back, query, key, value, grad))


def on_device(query_in, key_in, value_in, filter_taps, skip_gain, grad_out):
    seq_count, pair = lax.axis_size("seq"), lax.axis_size("pl")
    peers = seq_count * pair
    rows_dev, chan_dev = query_in.shape[1:]
    own = chan_dev // peers
    batch = query_in.shape[0] * lax.axis_size("dh") * lax.axis_size("dm") * pair
    factor = 1.0 / math.sqrt(batch * seq_count * rows_dev)
    query, key, value, grad = query_in[0], key_in[0], value_in[0], grad_out[0]
    place = lax.axis_index("pl") * seq_count + lax.axis_index("seq")
    skip_own = lax.dynamic_slice_in_dim(skip_gain, place * own, own)
    skip_own = jnp.broadcast_to(skip_own[:, None], (own, LANES))

    def swap(values, axes):
        return lax.all_to_all(values, axes, split_axis=0, concat_axis=0, tiled=True)

    signals = swap(gate(query, key, value, grad, filter_taps, peers), ("pl", "seq"))
    spectra, term = taps_grad(signals, own, factor)

    def exchange(values, axis):
        return lax.ppermute(values, axis, [(0, 1), (1, 0)])

    def plus(a, b):
        return (a.astype(F32) + b.astype(F32)).astype(BF16)

    taken = exchange(term, "dm")
    results = states(signals, spectra, skip_own, own)
    taken, results = lax.optimization_barrier((taken, results))
    term = plus(term, taken)
    term = plus(term, exchange(term, "dh"))
    copies = jnp.broadcast_to(term[None], (pair,) + term.shape).reshape((peers,) + term.shape[1:])
    back = swap(jnp.concatenate([results, copies], axis=1), ("pl", "seq"))
    outs = outputs(back, query, key, value, grad)
    return tuple(out[None] for out in outs[:4]) + (outs[4],)


def solution(mesh):
    dp, chan, seq = (mesh.shape[name] for name in ("dp", "chan", "seq"))
    split_mesh = Mesh(
        mesh.devices.reshape(dp // 4, 2, 2, chan, seq), ("dh", "dm", "pl", "chan", "seq")
    )
    rows = P(("dh", "dm", "pl"), "seq", "chan")
    taps = P("seq", "chan")
    return jax.shard_map(
        on_device,
        mesh=split_mesh,
        in_specs=(rows, rows, rows, taps, P("chan"), rows),
        out_specs=(rows, rows, rows, rows, taps),
        check_vma=False,
    )
```

```python
import math

import jax
import jax.numpy as jnp
import numpy as np
from jax import lax
from jax.experimental import pallas as pl
from jax.experimental.pallas import tpu as pltpu
from jax.sharding import Mesh
from jax.sharding import PartitionSpec as P

F32 = jnp.float32
BF16 = jnp.bfloat16
LANES = 128
ROWS = 16
FREQS = 2 * ROWS
HALF = ROWS + 1
CHUNK = 16
GROUPS = 2


def unit(numer, denom):
    angle = 2.0 * math.pi * numer / denom
    return (math.cos(angle), math.sin(angle))


def times_unit(value, numer, denom):
    re, im = value
    numer = numer % denom
    if 4 * numer % denom == 0:
        return ((re, im), (-im, re), (-re, -im), (im, -re))[4 * numer // denom]
    if 8 * numer % denom == 0:
        root = math.sqrt(0.5)
        summed, apart = (re + im) * root, (re - im) * root
        return {1: (apart, summed), 3: (-summed, apart), 5: (-apart, -summed), 7: (summed, -apart)}[
            8 * numer // denom
        ]
    cos, sin = unit(numer, denom)
    return (re * cos - im * sin, re * sin + im * cos)


def add(a, b):
    return (a[0] + b[0], a[1] + b[1])


def sub(a, b):
    return (a[0] - b[0], a[1] - b[1])


def conj(a):
    return (a[0], -a[1])


def complex_dft(values, sign):
    count = len(values)
    if count == 1:
        return list(values)
    even = complex_dft(values[0::2], sign)
    odd = complex_dft(values[1::2], sign)
    turned = [times_unit(v, sign * j, count) for j, v in enumerate(odd)]
    return [add(e, t) for e, t in zip(even, turned)] + [sub(e, t) for e, t in zip(even, turned)]


def odd_freqs(first, second, count):
    turned = [
        times_unit((a, -b), -r, count) for r, (a, b) in enumerate(zip(first, second))
    ]
    return {4 * j + 1: v for j, v in enumerate(complex_dft(turned, -1))}


def real_dft(values, count):
    half, quarter = count // 2, count // 4
    if count == 2:
        return [(values[0] + values[1], None), (values[0] - values[1], None)]
    if len(values) == half:
        folded, apart = values, values
    else:
        folded = [values[r] + values[r + half] for r in range(half)]
        apart = [values[r] - values[r + half] for r in range(half)]
    out = [None] * (half + 1)
    out[0::2] = real_dft(folded, half)
    for freq, value in odd_freqs(apart[:quarter], apart[quarter:], count).items():
        if freq <= half:
            out[freq] = value
        else:
            out[count - freq] = conj(value)
    return out


def real_inverse(freqs, count, keep_half):
    half, quarter = count // 2, count // 4
    if count == 2:
        first, last = freqs[0][0], freqs[1][0]
        return [first + last, first - last]
    even = real_inverse(freqs[0::2], half, False)
    picked = [
        freqs[4 * j + 1] if 4 * j + 1 <= half else conj(freqs[count - 4 * j - 1])
        for j in range(quarter)
    ]
    turned = [times_unit(v, r, count) for r, v in enumerate(complex_dft(picked, 1))]
    odd = [re for re, _ in turned] + [-im for _, im in turned]
    low = [e + o for e, o in zip(even, odd)]
    if keep_half:
        return low
    return low + [e - o for e, o in zip(even, odd)]


def split_table(table):
    high = table.astype(np.float32).astype(BF16)
    low = (table - high.astype(np.float64)).astype(BF16)
    return np.stack([high, low])


def lane_tables():
    idx = np.arange(LANES)
    angle = 2.0 * np.pi / LANES * (idx[:, None] * idx[None, :] % LANES)
    cos, sin = np.cos(angle), np.sin(angle)
    forward = np.block([[cos, -sin], [sin, cos]])
    inverse = np.block([[cos, sin], [-sin, cos]])
    return split_table(forward), split_table(inverse)


def twist_tables(factor):
    padded = FREQS * LANES
    angle = 2.0 * np.pi / padded * (np.arange(HALF)[:, None] * np.arange(LANES)[None, :])
    weight = np.full((HALF, 1), 2.0)
    weight[0] = weight[-1] = 1.0
    weight = weight / padded * factor
    cos, sin = np.cos(angle), np.sin(angle)
    return np.stack([cos, sin, cos * weight, sin * weight], axis=1).astype(np.float32)


def split_value(value):
    high = value.astype(BF16)
    return high, (value - high.astype(F32)).astype(BF16)


def start_copies(pairs, sems):
    copies = [pltpu.make_async_copy(a, b, sems.at[i]) for i, (a, b) in enumerate(pairs)]
    for copy in copies:
        copy.start()
    return copies


def gate_kernel(query, key, value, grad, taps, out, *scratch):
    held, sems = scratch[:5], scratch[5]
    key_v, value_v, grad_v, query_v, taps_v = held
    peers = out.shape[0]
    own = taps.shape[1] // peers
    share = out.shape[1] - 2 * own
    pieces = LANES // own
    width = taps.shape[1] // GROUPS
    begin = lax.axis_index("pl") * share
    arrivals = []
    for group in range(GROUPS):
        cols = pl.ds(group * width, width)
        pairs = [(a.at[:, cols], b.at[:, cols]) for a, b in zip((key, value, grad, query, taps), held)]
        arrivals.append(start_copies(pairs, sems.at[group]))
    for group, copies in enumerate(arrivals):
        for copy in copies:
            copy.wait()
        tiles = width // LANES
        for tile in range(group * tiles, (group + 1) * tiles):
            cols = pl.ds(tile * LANES, LANES)
            mixed = (key_v[:, cols].astype(F32) * value_v[:, cols].astype(F32)).astype(BF16)
            state = (grad_v[:, cols].astype(F32) * query_v[:, cols].astype(F32)).astype(BF16)
            for place, block in enumerate((mixed, state)):
                turned = block.T
                for i in range(pieces):
                    rows = pl.ds(place * own, own)
                    out[tile * pieces + i, rows, :] = turned[i * own : (i + 1) * own]
            turned = taps_v[:, cols].T
            for i in range(pieces):
                low = turned[i * own : i * own + share]
                high = turned[i * own + share : (i + 1) * own]
                rows = pl.ds(2 * own, share)
                out[tile * pieces + i, rows, :] = jnp.where(begin == 0, low, high)


def spectrum(get_row, twist_ref, lane_ref):
    freqs = real_dft([get_row(r) for r in range(ROWS)], FREQS)
    rows = []
    for k, (re, im) in enumerate(freqs):
        cos, sin = twist_ref[k, 0:1, :], twist_ref[k, 1:2, :]
        if im is None:
            rows.append(jnp.concatenate([re * cos, -re * sin], axis=1))
        else:
            rows.append(jnp.concatenate([re * cos + im * sin, im * cos - re * sin], axis=1))
    return lane_product(jnp.concatenate(rows, axis=0), lane_ref)


def lane_product(value, table_ref):
    high, low = split_value(value)
    out = jnp.dot(high, table_ref[0], preferred_element_type=F32)
    out += jnp.dot(low, table_ref[0], preferred_element_type=F32)
    return out + jnp.dot(high, table_ref[1], preferred_element_type=F32)


def conj_product(first, second):
    are, aim = first[:, :LANES], first[:, LANES:]
    bre, bim = second[:, :LANES], second[:, LANES:]
    return jnp.concatenate([are * bre + aim * bim, are * bim - aim * bre], axis=1)


def plain_product(first, second):
    are, aim = first[:, :LANES], first[:, LANES:]
    bre, bim = second[:, :LANES], second[:, LANES:]
    return jnp.concatenate([are * bre - aim * bim, are * bim + aim * bre], axis=1)


def signal_rows(spec, twist_ref, back_lane_ref):
    back = lane_product(spec, back_lane_ref)
    freqs = []
    for k in range(HALF):
        re = back[k * CHUNK : (k + 1) * CHUNK, :LANES]
        im = back[k * CHUNK : (k + 1) * CHUNK, LANES:]
        cos, sin = twist_ref[k, 2:3, :], twist_ref[k, 3:4, :]
        if k in (0, ROWS):
            freqs.append((re * cos - im * sin, None))
        else:
            freqs.append((re * cos - im * sin, im * cos + re * sin))
    return real_inverse(freqs, FREQS, True)


def taps_grad_kernel(signals, lane_ref, back_lane_ref, twist_ref, spec_ref, out):
    batch = signals.shape[0] // ROWS
    chans = out.shape[1]
    total = HALF * chans

    def chunk(first):
        rows = {}
        for which in range(2):
            place = pl.ds(which * chans + first, CHUNK)
            for b in range(batch):
                rows[which, b] = spectrum(
                    lambda r: signals[b * ROWS + r, place, :].astype(F32), twist_ref, lane_ref
                )
                base = (which * batch + b) * total
                for k in range(HALF):
                    spec_ref[pl.ds(base + k * chans + first, CHUNK), :] = rows[which, b][
                        k * CHUNK : (k + 1) * CHUNK
                    ]
        product = conj_product(rows[0, 0], rows[1, 0])
        for b in range(1, batch):
            product = product + conj_product(rows[0, b], rows[1, b])
        for r, row in enumerate(signal_rows(product, twist_ref, back_lane_ref)):
            out[r, pl.ds(first, CHUNK), :] = row.astype(BF16)

    for first in range(0, chans, CHUNK):
        chunk(first)


def state_kernel(signals, spec_ref, gain_ref, lane_ref, back_lane_ref, twist_ref, out, skip_ref):
    batch = signals.shape[0] // ROWS
    chans = out.shape[1] // 2
    share = signals.shape[1] - 2 * chans
    total = HALF * chans
    place = lax.axis_index("pl") * lax.axis_size("seq") + lax.axis_index("seq")
    pieces = LANES // chans
    gains = jnp.broadcast_to(gain_ref[pl.ds(place // pieces, 1), :], (LANES, LANES))
    skip_ref[...] = gains.T
    begin = pl.multiple_of(place % pieces * chans, chans)
    for first in range(0, chans, CHUNK):
        source, place = divmod(first, share)
        taps = spectrum(
            lambda r: signals[source * ROWS + r, pl.ds(2 * chans + place, CHUNK), :].astype(F32),
            twist_ref,
            lane_ref,
        )
        skip = skip_ref[pl.ds(begin + first, CHUNK), :]
        for which, product in enumerate((plain_product, conj_product)):
            place = pl.ds(which * chans + first, CHUNK)
            for b in range(batch):
                base = (which * batch + b) * total + first
                other = [spec_ref[pl.ds(base + k * chans, CHUNK), :] for k in range(HALF)]
                spec = product(taps, jnp.concatenate(other, axis=0))
                for r, row in enumerate(signal_rows(spec, twist_ref, back_lane_ref)):
                    own = signals[b * ROWS + r, place, :].astype(F32)
                    out[b * ROWS + r, place, :] = (row + skip * own).astype(BF16)


def output_kernel(back, query, key, value, grad, *refs):
    outs, held, sems = refs[:5], refs[5:10], refs[10]
    own = back.shape[1] // 3
    pieces = LANES // own
    width = query.shape[1] // GROUPS
    sent = []
    for group in range(GROUPS):
        for tile in range(group * width // LANES, (group + 1) * width // LANES):
            cols = pl.ds(tile * LANES, LANES)
            state, dmixed, term = (
                jnp.concatenate(
                    [back[tile * pieces + i, pl.ds(which * own, own), :] for i in range(pieces)],
                    axis=0,
                ).T
                for which in range(3)
            )
            state, dmixed = state.astype(F32), dmixed.astype(F32)
            held[0][:, cols] = (query[:, cols].astype(F32) * state).astype(BF16)
            held[1][:, cols] = (grad[:, cols].astype(F32) * state).astype(BF16)
            held[2][:, cols] = (dmixed * value[:, cols].astype(F32)).astype(BF16)
            held[3][:, cols] = (dmixed * key[:, cols].astype(F32)).astype(BF16)
            held[4][:, cols] = term
        cols = pl.ds(group * width, width)
        pairs = [(a.at[:, cols], b.at[:, cols]) for a, b in zip(held, outs)]
        sent += start_copies(pairs, sems.at[group])
    for copy in sent:
        copy.wait()


def call(kernel, shapes, args, scratch=(), in_hbm=False, out_hbm=False, flops=0, moved=2 << 20, limit=24):
    place = lambda hbm: pl.BlockSpec(memory_space=pltpu.HBM if hbm else pltpu.VMEM)
    return pl.pallas_call(
        kernel,
        out_shape=shapes,
        in_specs=[place(in_hbm)] * len(args),
        out_specs=jax.tree.map(lambda _: place(out_hbm), shapes),
        scratch_shapes=list(scratch),
        compiler_params=pltpu.CompilerParams(vmem_limit_bytes=limit << 20),
        cost_estimate=pl.CostEstimate(flops=flops, bytes_accessed=moved, transcendentals=0),
    )(*[pltpu.with_memory_space_constraint(a, pltpu.HBM) for a in args] if in_hbm else args)


def gate(query, key, value, grad, taps, peers):
    rows_dev, chan_dev = query.shape
    own = chan_dev // peers
    out_shape = (peers, 2 * own + own // 2, rows_dev)
    return call(
        gate_kernel,
        jax.ShapeDtypeStruct(out_shape, BF16),
        (query, key, value, grad, taps),
        [pltpu.VMEM((rows_dev, chan_dev), BF16)] * 5
        + [
            pltpu.SemaphoreType.DMA((GROUPS, 5)),
        ],
        in_hbm=True,
    )


def taps_grad(signals, own, factor):
    total = HALF * own
    batch = signals.shape[0] // ROWS
    forward_lane, inverse_lane = lane_tables()
    shape = jax.ShapeDtypeStruct
    return call(
        taps_grad_kernel,
        (
            shape((2 * batch * total, 2 * LANES), F32),
            shape((ROWS, own, LANES), BF16),
        ),
        (signals, forward_lane, inverse_lane, twist_tables(factor)),
        flops=5 * 10**9,
    )


def states(signals, spectra, skip_gain, own):
    total = HALF * own
    batch = signals.shape[0] // ROWS
    forward_lane, inverse_lane = lane_tables()
    return call(
        state_kernel,
        jax.ShapeDtypeStruct((batch * ROWS, 2 * own, LANES), BF16),
        (signals, spectra, skip_gain.reshape(-1, LANES), forward_lane, inverse_lane, twist_tables(1.0)),
        (pltpu.VMEM((LANES, LANES), F32),),
        flops=5 * 10**9,
    )


def outputs(back, query, key, value, grad):
    block = jax.ShapeDtypeStruct(query.shape, BF16)
    return call(
        output_kernel,
        (block,) * 5,
        (back, query, key, value, grad),
        [pltpu.VMEM(query.shape, BF16)] * 5 + [pltpu.SemaphoreType.DMA((GROUPS, 5))],
        out_hbm=True,
    )


def on_device(query_in, key_in, value_in, filter_taps, skip_gain, grad_out):
    seq_count, pair = lax.axis_size("seq"), lax.axis_size("pl")
    peers = seq_count * pair
    rows_dev, chan_dev = query_in.shape[1:]
    own = chan_dev // peers
    batch = query_in.shape[0] * lax.axis_size("dh") * lax.axis_size("dm") * pair
    factor = 1.0 / math.sqrt(batch * seq_count * rows_dev)
    query, key, value, grad = query_in[0], key_in[0], value_in[0], grad_out[0]

    def swap(values, axes):
        return lax.all_to_all(values, axes, split_axis=0, concat_axis=0, tiled=True)

    signals = swap(gate(query, key, value, grad, filter_taps, peers), ("pl", "seq"))
    spectra, term = taps_grad(signals, own, factor)

    def exchange(values, axis):
        return lax.ppermute(values, axis, [(0, 1), (1, 0)])

    def plus(a, b):
        return (a.astype(F32) + b.astype(F32)).astype(BF16)

    taken = exchange(term, "dm")
    results = states(signals, spectra, skip_gain, own)
    taken, results = lax.optimization_barrier((taken, results))
    term = plus(term, taken)
    term = plus(term, exchange(term, "dh"))
    copies = jnp.broadcast_to(term[None], (pair,) + term.shape).reshape((peers,) + term.shape[1:])
    back = swap(jnp.concatenate([results, copies], axis=1), ("pl", "seq"))
    outs = outputs(back, query, key, value, grad)
    return tuple(out[None] for out in outs[:4]) + (outs[4],)


def solution(mesh):
    dp, chan, seq = (mesh.shape[name] for name in ("dp", "chan", "seq"))
    split_mesh = Mesh(
        mesh.devices.reshape(dp // 4, 2, 2, chan, seq), ("dh", "dm", "pl", "chan", "seq")
    )
    rows = P(("dh", "dm", "pl"), "seq", "chan")
    taps = P("seq", "chan")
    return jax.shard_map(
        on_device,
        mesh=split_mesh,
        in_specs=(rows, rows, rows, taps, P("chan"), rows),
        out_specs=(rows, rows, rows, rows, taps),
        check_vma=False,
    )
```

```python
import functools
import math

import jax
import jax.numpy as jnp
import numpy as np
from jax import lax
from jax.experimental import pallas as pl
from jax.experimental.pallas import tpu as pltpu
from jax.sharding import Mesh
from jax.sharding import PartitionSpec as P

F32 = jnp.float32
BF16 = jnp.bfloat16
LANES = 128
ROWS = 16
FREQS = 2 * ROWS
HALF = ROWS + 1
CHUNK = 16
GROUPS = 2


def unit(numer, denom):
    angle = 2.0 * math.pi * numer / denom
    return (math.cos(angle), math.sin(angle))


def times_unit(value, numer, denom):
    re, im = value
    numer = numer % denom
    if 4 * numer % denom == 0:
        return ((re, im), (-im, re), (-re, -im), (im, -re))[4 * numer // denom]
    if 8 * numer % denom == 0:
        root = math.sqrt(0.5)
        summed, apart = (re + im) * root, (re - im) * root
        return {1: (apart, summed), 3: (-summed, apart), 5: (-apart, -summed), 7: (summed, -apart)}[
            8 * numer // denom
        ]
    cos, sin = unit(numer, denom)
    return (re * cos - im * sin, re * sin + im * cos)


def add(a, b):
    return (a[0] + b[0], a[1] + b[1])


def sub(a, b):
    return (a[0] - b[0], a[1] - b[1])


def conj(a):
    return (a[0], -a[1])


def complex_dft(values, sign):
    count = len(values)
    if count == 1:
        return list(values)
    even = complex_dft(values[0::2], sign)
    odd = complex_dft(values[1::2], sign)
    turned = [times_unit(v, sign * j, count) for j, v in enumerate(odd)]
    return [add(e, t) for e, t in zip(even, turned)] + [sub(e, t) for e, t in zip(even, turned)]


def odd_freqs(first, second, count):
    turned = [
        times_unit((a, -b), -r, count) for r, (a, b) in enumerate(zip(first, second))
    ]
    return {4 * j + 1: v for j, v in enumerate(complex_dft(turned, -1))}


def real_dft(values, count):
    half, quarter = count // 2, count // 4
    if count == 2:
        return [(values[0] + values[1], None), (values[0] - values[1], None)]
    if len(values) == half:
        folded, apart = values, values
    else:
        folded = [values[r] + values[r + half] for r in range(half)]
        apart = [values[r] - values[r + half] for r in range(half)]
    out = [None] * (half + 1)
    out[0::2] = real_dft(folded, half)
    for freq, value in odd_freqs(apart[:quarter], apart[quarter:], count).items():
        if freq <= half:
            out[freq] = value
        else:
            out[count - freq] = conj(value)
    return out


def real_inverse(freqs, count, keep_half):
    half, quarter = count // 2, count // 4
    if count == 2:
        first, last = freqs[0][0], freqs[1][0]
        return [first + last, first - last]
    even = real_inverse(freqs[0::2], half, False)
    picked = [
        freqs[4 * j + 1] if 4 * j + 1 <= half else conj(freqs[count - 4 * j - 1])
        for j in range(quarter)
    ]
    turned = [times_unit(v, r, count) for r, v in enumerate(complex_dft(picked, 1))]
    odd = [re for re, _ in turned] + [-im for _, im in turned]
    low = [e + o for e, o in zip(even, odd)]
    if keep_half:
        return low
    return low + [e - o for e, o in zip(even, odd)]


def split_table(table):
    high = table.astype(np.float32).astype(BF16)
    low = (table - high.astype(np.float64)).astype(BF16)
    return np.stack([high, low])


def lane_tables():
    idx = np.arange(LANES)
    angle = 2.0 * np.pi / LANES * (idx[:, None] * idx[None, :] % LANES)
    cos, sin = np.cos(angle), np.sin(angle)
    forward = np.block([[cos, -sin], [sin, cos]])
    inverse = np.block([[cos, sin], [-sin, cos]])
    return split_table(forward), split_table(inverse)


def twist_tables(factor):
    padded = FREQS * LANES
    angle = 2.0 * np.pi / padded * (np.arange(HALF)[:, None] * np.arange(LANES)[None, :])
    weight = np.full((HALF, 1), 2.0)
    weight[0] = weight[-1] = 1.0
    weight = weight / padded * factor
    cos, sin = np.cos(angle), np.sin(angle)
    return np.stack([cos, sin, cos * weight, sin * weight], axis=1).astype(np.float32)


def split_value(value):
    high = value.astype(BF16)
    return high, (value - high.astype(F32)).astype(BF16)


def start_copies(pairs, sems):
    copies = [pltpu.make_async_copy(a, b, sems.at[i]) for i, (a, b) in enumerate(pairs)]
    for copy in copies:
        copy.start()
    return copies


def gate_kernel(query, key, value, grad, taps, out, *scratch):
    held, sems = scratch[:5], scratch[5]
    key_v, value_v, grad_v, query_v, taps_v = held
    peers = out.shape[0]
    own = taps.shape[1] // peers
    share = out.shape[1] - 2 * own
    pieces = LANES // own
    width = taps.shape[1] // GROUPS
    begin = lax.axis_index("pl") * share
    arrivals = []
    for group in range(GROUPS):
        cols = pl.ds(group * width, width)
        pairs = [(a.at[:, cols], b.at[:, cols]) for a, b in zip((key, value, grad, query, taps), held)]
        arrivals.append(start_copies(pairs, sems.at[group]))
    for group, copies in enumerate(arrivals):
        for copy in copies:
            copy.wait()
        tiles = width // LANES
        for tile in range(group * tiles, (group + 1) * tiles):
            cols = pl.ds(tile * LANES, LANES)
            mixed = (key_v[:, cols].astype(F32) * value_v[:, cols].astype(F32)).astype(BF16)
            state = (grad_v[:, cols].astype(F32) * query_v[:, cols].astype(F32)).astype(BF16)
            for place, block in enumerate((mixed, state)):
                turned = block.T
                for i in range(pieces):
                    rows = pl.ds(place * own, own)
                    out[tile * pieces + i, rows, :] = turned[i * own : (i + 1) * own]
            turned = taps_v[:, cols].T
            for i in range(pieces):
                low = turned[i * own : i * own + share]
                high = turned[i * own + share : (i + 1) * own]
                rows = pl.ds(2 * own, share)
                out[tile * pieces + i, rows, :] = jnp.where(begin == 0, low, high)


def spectrum(get_row, twist_ref, lane_ref):
    freqs = real_dft([get_row(r) for r in range(ROWS)], FREQS)
    rows = []
    for k, (re, im) in enumerate(freqs):
        cos, sin = twist_ref[k, 0:1, :], twist_ref[k, 1:2, :]
        if im is None:
            rows.append(jnp.concatenate([re * cos, -re * sin], axis=1))
        else:
            rows.append(jnp.concatenate([re * cos + im * sin, im * cos - re * sin], axis=1))
    return lane_product(jnp.concatenate(rows, axis=0), lane_ref)


def lane_product(value, table_ref):
    high, low = split_value(value)
    out = jnp.dot(high, table_ref[0], preferred_element_type=F32)
    out += jnp.dot(low, table_ref[0], preferred_element_type=F32)
    return out + jnp.dot(high, table_ref[1], preferred_element_type=F32)


def conj_product(first, second):
    are, aim = first[:, :LANES], first[:, LANES:]
    bre, bim = second[:, :LANES], second[:, LANES:]
    return jnp.concatenate([are * bre + aim * bim, are * bim - aim * bre], axis=1)


def plain_product(first, second):
    are, aim = first[:, :LANES], first[:, LANES:]
    bre, bim = second[:, :LANES], second[:, LANES:]
    return jnp.concatenate([are * bre - aim * bim, are * bim + aim * bre], axis=1)


def signal_rows(spec, twist_ref, back_lane_ref):
    back = lane_product(spec, back_lane_ref)
    freqs = []
    for k in range(HALF):
        re = back[k * CHUNK : (k + 1) * CHUNK, :LANES]
        im = back[k * CHUNK : (k + 1) * CHUNK, LANES:]
        cos, sin = twist_ref[k, 2:3, :], twist_ref[k, 3:4, :]
        if k in (0, ROWS):
            freqs.append((re * cos - im * sin, None))
        else:
            freqs.append((re * cos - im * sin, im * cos + re * sin))
    return real_inverse(freqs, FREQS, True)


def taps_grad_kernel(first, signals, lane_ref, back_lane_ref, twist_ref, spec_ref, out):
    batch = signals.shape[0] // ROWS
    chans = 2 * (signals.shape[1] // 5)
    rows = {}
    for which in range(2):
        place = pl.ds(which * chans + first, CHUNK)
        for b in range(batch):
            rows[which, b] = spectrum(
                lambda r: signals[b * ROWS + r, place, :].astype(F32), twist_ref, lane_ref
            )
            spec_ref[which * batch + b] = rows[which, b]
    product = conj_product(rows[0, 0], rows[1, 0])
    for b in range(1, batch):
        product = product + conj_product(rows[0, b], rows[1, b])
    for r, row in enumerate(signal_rows(product, twist_ref, back_lane_ref)):
        out[r] = row.astype(BF16)


def state_kernel(signals, gain_ref, lane_ref, back_lane_ref, twist_ref, *refs):
    *specs, out, skip_ref = refs
    batch = signals.shape[0] // ROWS
    chans = out.shape[1] // 2
    share = signals.shape[1] - 2 * chans
    place = lax.axis_index("pl") * lax.axis_size("seq") + lax.axis_index("seq")
    pieces = LANES // chans
    gains = jnp.broadcast_to(gain_ref[pl.ds(place // pieces, 1), :], (LANES, LANES))
    skip_ref[...] = gains.T
    begin = pl.multiple_of(place % pieces * chans, chans)
    for first in range(0, chans, CHUNK):
        source, place = divmod(first, share)
        taps = spectrum(
            lambda r: signals[source * ROWS + r, pl.ds(2 * chans + place, CHUNK), :].astype(F32),
            twist_ref,
            lane_ref,
        )
        skip = skip_ref[pl.ds(begin + first, CHUNK), :]
        for which, product in enumerate((plain_product, conj_product)):
            place = pl.ds(which * chans + first, CHUNK)
            for b in range(batch):
                spec = product(taps, specs[first // CHUNK][which * batch + b])
                for r, row in enumerate(signal_rows(spec, twist_ref, back_lane_ref)):
                    own = signals[b * ROWS + r, place, :].astype(F32)
                    out[b * ROWS + r, place, :] = (row + skip * own).astype(BF16)


def output_kernel(back, query, key, value, grad, *refs):
    outs, held, sems = refs[:5], refs[5:10], refs[10]
    own = back.shape[1] // 3
    pieces = LANES // own
    width = query.shape[1] // GROUPS
    sent = []
    for group in range(GROUPS):
        for tile in range(group * width // LANES, (group + 1) * width // LANES):
            cols = pl.ds(tile * LANES, LANES)
            state, dmixed, term = (
                jnp.concatenate(
                    [back[tile * pieces + i, pl.ds(which * own, own), :] for i in range(pieces)],
                    axis=0,
                ).T
                for which in range(3)
            )
            state, dmixed = state.astype(F32), dmixed.astype(F32)
            held[0][:, cols] = (query[:, cols].astype(F32) * state).astype(BF16)
            held[1][:, cols] = (grad[:, cols].astype(F32) * state).astype(BF16)
            held[2][:, cols] = (dmixed * value[:, cols].astype(F32)).astype(BF16)
            held[3][:, cols] = (dmixed * key[:, cols].astype(F32)).astype(BF16)
            held[4][:, cols] = term
        cols = pl.ds(group * width, width)
        pairs = [(a.at[:, cols], b.at[:, cols]) for a, b in zip(held, outs)]
        sent += start_copies(pairs, sems.at[group])
    for copy in sent:
        copy.wait()


def call(kernel, shapes, args, scratch=(), in_hbm=False, out_hbm=False, flops=0, moved=2 << 20, limit=24):
    place = lambda hbm: pl.BlockSpec(memory_space=pltpu.HBM if hbm else pltpu.VMEM)
    return pl.pallas_call(
        kernel,
        out_shape=shapes,
        in_specs=[place(in_hbm)] * len(args),
        out_specs=jax.tree.map(lambda _: place(out_hbm), shapes),
        scratch_shapes=list(scratch),
        compiler_params=pltpu.CompilerParams(vmem_limit_bytes=limit << 20),
        cost_estimate=pl.CostEstimate(flops=flops, bytes_accessed=moved, transcendentals=0),
    )(*[pltpu.with_memory_space_constraint(a, pltpu.HBM) for a in args] if in_hbm else args)


def gate(query, key, value, grad, taps, peers):
    rows_dev, chan_dev = query.shape
    own = chan_dev // peers
    out_shape = (peers, 2 * own + own // 2, rows_dev)
    return call(
        gate_kernel,
        jax.ShapeDtypeStruct(out_shape, BF16),
        (query, key, value, grad, taps),
        [pltpu.VMEM((rows_dev, chan_dev), BF16)] * 5
        + [
            pltpu.SemaphoreType.DMA((GROUPS, 5)),
        ],
        in_hbm=True,
    )


def taps_grad(signals, first, factor):
    batch = signals.shape[0] // ROWS
    forward_lane, inverse_lane = lane_tables()
    shape = jax.ShapeDtypeStruct
    return call(
        functools.partial(taps_grad_kernel, first),
        (
            shape((2 * batch, HALF * CHUNK, 2 * LANES), F32),
            shape((ROWS, CHUNK, LANES), BF16),
        ),
        (signals, forward_lane, inverse_lane, twist_tables(factor)),
        flops=2 * 10**9,
    )


def states(signals, spectra, skip_gain, own):
    batch = signals.shape[0] // ROWS
    forward_lane, inverse_lane = lane_tables()
    return call(
        state_kernel,
        jax.ShapeDtypeStruct((batch * ROWS, 2 * own, LANES), BF16),
        (signals, skip_gain.reshape(-1, LANES), forward_lane, inverse_lane, twist_tables(1.0), *spectra),
        (pltpu.VMEM((LANES, LANES), F32),),
        flops=3 * 10**9,
    )


def outputs(back, query, key, value, grad):
    block = jax.ShapeDtypeStruct(query.shape, BF16)
    return call(
        output_kernel,
        (block,) * 5,
        (back, query, key, value, grad),
        [pltpu.VMEM(query.shape, BF16)] * 5 + [pltpu.SemaphoreType.DMA((GROUPS, 5))],
        out_hbm=True,
    )


def on_device(query_in, key_in, value_in, filter_taps, skip_gain, grad_out):
    seq_count, pair = lax.axis_size("seq"), lax.axis_size("pl")
    peers = seq_count * pair
    rows_dev, chan_dev = query_in.shape[1:]
    own = chan_dev // peers
    batch = query_in.shape[0] * lax.axis_size("dh") * lax.axis_size("dm") * pair
    factor = 1.0 / math.sqrt(batch * seq_count * rows_dev)
    query, key, value, grad = query_in[0], key_in[0], value_in[0], grad_out[0]

    def swap(values, axes):
        return lax.all_to_all(values, axes, split_axis=0, concat_axis=0, tiled=True)

    signals = swap(gate(query, key, value, grad, filter_taps, peers), ("pl", "seq"))

    def exchange(values, axis):
        return lax.ppermute(values, axis, [(0, 1), (1, 0)])

    def plus(a, b):
        return (a.astype(F32) + b.astype(F32)).astype(BF16)

    spectra, terms = zip(*(taps_grad(signals, first, factor) for first in range(0, own, CHUNK)))
    orders = [("dm", "dh"), ("dh", "dm")]
    terms = [plus(term, exchange(term, order[0])) for term, order in zip(terms, orders)]
    others = [exchange(term, order[1]) for term, order in zip(terms, orders)]
    spectra, _ = lax.optimization_barrier((spectra, terms[0]))
    results = states(signals, spectra, skip_gain, own)
    others, results = lax.optimization_barrier((others, results))
    terms = [plus(term, other) for term, other in zip(terms, others)]
    copies = [jnp.broadcast_to(t[None], (pair,) + t.shape).reshape((peers,) + t.shape[1:]) for t in terms]
    back = swap(jnp.concatenate([results, *copies], axis=1), ("pl", "seq"))
    outs = outputs(back, query, key, value, grad)
    return tuple(out[None] for out in outs[:4]) + (outs[4],)


def solution(mesh):
    dp, chan, seq = (mesh.shape[name] for name in ("dp", "chan", "seq"))
    split_mesh = Mesh(
        mesh.devices.reshape(dp // 4, 2, 2, chan, seq), ("dh", "dm", "pl", "chan", "seq")
    )
    rows = P(("dh", "dm", "pl"), "seq", "chan")
    taps = P("seq", "chan")
    return jax.shard_map(
        on_device,
        mesh=split_mesh,
        in_specs=(rows, rows, rows, taps, P("chan"), rows),
        out_specs=(rows, rows, rows, rows, taps),
        check_vma=False,
    )
```

```python
import functools
import math

import jax
import jax.numpy as jnp
import numpy as np
from jax import lax
from jax.experimental import pallas as pl
from jax.experimental.pallas import tpu as pltpu
from jax.sharding import Mesh
from jax.sharding import PartitionSpec as P

F32 = jnp.float32
BF16 = jnp.bfloat16
LANES = 128
ROWS = 16
FREQS = 2 * ROWS
HALF = ROWS + 1
CHUNK = 16
GROUPS = 2


def unit(numer, denom):
    angle = 2.0 * math.pi * numer / denom
    return (math.cos(angle), math.sin(angle))


def times_unit(value, numer, denom):
    re, im = value
    numer = numer % denom
    if 4 * numer % denom == 0:
        return ((re, im), (-im, re), (-re, -im), (im, -re))[4 * numer // denom]
    if 8 * numer % denom == 0:
        root = math.sqrt(0.5)
        summed, apart = (re + im) * root, (re - im) * root
        return {1: (apart, summed), 3: (-summed, apart), 5: (-apart, -summed), 7: (summed, -apart)}[
            8 * numer // denom
        ]
    cos, sin = unit(numer, denom)
    return (re * cos - im * sin, re * sin + im * cos)


def add(a, b):
    return (a[0] + b[0], a[1] + b[1])


def sub(a, b):
    return (a[0] - b[0], a[1] - b[1])


def conj(a):
    return (a[0], -a[1])


def complex_dft(values, sign):
    count = len(values)
    if count == 1:
        return list(values)
    even = complex_dft(values[0::2], sign)
    odd = complex_dft(values[1::2], sign)
    turned = [times_unit(v, sign * j, count) for j, v in enumerate(odd)]
    return [add(e, t) for e, t in zip(even, turned)] + [sub(e, t) for e, t in zip(even, turned)]


def odd_freqs(first, second, count):
    turned = [
        times_unit((a, -b), -r, count) for r, (a, b) in enumerate(zip(first, second))
    ]
    return {4 * j + 1: v for j, v in enumerate(complex_dft(turned, -1))}


def real_dft(values, count):
    half, quarter = count // 2, count // 4
    if count == 2:
        return [(values[0] + values[1], None), (values[0] - values[1], None)]
    if len(values) == half:
        folded, apart = values, values
    else:
        folded = [values[r] + values[r + half] for r in range(half)]
        apart = [values[r] - values[r + half] for r in range(half)]
    out = [None] * (half + 1)
    out[0::2] = real_dft(folded, half)
    for freq, value in odd_freqs(apart[:quarter], apart[quarter:], count).items():
        if freq <= half:
            out[freq] = value
        else:
            out[count - freq] = conj(value)
    return out


def real_inverse(freqs, count, keep_half):
    half, quarter = count // 2, count // 4
    if count == 2:
        first, last = freqs[0][0], freqs[1][0]
        return [first + last, first - last]
    even = real_inverse(freqs[0::2], half, False)
    picked = [
        freqs[4 * j + 1] if 4 * j + 1 <= half else conj(freqs[count - 4 * j - 1])
        for j in range(quarter)
    ]
    turned = [times_unit(v, r, count) for r, v in enumerate(complex_dft(picked, 1))]
    odd = [re for re, _ in turned] + [-im for _, im in turned]
    low = [e + o for e, o in zip(even, odd)]
    if keep_half:
        return low
    return low + [e - o for e, o in zip(even, odd)]


def split_table(table):
    high = table.astype(np.float32).astype(BF16)
    low = (table - high.astype(np.float64)).astype(BF16)
    return np.stack([high, low])


def lane_tables():
    idx = np.arange(LANES)
    angle = 2.0 * np.pi / LANES * (idx[:, None] * idx[None, :] % LANES)
    cos, sin = np.cos(angle), np.sin(angle)
    forward = np.block([[cos, -sin], [sin, cos]])
    inverse = np.block([[cos, sin], [-sin, cos]])
    return split_table(forward), split_table(inverse)


def twist_tables(factor):
    padded = FREQS * LANES
    angle = 2.0 * np.pi / padded * (np.arange(HALF)[:, None] * np.arange(LANES)[None, :])
    weight = np.full((HALF, 1), 2.0)
    weight[0] = weight[-1] = 1.0
    weight = weight / padded * factor
    cos, sin = np.cos(angle), np.sin(angle)
    return np.stack([cos, sin, cos * weight, sin * weight], axis=1).astype(np.float32)


def split_value(value):
    high = value.astype(BF16)
    return high, (value - high.astype(F32)).astype(BF16)


def start_copies(pairs, sems):
    copies = [pltpu.make_async_copy(a, b, sems.at[i]) for i, (a, b) in enumerate(pairs)]
    for copy in copies:
        copy.start()
    return copies


def gate_kernel(query, key, value, grad, taps, out, *scratch):
    held, sems = scratch[:5], scratch[5]
    key_v, value_v, grad_v, query_v, taps_v = held
    peers = out.shape[0]
    own = taps.shape[1] // peers
    share = out.shape[1] - 2 * own
    pieces = LANES // own
    width = taps.shape[1] // GROUPS
    begin = lax.axis_index("pl") * share
    arrivals = []
    for group in range(GROUPS):
        cols = pl.ds(group * width, width)
        pairs = [(a.at[:, cols], b.at[:, cols]) for a, b in zip((key, value, grad, query, taps), held)]
        arrivals.append(start_copies(pairs, sems.at[group]))
    for group, copies in enumerate(arrivals):
        for copy in copies:
            copy.wait()
        tiles = width // LANES
        for tile in range(group * tiles, (group + 1) * tiles):
            cols = pl.ds(tile * LANES, LANES)
            mixed = (key_v[:, cols].astype(F32) * value_v[:, cols].astype(F32)).astype(BF16)
            state = (grad_v[:, cols].astype(F32) * query_v[:, cols].astype(F32)).astype(BF16)
            for place, block in enumerate((mixed, state)):
                turned = block.T
                for i in range(pieces):
                    rows = pl.ds(place * own, own)
                    out[tile * pieces + i, rows, :] = turned[i * own : (i + 1) * own]
            turned = taps_v[:, cols].T
            for i in range(pieces):
                low = turned[i * own : i * own + share]
                high = turned[i * own + share : (i + 1) * own]
                rows = pl.ds(2 * own, share)
                out[tile * pieces + i, rows, :] = jnp.where(begin == 0, low, high)


def spectrum(get_row, twist_ref, lane_ref):
    freqs = real_dft([get_row(r) for r in range(ROWS)], FREQS)
    rows = []
    for k, (re, im) in enumerate(freqs):
        cos, sin = twist_ref[k, 0:1, :], twist_ref[k, 1:2, :]
        if im is None:
            rows.append(jnp.concatenate([re * cos, -re * sin], axis=1))
        else:
            rows.append(jnp.concatenate([re * cos + im * sin, im * cos - re * sin], axis=1))
    return lane_product(jnp.concatenate(rows, axis=0), lane_ref)


def lane_product(value, table_ref):
    high, low = split_value(value)
    out = jnp.dot(high, table_ref[0], preferred_element_type=F32)
    out += jnp.dot(low, table_ref[0], preferred_element_type=F32)
    return out + jnp.dot(high, table_ref[1], preferred_element_type=F32)


def conj_product(first, second):
    are, aim = first[:, :LANES], first[:, LANES:]
    bre, bim = second[:, :LANES], second[:, LANES:]
    return jnp.concatenate([are * bre + aim * bim, are * bim - aim * bre], axis=1)


def plain_product(first, second):
    are, aim = first[:, :LANES], first[:, LANES:]
    bre, bim = second[:, :LANES], second[:, LANES:]
    return jnp.concatenate([are * bre - aim * bim, are * bim + aim * bre], axis=1)


def signal_rows(spec, twist_ref, back_lane_ref):
    back = lane_product(spec, back_lane_ref)
    freqs = []
    for k in range(HALF):
        re = back[k * CHUNK : (k + 1) * CHUNK, :LANES]
        im = back[k * CHUNK : (k + 1) * CHUNK, LANES:]
        cos, sin = twist_ref[k, 2:3, :], twist_ref[k, 3:4, :]
        if k in (0, ROWS):
            freqs.append((re * cos - im * sin, None))
        else:
            freqs.append((re * cos - im * sin, im * cos + re * sin))
    return real_inverse(freqs, FREQS, True)


def half_start(kept):
    mine = lax.axis_index("dm")
    return pl.multiple_of((mine if kept else 1 - mine) * CHUNK, CHUNK)


def taps_grad_kernel(kept, signals, lane_ref, back_lane_ref, twist_ref, spec_ref, out):
    first = half_start(kept)
    batch = signals.shape[0] // ROWS
    chans = 2 * (signals.shape[1] // 5)
    rows = {}
    for which in range(2):
        place = pl.ds(pl.multiple_of(which * chans + first, CHUNK), CHUNK)
        for b in range(batch):
            rows[which, b] = spectrum(
                lambda r: signals[b * ROWS + r, place, :].astype(F32), twist_ref, lane_ref
            )
            spec_ref[which * batch + b] = rows[which, b]
    product = conj_product(rows[0, 0], rows[1, 0])
    for b in range(1, batch):
        product = product + conj_product(rows[0, b], rows[1, b])
    for r, row in enumerate(signal_rows(product, twist_ref, back_lane_ref)):
        out[r] = row.astype(BF16)


def state_kernel(signals, gain_ref, lane_ref, back_lane_ref, twist_ref, *refs):
    *specs, out, skip_ref = refs
    batch = signals.shape[0] // ROWS
    chans = out.shape[1] // 2
    share = signals.shape[1] - 2 * chans
    place = lax.axis_index("pl") * lax.axis_size("seq") + lax.axis_index("seq")
    pieces = LANES // chans
    gains = jnp.broadcast_to(gain_ref[pl.ds(place // pieces, 1), :], (LANES, LANES))
    skip_ref[...] = gains.T
    begin = pl.multiple_of(place % pieces * chans, chans)
    for kept, spec_ref in enumerate(specs):
        first = half_start(kept)
        source = first // share
        taps = spectrum(
            lambda r: signals[source * ROWS + r, pl.ds(2 * chans, CHUNK), :].astype(F32),
            twist_ref,
            lane_ref,
        )
        skip = skip_ref[pl.ds(pl.multiple_of(begin + first, CHUNK), CHUNK), :]
        for which, product in enumerate((plain_product, conj_product)):
            place = pl.ds(pl.multiple_of(which * chans + first, CHUNK), CHUNK)
            for b in range(batch):
                spec = product(taps, spec_ref[which * batch + b])
                for r, row in enumerate(signal_rows(spec, twist_ref, back_lane_ref)):
                    own = signals[b * ROWS + r, place, :].astype(F32)
                    out[b * ROWS + r, place, :] = (row + skip * own).astype(BF16)


def output_kernel(back, query, key, value, grad, *refs):
    outs, held, sems = refs[:5], refs[5:10], refs[10]
    own = back.shape[1] // 3
    pieces = LANES // own
    width = query.shape[1] // GROUPS
    places = (half_start(1), half_start(0))
    halves = [pl.ds(pl.multiple_of(2 * own + place, CHUNK), CHUNK) for place in places]
    sent = []
    for group in range(GROUPS):
        for tile in range(group * width // LANES, (group + 1) * width // LANES):
            cols = pl.ds(tile * LANES, LANES)
            blocks = [tile * pieces + i for i in range(pieces)]
            state, dmixed = (
                jnp.concatenate([back[i, pl.ds(which * own, own), :] for i in blocks], axis=0).T
                for which in range(2)
            )
            term = jnp.concatenate([back[i, half, :] for i in blocks for half in halves], axis=0).T
            state, dmixed = state.astype(F32), dmixed.astype(F32)
            held[0][:, cols] = (query[:, cols].astype(F32) * state).astype(BF16)
            held[1][:, cols] = (grad[:, cols].astype(F32) * state).astype(BF16)
            held[2][:, cols] = (dmixed * value[:, cols].astype(F32)).astype(BF16)
            held[3][:, cols] = (dmixed * key[:, cols].astype(F32)).astype(BF16)
            held[4][:, cols] = term
        cols = pl.ds(group * width, width)
        pairs = [(a.at[:, cols], b.at[:, cols]) for a, b in zip(held, outs)]
        sent += start_copies(pairs, sems.at[group])
    for copy in sent:
        copy.wait()


def call(kernel, shapes, args, scratch=(), in_hbm=False, out_hbm=False, flops=0, moved=2 << 20, limit=24):
    place = lambda hbm: pl.BlockSpec(memory_space=pltpu.HBM if hbm else pltpu.VMEM)
    return pl.pallas_call(
        kernel,
        out_shape=shapes,
        in_specs=[place(in_hbm)] * len(args),
        out_specs=jax.tree.map(lambda _: place(out_hbm), shapes),
        scratch_shapes=list(scratch),
        compiler_params=pltpu.CompilerParams(vmem_limit_bytes=limit << 20),
        cost_estimate=pl.CostEstimate(flops=flops, bytes_accessed=moved, transcendentals=0),
    )(*[pltpu.with_memory_space_constraint(a, pltpu.HBM) for a in args] if in_hbm else args)


def gate(query, key, value, grad, taps, peers):
    rows_dev, chan_dev = query.shape
    own = chan_dev // peers
    out_shape = (peers, 2 * own + own // 2, rows_dev)
    return call(
        gate_kernel,
        jax.ShapeDtypeStruct(out_shape, BF16),
        (query, key, value, grad, taps),
        [pltpu.VMEM((rows_dev, chan_dev), BF16)] * 5
        + [
            pltpu.SemaphoreType.DMA((GROUPS, 5)),
        ],
        in_hbm=True,
    )


def taps_grad(signals, kept, factor):
    batch = signals.shape[0] // ROWS
    forward_lane, inverse_lane = lane_tables()
    shape = jax.ShapeDtypeStruct
    return call(
        functools.partial(taps_grad_kernel, kept),
        (
            shape((2 * batch, HALF * CHUNK, 2 * LANES), F32),
            shape((ROWS, CHUNK, LANES), BF16),
        ),
        (signals, forward_lane, inverse_lane, twist_tables(factor)),
        flops=2 * 10**9,
    )


def states(signals, spectra, skip_gain, own):
    batch = signals.shape[0] // ROWS
    forward_lane, inverse_lane = lane_tables()
    return call(
        state_kernel,
        jax.ShapeDtypeStruct((batch * ROWS, 2 * own, LANES), BF16),
        (signals, skip_gain.reshape(-1, LANES), forward_lane, inverse_lane, twist_tables(1.0), *spectra),
        (pltpu.VMEM((LANES, LANES), F32),),
        flops=3 * 10**9,
    )


def outputs(back, query, key, value, grad):
    block = jax.ShapeDtypeStruct(query.shape, BF16)
    return call(
        output_kernel,
        (block,) * 5,
        (back, query, key, value, grad),
        [pltpu.VMEM(query.shape, BF16)] * 5 + [pltpu.SemaphoreType.DMA((GROUPS, 5))],
        out_hbm=True,
    )


def on_device(query_in, key_in, value_in, filter_taps, skip_gain, grad_out):
    seq_count, pair = lax.axis_size("seq"), lax.axis_size("pl")
    peers = seq_count * pair
    rows_dev, chan_dev = query_in.shape[1:]
    own = chan_dev // peers
    batch = query_in.shape[0] * lax.axis_size("dh") * lax.axis_size("dm") * pair
    factor = 1.0 / math.sqrt(batch * seq_count * rows_dev)
    query, key, value, grad = query_in[0], key_in[0], value_in[0], grad_out[0]

    def swap(values, axes):
        return lax.all_to_all(values, axes, split_axis=0, concat_axis=0, tiled=True)

    signals = swap(gate(query, key, value, grad, filter_taps, peers), ("pl", "seq"))

    def exchange(values, axis):
        return lax.ppermute(values, axis, [(0, 1), (1, 0)])

    def plus(a, b):
        return (a.astype(F32) + b.astype(F32)).astype(BF16)

    spectra, (given, term) = zip(*(taps_grad(signals, kept, factor) for kept in range(2)))
    term = plus(term, exchange(given, "dm"))
    other = exchange(term, "dh")
    spectra, _ = lax.optimization_barrier((spectra, term))
    results = states(signals, spectra, skip_gain, own)
    other, results = lax.optimization_barrier((other, results))
    term = plus(term, other)
    copies = [
        jnp.broadcast_to(t[None], (pair,) + t.shape).reshape((peers,) + t.shape[1:])
        for t in (term, exchange(term, "dm"))
    ]
    back = swap(jnp.concatenate([results, *copies], axis=1), ("pl", "seq"))
    outs = outputs(back, query, key, value, grad)
    return tuple(out[None] for out in outs[:4]) + (outs[4],)


def solution(mesh):
    dp, chan, seq = (mesh.shape[name] for name in ("dp", "chan", "seq"))
    split_mesh = Mesh(
        mesh.devices.reshape(dp // 4, 2, 2, chan, seq), ("dh", "dm", "pl", "chan", "seq")
    )
    rows = P(("dh", "dm", "pl"), "seq", "chan")
    taps = P("seq", "chan")
    return jax.shard_map(
        on_device,
        mesh=split_mesh,
        in_specs=(rows, rows, rows, taps, P("chan"), rows),
        out_specs=(rows, rows, rows, rows, taps),
        check_vma=False,
    )
```

```python
import functools
import math

import jax
import jax.numpy as jnp
import numpy as np
from jax import lax
from jax.experimental import pallas as pl
from jax.experimental.pallas import tpu as pltpu
from jax.sharding import Mesh
from jax.sharding import PartitionSpec as P

F32 = jnp.float32
BF16 = jnp.bfloat16
LANES = 128
ROWS = 16
SIDE = 4
FREQS = 2 * ROWS
HALF = ROWS + 1
CHUNK = 16
GROUPS = 2


def unit(numer, denom):
    angle = 2.0 * math.pi * numer / denom
    return (math.cos(angle), math.sin(angle))


def times_unit(value, numer, denom):
    re, im = value
    numer = numer % denom
    if 4 * numer % denom == 0:
        return ((re, im), (-im, re), (-re, -im), (im, -re))[4 * numer // denom]
    if 8 * numer % denom == 0:
        root = math.sqrt(0.5)
        summed, apart = (re + im) * root, (re - im) * root
        return {1: (apart, summed), 3: (-summed, apart), 5: (-apart, -summed), 7: (summed, -apart)}[
            8 * numer // denom
        ]
    cos, sin = unit(numer, denom)
    return (re * cos - im * sin, re * sin + im * cos)


def add(a, b):
    return (a[0] + b[0], a[1] + b[1])


def sub(a, b):
    return (a[0] - b[0], a[1] - b[1])


def conj(a):
    return (a[0], -a[1])


def complex_dft(values, sign):
    count = len(values)
    if count == 1:
        return list(values)
    even = complex_dft(values[0::2], sign)
    odd = complex_dft(values[1::2], sign)
    turned = [times_unit(v, sign * j, count) for j, v in enumerate(odd)]
    return [add(e, t) for e, t in zip(even, turned)] + [sub(e, t) for e, t in zip(even, turned)]


def odd_freqs(first, second, count):
    turned = [
        times_unit((a, -b), -r, count) for r, (a, b) in enumerate(zip(first, second))
    ]
    return {4 * j + 1: v for j, v in enumerate(complex_dft(turned, -1))}


def real_dft(values, count):
    half, quarter = count // 2, count // 4
    if count == 2:
        return [(values[0] + values[1], None), (values[0] - values[1], None)]
    if len(values) == half:
        folded, apart = values, values
    else:
        folded = [values[r] + values[r + half] for r in range(half)]
        apart = [values[r] - values[r + half] for r in range(half)]
    out = [None] * (half + 1)
    out[0::2] = real_dft(folded, half)
    for freq, value in odd_freqs(apart[:quarter], apart[quarter:], count).items():
        if freq <= half:
            out[freq] = value
        else:
            out[count - freq] = conj(value)
    return out


def real_inverse(freqs, count, keep_half):
    half, quarter = count // 2, count // 4
    if count == 2:
        first, last = freqs[0][0], freqs[1][0]
        return [first + last, first - last]
    even = real_inverse(freqs[0::2], half, False)
    picked = [
        freqs[4 * j + 1] if 4 * j + 1 <= half else conj(freqs[count - 4 * j - 1])
        for j in range(quarter)
    ]
    turned = [times_unit(v, r, count) for r, v in enumerate(complex_dft(picked, 1))]
    odd = [re for re, _ in turned] + [-im for _, im in turned]
    low = [e + o for e, o in zip(even, odd)]
    if keep_half:
        return low
    return low + [e - o for e, o in zip(even, odd)]


def split_table(table):
    high = table.astype(np.float32).astype(BF16)
    low = (table - high.astype(np.float64)).astype(BF16)
    return np.stack([high, low])


def lane_tables():
    idx = np.arange(LANES)
    angle = 2.0 * np.pi / LANES * (idx[:, None] * idx[None, :] % LANES)
    cos, sin = np.cos(angle), np.sin(angle)
    forward = np.block([[cos, -sin], [sin, cos]])
    inverse = np.block([[cos, sin], [-sin, cos]])
    return split_table(forward), split_table(inverse)


def twist_tables(factor):
    padded = FREQS * LANES
    angle = 2.0 * np.pi / padded * (np.arange(HALF)[:, None] * np.arange(LANES)[None, :])
    weight = np.full((HALF, 1), 2.0)
    weight[0] = weight[-1] = 1.0
    weight = weight / padded * factor
    cos, sin = np.cos(angle), np.sin(angle)
    return np.stack([cos, sin, cos * weight, sin * weight], axis=1).astype(np.float32)


def split_value(value):
    high = value.astype(BF16)
    return high, (value - high.astype(F32)).astype(BF16)


def start_copies(pairs, sems):
    copies = [pltpu.make_async_copy(a, b, sems.at[i]) for i, (a, b) in enumerate(pairs)]
    for copy in copies:
        copy.start()
    return copies


def gate_kernel(query, key, value, grad, taps, out, *scratch):
    held, sems = scratch[:5], scratch[5]
    key_v, value_v, grad_v, query_v, taps_v = held
    peers = out.shape[0]
    own = taps.shape[1] // peers
    share = out.shape[1] - 2 * own
    pieces = LANES // own
    width = taps.shape[1] // GROUPS
    begin = lax.axis_index("pl") * share
    arrivals = []
    for group in range(GROUPS):
        cols = pl.ds(group * width, width)
        pairs = [(a.at[:, cols], b.at[:, cols]) for a, b in zip((key, value, grad, query, taps), held)]
        arrivals.append(start_copies(pairs, sems.at[group]))
    for group, copies in enumerate(arrivals):
        for copy in copies:
            copy.wait()
        tiles = width // LANES
        for tile in range(group * tiles, (group + 1) * tiles):
            cols = pl.ds(tile * LANES, LANES)
            mixed = (key_v[:, cols].astype(F32) * value_v[:, cols].astype(F32)).astype(BF16)
            state = (grad_v[:, cols].astype(F32) * query_v[:, cols].astype(F32)).astype(BF16)
            for place, block in enumerate((mixed, state)):
                turned = block.T
                for i in range(pieces):
                    rows = pl.ds(place * own, own)
                    out[tile * pieces + i, rows, :] = turned[i * own : (i + 1) * own]
            turned = taps_v[:, cols].T
            for i in range(pieces):
                low = turned[i * own : i * own + share]
                high = turned[i * own + share : (i + 1) * own]
                rows = pl.ds(2 * own, share)
                out[tile * pieces + i, rows, :] = jnp.where(begin == 0, low, high)


def spectrum(get_row, twist_ref, lane_ref):
    freqs = real_dft([get_row(r) for r in range(ROWS)], FREQS)
    rows = []
    for k, (re, im) in enumerate(freqs):
        cos, sin = twist_ref[k, 0:1, :], twist_ref[k, 1:2, :]
        if im is None:
            rows.append(jnp.concatenate([re * cos, -re * sin], axis=1))
        else:
            rows.append(jnp.concatenate([re * cos + im * sin, im * cos - re * sin], axis=1))
    return lane_product(jnp.concatenate(rows, axis=0), lane_ref)


def lane_product(value, table_ref):
    high, low = split_value(value)
    out = jnp.dot(high, table_ref[0], preferred_element_type=F32)
    out += jnp.dot(low, table_ref[0], preferred_element_type=F32)
    return out + jnp.dot(high, table_ref[1], preferred_element_type=F32)


def conj_product(first, second):
    are, aim = first[:, :LANES], first[:, LANES:]
    bre, bim = second[:, :LANES], second[:, LANES:]
    return jnp.concatenate([are * bre + aim * bim, are * bim - aim * bre], axis=1)


def plain_product(first, second):
    are, aim = first[:, :LANES], first[:, LANES:]
    bre, bim = second[:, :LANES], second[:, LANES:]
    return jnp.concatenate([are * bre - aim * bim, are * bim + aim * bre], axis=1)


def signal_rows(spec, twist_ref, back_lane_ref):
    back = lane_product(spec, back_lane_ref)
    freqs = []
    for k in range(HALF):
        re = back[k * CHUNK : (k + 1) * CHUNK, :LANES]
        im = back[k * CHUNK : (k + 1) * CHUNK, LANES:]
        cos, sin = twist_ref[k, 2:3, :], twist_ref[k, 3:4, :]
        if k in (0, ROWS):
            freqs.append((re * cos - im * sin, None))
        else:
            freqs.append((re * cos - im * sin, im * cos + re * sin))
    return real_inverse(freqs, FREQS, True)


def slot(row):
    return row % SIDE * SIDE + row // SIDE


def half_start(kept):
    mine = lax.axis_index("dm")
    return pl.multiple_of((mine if kept else 1 - mine) * CHUNK, CHUNK)


def taps_grad_kernel(kept, signals, lane_ref, back_lane_ref, twist_ref, spec_ref, out):
    first = half_start(kept)
    batch = signals.shape[0] // ROWS
    chans = 2 * (signals.shape[1] // 5)
    rows = {}
    for which in range(2):
        place = pl.ds(pl.multiple_of(which * chans + first, CHUNK), CHUNK)
        for b in range(batch):
            rows[which, b] = spectrum(
                lambda r: signals[b * ROWS + slot(r), place, :].astype(F32), twist_ref, lane_ref
            )
            spec_ref[which * batch + b] = rows[which, b]
    product = conj_product(rows[0, 0], rows[1, 0])
    for b in range(1, batch):
        product = product + conj_product(rows[0, b], rows[1, b])
    for r, row in enumerate(signal_rows(product, twist_ref, back_lane_ref)):
        out[slot(r)] = row.astype(BF16)


def state_kernel(signals, gain_ref, lane_ref, back_lane_ref, twist_ref, *refs):
    *specs, out, skip_ref = refs
    batch = signals.shape[0] // ROWS
    chans = out.shape[1] // 2
    share = signals.shape[1] - 2 * chans
    place = (lax.axis_index("pl") * SIDE + lax.axis_index("x")) * SIDE + lax.axis_index("y")
    pieces = LANES // chans
    gains = jnp.broadcast_to(gain_ref[pl.ds(place // pieces, 1), :], (LANES, LANES))
    skip_ref[...] = gains.T
    begin = pl.multiple_of(place % pieces * chans, chans)
    for kept, spec_ref in enumerate(specs):
        first = half_start(kept)
        source = first // share
        taps = spectrum(
            lambda r: signals[source * ROWS + slot(r), pl.ds(2 * chans, CHUNK), :].astype(F32),
            twist_ref,
            lane_ref,
        )
        skip = skip_ref[pl.ds(pl.multiple_of(begin + first, CHUNK), CHUNK), :]
        for which, product in enumerate((plain_product, conj_product)):
            place = pl.ds(pl.multiple_of(which * chans + first, CHUNK), CHUNK)
            for b in range(batch):
                spec = product(taps, spec_ref[which * batch + b])
                for r, row in enumerate(signal_rows(spec, twist_ref, back_lane_ref)):
                    own = signals[b * ROWS + slot(r), place, :].astype(F32)
                    out[b * ROWS + slot(r), place, :] = (row + skip * own).astype(BF16)


def output_kernel(back, query, key, value, grad, *refs):
    outs, held, sems = refs[:5], refs[5:10], refs[10]
    own = back.shape[1] // 3
    pieces = LANES // own
    width = query.shape[1] // GROUPS
    places = (half_start(1), half_start(0))
    halves = [pl.ds(pl.multiple_of(2 * own + place, CHUNK), CHUNK) for place in places]
    sent = []
    for group in range(GROUPS):
        for tile in range(group * width // LANES, (group + 1) * width // LANES):
            cols = pl.ds(tile * LANES, LANES)
            blocks = [tile * pieces + i for i in range(pieces)]
            state, dmixed = (
                jnp.concatenate([back[i, pl.ds(which * own, own), :] for i in blocks], axis=0).T
                for which in range(2)
            )
            term = jnp.concatenate([back[i, half, :] for i in blocks for half in halves], axis=0).T
            state, dmixed = state.astype(F32), dmixed.astype(F32)
            held[0][:, cols] = (query[:, cols].astype(F32) * state).astype(BF16)
            held[1][:, cols] = (grad[:, cols].astype(F32) * state).astype(BF16)
            held[2][:, cols] = (dmixed * value[:, cols].astype(F32)).astype(BF16)
            held[3][:, cols] = (dmixed * key[:, cols].astype(F32)).astype(BF16)
            held[4][:, cols] = term
        cols = pl.ds(group * width, width)
        pairs = [(a.at[:, cols], b.at[:, cols]) for a, b in zip(held, outs)]
        sent += start_copies(pairs, sems.at[group])
    for copy in sent:
        copy.wait()


def call(kernel, shapes, args, scratch=(), in_hbm=False, out_hbm=False, flops=0, moved=2 << 20, limit=24):
    place = lambda hbm: pl.BlockSpec(memory_space=pltpu.HBM if hbm else pltpu.VMEM)
    return pl.pallas_call(
        kernel,
        out_shape=shapes,
        in_specs=[place(in_hbm)] * len(args),
        out_specs=jax.tree.map(lambda _: place(out_hbm), shapes),
        scratch_shapes=list(scratch),
        compiler_params=pltpu.CompilerParams(vmem_limit_bytes=limit << 20),
        cost_estimate=pl.CostEstimate(flops=flops, bytes_accessed=moved, transcendentals=0),
    )(*[pltpu.with_memory_space_constraint(a, pltpu.HBM) for a in args] if in_hbm else args)


def gate(query, key, value, grad, taps, peers):
    rows_dev, chan_dev = query.shape
    own = chan_dev // peers
    out_shape = (peers, 2 * own + own // 2, rows_dev)
    return call(
        gate_kernel,
        jax.ShapeDtypeStruct(out_shape, BF16),
        (query, key, value, grad, taps),
        [pltpu.VMEM((rows_dev, chan_dev), BF16)] * 5
        + [
            pltpu.SemaphoreType.DMA((GROUPS, 5)),
        ],
        in_hbm=True,
    )


def taps_grad(signals, kept, factor):
    batch = signals.shape[0] // ROWS
    forward_lane, inverse_lane = lane_tables()
    shape = jax.ShapeDtypeStruct
    return call(
        functools.partial(taps_grad_kernel, kept),
        (
            shape((2 * batch, HALF * CHUNK, 2 * LANES), F32),
            shape((ROWS, CHUNK, LANES), BF16),
        ),
        (signals, forward_lane, inverse_lane, twist_tables(factor)),
        flops=2 * 10**9,
    )


def states(signals, spectra, skip_gain, own):
    batch = signals.shape[0] // ROWS
    forward_lane, inverse_lane = lane_tables()
    return call(
        state_kernel,
        jax.ShapeDtypeStruct((batch * ROWS, 2 * own, LANES), BF16),
        (signals, skip_gain.reshape(-1, LANES), forward_lane, inverse_lane, twist_tables(1.0), *spectra),
        (pltpu.VMEM((LANES, LANES), F32),),
        flops=3 * 10**9,
    )


def outputs(back, query, key, value, grad):
    block = jax.ShapeDtypeStruct(query.shape, BF16)
    return call(
        output_kernel,
        (block,) * 5,
        (back, query, key, value, grad),
        [pltpu.VMEM(query.shape, BF16)] * 5 + [pltpu.SemaphoreType.DMA((GROUPS, 5))],
        out_hbm=True,
    )


def on_device(query_in, key_in, value_in, filter_taps, skip_gain, grad_out):
    seq_count, pair = lax.axis_size("y") * lax.axis_size("x"), lax.axis_size("pl")
    peers = seq_count * pair
    rows_dev, chan_dev = query_in.shape[1:]
    own = chan_dev // peers
    batch = query_in.shape[0] * lax.axis_size("dh") * lax.axis_size("dm") * pair
    factor = 1.0 / math.sqrt(batch * seq_count * rows_dev)
    query, key, value, grad = query_in[0], key_in[0], value_in[0], grad_out[0]

    def swap(values, axes):
        return lax.all_to_all(values, axes, split_axis=0, concat_axis=0, tiled=True)

    signals = swap(gate(query, key, value, grad, filter_taps, peers), ("pl", "x", "y"))

    def exchange(values, axis):
        return lax.ppermute(values, axis, [(0, 1), (1, 0)])

    def plus(a, b):
        return (a.astype(F32) + b.astype(F32)).astype(BF16)

    spectra, (given, term) = zip(*(taps_grad(signals, kept, factor) for kept in range(2)))
    term = plus(term, exchange(given, "dm"))
    other = exchange(term, "dh")
    spectra, _ = lax.optimization_barrier((spectra, term))
    results = states(signals, spectra, skip_gain, own)
    other, results = lax.optimization_barrier((other, results))
    term = plus(term, other)
    copies = [
        jnp.broadcast_to(t[None], (pair,) + t.shape).reshape((peers,) + t.shape[1:])
        for t in (term, exchange(term, "dm"))
    ]
    back = swap(jnp.concatenate([results, *copies], axis=1), ("pl", "x", "y"))
    outs = outputs(back, query, key, value, grad)
    return tuple(out[None] for out in outs[:4]) + (outs[4],)


def solution(mesh):
    dp, chan, seq = (mesh.shape[name] for name in ("dp", "chan", "seq"))
    split_mesh = Mesh(
        mesh.devices.reshape(dp // 4, 2, 2, chan, seq // SIDE, SIDE),
        ("dh", "dm", "pl", "chan", "y", "x"),
    )
    rows = P(("dh", "dm", "pl"), ("y", "x"), "chan")
    taps = P(("y", "x"), "chan")
    return jax.shard_map(
        on_device,
        mesh=split_mesh,
        in_specs=(rows, rows, rows, taps, P("chan"), rows),
        out_specs=(rows, rows, rows, rows, taps),
        check_vma=False,
    )
```

```python
import functools
import math

import jax
import jax.numpy as jnp
import numpy as np
from jax import lax
from jax.experimental import pallas as pl
from jax.experimental.pallas import tpu as pltpu
from jax.sharding import Mesh
from jax.sharding import PartitionSpec as P

F32 = jnp.float32
BF16 = jnp.bfloat16
LANES = 128
ROWS = 16
SIDE = 4
FREQS = 2 * ROWS
HALF = ROWS + 1
CHUNK = 16
GROUPS = 2


def unit(numer, denom):
    angle = 2.0 * math.pi * numer / denom
    return (math.cos(angle), math.sin(angle))


def times_unit(value, numer, denom):
    re, im = value
    numer = numer % denom
    if 4 * numer % denom == 0:
        return ((re, im), (-im, re), (-re, -im), (im, -re))[4 * numer // denom]
    if 8 * numer % denom == 0:
        root = math.sqrt(0.5)
        summed, apart = (re + im) * root, (re - im) * root
        return {1: (apart, summed), 3: (-summed, apart), 5: (-apart, -summed), 7: (summed, -apart)}[
            8 * numer // denom
        ]
    cos, sin = unit(numer, denom)
    return (re * cos - im * sin, re * sin + im * cos)


def add(a, b):
    return (a[0] + b[0], a[1] + b[1])


def sub(a, b):
    return (a[0] - b[0], a[1] - b[1])


def conj(a):
    return (a[0], -a[1])


def complex_dft(values, sign):
    count = len(values)
    if count == 1:
        return list(values)
    even = complex_dft(values[0::2], sign)
    odd = complex_dft(values[1::2], sign)
    turned = [times_unit(v, sign * j, count) for j, v in enumerate(odd)]
    return [add(e, t) for e, t in zip(even, turned)] + [sub(e, t) for e, t in zip(even, turned)]


def odd_freqs(first, second, count):
    turned = [
        times_unit((a, -b), -r, count) for r, (a, b) in enumerate(zip(first, second))
    ]
    return {4 * j + 1: v for j, v in enumerate(complex_dft(turned, -1))}


def real_dft(values, count):
    half, quarter = count // 2, count // 4
    if count == 2:
        return [(values[0] + values[1], None), (values[0] - values[1], None)]
    if len(values) == half:
        folded, apart = values, values
    else:
        folded = [values[r] + values[r + half] for r in range(half)]
        apart = [values[r] - values[r + half] for r in range(half)]
    out = [None] * (half + 1)
    out[0::2] = real_dft(folded, half)
    for freq, value in odd_freqs(apart[:quarter], apart[quarter:], count).items():
        if freq <= half:
            out[freq] = value
        else:
            out[count - freq] = conj(value)
    return out


def real_inverse(freqs, count, keep_half):
    half, quarter = count // 2, count // 4
    if count == 2:
        first, last = freqs[0][0], freqs[1][0]
        return [first + last, first - last]
    even = real_inverse(freqs[0::2], half, False)
    picked = [
        freqs[4 * j + 1] if 4 * j + 1 <= half else conj(freqs[count - 4 * j - 1])
        for j in range(quarter)
    ]
    turned = [times_unit(v, r, count) for r, v in enumerate(complex_dft(picked, 1))]
    odd = [re for re, _ in turned] + [-im for _, im in turned]
    low = [e + o for e, o in zip(even, odd)]
    if keep_half:
        return low
    return low + [e - o for e, o in zip(even, odd)]


def split_table(table):
    high = table.astype(np.float32).astype(BF16)
    low = (table - high.astype(np.float64)).astype(BF16)
    return np.stack([high, low])


def lane_tables():
    idx = np.arange(LANES)
    angle = 2.0 * np.pi / LANES * (idx[:, None] * idx[None, :] % LANES)
    cos, sin = np.cos(angle), np.sin(angle)
    forward = np.block([[cos, -sin], [sin, cos]])
    inverse = np.block([[cos, sin], [-sin, cos]])
    return split_table(forward), split_table(inverse)


def twist_tables(factor):
    padded = FREQS * LANES
    angle = 2.0 * np.pi / padded * (np.arange(HALF)[:, None] * np.arange(LANES)[None, :])
    weight = np.full((HALF, 1), 2.0)
    weight[0] = weight[-1] = 1.0
    weight = weight / padded * factor
    cos, sin = np.cos(angle), np.sin(angle)
    return np.stack([cos, sin, cos * weight, sin * weight], axis=1).astype(np.float32)


def split_value(value):
    high = value.astype(BF16)
    return high, (value - high.astype(F32)).astype(BF16)


def start_copies(pairs, sems):
    copies = [pltpu.make_async_copy(a, b, sems.at[i]) for i, (a, b) in enumerate(pairs)]
    for copy in copies:
        copy.start()
    return copies


def gate_kernel(query, key, value, grad, taps, out, *scratch):
    held, sems = scratch[:5], scratch[5]
    key_v, value_v, grad_v, query_v, taps_v = held
    peers = out.shape[0]
    own = taps.shape[1] // peers
    share = out.shape[1] - 2 * own
    pieces = LANES // own
    width = taps.shape[1] // GROUPS
    begin = lax.axis_index("pl") * share
    arrivals = []
    for group in range(GROUPS):
        cols = pl.ds(group * width, width)
        pairs = [(a.at[:, cols], b.at[:, cols]) for a, b in zip((key, value, grad, query, taps), held)]
        arrivals.append(start_copies(pairs, sems.at[group]))
    for group, copies in enumerate(arrivals):
        for copy in copies:
            copy.wait()
        tiles = width // LANES
        for tile in range(group * tiles, (group + 1) * tiles):
            cols = pl.ds(tile * LANES, LANES)
            mixed = (key_v[:, cols].astype(F32) * value_v[:, cols].astype(F32)).astype(BF16)
            state = (grad_v[:, cols].astype(F32) * query_v[:, cols].astype(F32)).astype(BF16)
            for place, block in enumerate((mixed, state)):
                turned = block.T
                for i in range(pieces):
                    rows = pl.ds(place * own, own)
                    out[tile * pieces + i, rows, :] = turned[i * own : (i + 1) * own]
            turned = taps_v[:, cols].T
            for i in range(pieces):
                low = turned[i * own : i * own + share]
                high = turned[i * own + share : (i + 1) * own]
                rows = pl.ds(2 * own, share)
                out[tile * pieces + i, rows, :] = jnp.where(begin == 0, low, high)


def spectrum(get_row, twist_ref, lane_ref):
    freqs = real_dft([get_row(r) for r in range(ROWS)], FREQS)
    rows = []
    for k, (re, im) in enumerate(freqs):
        cos, sin = twist_ref[k, 0:1, :], twist_ref[k, 1:2, :]
        if im is None:
            rows.append(jnp.concatenate([re * cos, -re * sin], axis=1))
        else:
            rows.append(jnp.concatenate([re * cos + im * sin, im * cos - re * sin], axis=1))
    return lane_product(jnp.concatenate(rows, axis=0), lane_ref)


def lane_product(value, table_ref):
    high, low = split_value(value)
    out = jnp.dot(high, table_ref[0], preferred_element_type=F32)
    out += jnp.dot(low, table_ref[0], preferred_element_type=F32)
    return out + jnp.dot(high, table_ref[1], preferred_element_type=F32)


def conj_product(first, second):
    are, aim = first[:, :LANES], first[:, LANES:]
    bre, bim = second[:, :LANES], second[:, LANES:]
    return jnp.concatenate([are * bre + aim * bim, are * bim - aim * bre], axis=1)


def plain_product(first, second):
    are, aim = first[:, :LANES], first[:, LANES:]
    bre, bim = second[:, :LANES], second[:, LANES:]
    return jnp.concatenate([are * bre - aim * bim, are * bim + aim * bre], axis=1)


def signal_rows(spec, twist_ref, back_lane_ref):
    back = lane_product(spec, back_lane_ref)
    freqs = []
    for k in range(HALF):
        re = back[k * CHUNK : (k + 1) * CHUNK, :LANES]
        im = back[k * CHUNK : (k + 1) * CHUNK, LANES:]
        cos, sin = twist_ref[k, 2:3, :], twist_ref[k, 3:4, :]
        if k in (0, ROWS):
            freqs.append((re * cos - im * sin, None))
        else:
            freqs.append((re * cos - im * sin, im * cos + re * sin))
    return real_inverse(freqs, FREQS, True)


def slot(row):
    return row % SIDE * SIDE + row // SIDE


def half_start(kept):
    mine = lax.axis_index("dm")
    return pl.multiple_of((mine if kept else 1 - mine) * CHUNK, CHUNK)


def taps_grad_kernel(kept, signals, lane_ref, back_lane_ref, twist_ref, spec_ref, out):
    first = half_start(kept)
    batch = signals.shape[0] // ROWS
    chans = 2 * (signals.shape[1] // 5)
    rows = {}
    for which in range(2):
        place = pl.ds(pl.multiple_of(which * chans + first, CHUNK), CHUNK)
        for b in range(batch):
            rows[which, b] = spectrum(
                lambda r: signals[b * ROWS + slot(r), place, :].astype(F32), twist_ref, lane_ref
            )
            spec_ref[which * batch + b] = rows[which, b]
    product = conj_product(rows[0, 0], rows[1, 0])
    for b in range(1, batch):
        product = product + conj_product(rows[0, b], rows[1, b])
    for r, row in enumerate(signal_rows(product, twist_ref, back_lane_ref)):
        out[slot(r)] = row.astype(BF16)


def state_kernel(signals, gain_ref, lane_ref, back_lane_ref, twist_ref, *refs):
    *specs, out, skip_ref = refs
    batch = signals.shape[0] // ROWS
    chans = out.shape[1] // 2
    share = signals.shape[1] - 2 * chans
    place = (lax.axis_index("pl") * SIDE + lax.axis_index("x")) * SIDE + lax.axis_index("y")
    pieces = LANES // chans
    gains = jnp.broadcast_to(gain_ref[pl.ds(place // pieces, 1), :], (LANES, LANES))
    skip_ref[...] = gains.T
    begin = pl.multiple_of(place % pieces * chans, chans)
    for kept, spec_ref in enumerate(specs):
        first = half_start(kept)
        source = first // share
        taps = spectrum(
            lambda r: signals[source * ROWS + slot(r), pl.ds(2 * chans, CHUNK), :].astype(F32),
            twist_ref,
            lane_ref,
        )
        skip = skip_ref[pl.ds(pl.multiple_of(begin + first, CHUNK), CHUNK), :]
        for which, product in enumerate((plain_product, conj_product)):
            place = pl.ds(pl.multiple_of(which * chans + first, CHUNK), CHUNK)
            for b in range(batch):
                spec = product(taps, spec_ref[which * batch + b])
                for r, row in enumerate(signal_rows(spec, twist_ref, back_lane_ref)):
                    own = signals[b * ROWS + slot(r), place, :].astype(F32)
                    out[b * ROWS + slot(r), place, :] = (row + skip * own).astype(BF16)


def output_kernel(back, query, key, value, grad, *refs):
    outs, held, sems = refs[:5], refs[5:10], refs[10]
    own = back.shape[1] // 3
    pieces = LANES // own
    width = query.shape[1] // GROUPS
    sent = []
    for group in range(GROUPS):
        for tile in range(group * width // LANES, (group + 1) * width // LANES):
            cols = pl.ds(tile * LANES, LANES)
            blocks = [tile * pieces + i for i in range(pieces)]
            state, dmixed, term = (
                jnp.concatenate([back[i, pl.ds(which * own, own), :] for i in blocks], axis=0).T
                for which in range(3)
            )
            state, dmixed = state.astype(F32), dmixed.astype(F32)
            held[0][:, cols] = (query[:, cols].astype(F32) * state).astype(BF16)
            held[1][:, cols] = (grad[:, cols].astype(F32) * state).astype(BF16)
            held[2][:, cols] = (dmixed * value[:, cols].astype(F32)).astype(BF16)
            held[3][:, cols] = (dmixed * key[:, cols].astype(F32)).astype(BF16)
            held[4][:, cols] = term
        cols = pl.ds(group * width, width)
        pairs = [(a.at[:, cols], b.at[:, cols]) for a, b in zip(held, outs)]
        sent += start_copies(pairs, sems.at[group])
    for copy in sent:
        copy.wait()


def call(kernel, shapes, args, scratch=(), in_hbm=False, out_hbm=False, flops=0, moved=2 << 20, limit=24):
    place = lambda hbm: pl.BlockSpec(memory_space=pltpu.HBM if hbm else pltpu.VMEM)
    return pl.pallas_call(
        kernel,
        out_shape=shapes,
        in_specs=[place(in_hbm)] * len(args),
        out_specs=jax.tree.map(lambda _: place(out_hbm), shapes),
        scratch_shapes=list(scratch),
        compiler_params=pltpu.CompilerParams(vmem_limit_bytes=limit << 20),
        cost_estimate=pl.CostEstimate(flops=flops, bytes_accessed=moved, transcendentals=0),
    )(*[pltpu.with_memory_space_constraint(a, pltpu.HBM) for a in args] if in_hbm else args)


def gate(query, key, value, grad, taps, peers):
    rows_dev, chan_dev = query.shape
    own = chan_dev // peers
    out_shape = (peers, 2 * own + own // 2, rows_dev)
    return call(
        gate_kernel,
        jax.ShapeDtypeStruct(out_shape, BF16),
        (query, key, value, grad, taps),
        [pltpu.VMEM((rows_dev, chan_dev), BF16)] * 5
        + [
            pltpu.SemaphoreType.DMA((GROUPS, 5)),
        ],
        in_hbm=True,
    )


def taps_grad(signals, kept, factor):
    batch = signals.shape[0] // ROWS
    forward_lane, inverse_lane = lane_tables()
    shape = jax.ShapeDtypeStruct
    return call(
        functools.partial(taps_grad_kernel, kept),
        (
            shape((2 * batch, HALF * CHUNK, 2 * LANES), F32),
            shape((ROWS, CHUNK, LANES), BF16),
        ),
        (signals, forward_lane, inverse_lane, twist_tables(factor)),
        flops=2 * 10**9,
    )


def states(signals, spectra, skip_gain, own):
    batch = signals.shape[0] // ROWS
    forward_lane, inverse_lane = lane_tables()
    return call(
        state_kernel,
        jax.ShapeDtypeStruct((batch * ROWS, 2 * own, LANES), BF16),
        (signals, skip_gain.reshape(-1, LANES), forward_lane, inverse_lane, twist_tables(1.0), *spectra),
        (pltpu.VMEM((LANES, LANES), F32),),
        flops=3 * 10**9,
    )


def outputs(back, query, key, value, grad):
    block = jax.ShapeDtypeStruct(query.shape, BF16)
    return call(
        output_kernel,
        (block,) * 5,
        (back, query, key, value, grad),
        [pltpu.VMEM(query.shape, BF16)] * 5 + [pltpu.SemaphoreType.DMA((GROUPS, 5))],
        out_hbm=True,
    )


def on_device(query_in, key_in, value_in, filter_taps, skip_gain, grad_out):
    seq_count, pair = lax.axis_size("y") * lax.axis_size("x"), lax.axis_size("pl")
    peers = seq_count * pair
    rows_dev, chan_dev = query_in.shape[1:]
    own = chan_dev // peers
    batch = query_in.shape[0] * lax.axis_size("dh") * lax.axis_size("dm") * pair
    factor = 1.0 / math.sqrt(batch * seq_count * rows_dev)
    query, key, value, grad = query_in[0], key_in[0], value_in[0], grad_out[0]

    def swap(values, axes):
        return lax.all_to_all(values, axes, split_axis=0, concat_axis=0, tiled=True)

    signals = swap(gate(query, key, value, grad, filter_taps, peers), ("pl", "x", "y"))

    def exchange(values, axis):
        return lax.ppermute(values, axis, [(0, 1), (1, 0)])

    def plus(a, b):
        return (a.astype(F32) + b.astype(F32)).astype(BF16)

    spectra, (given, term) = zip(*(taps_grad(signals, kept, factor) for kept in range(2)))
    term = plus(term, exchange(given, "dm"))
    other = exchange(term, "dh")
    spectra, _ = lax.optimization_barrier((spectra, term))
    results = states(signals, spectra, skip_gain, own)
    other, results = lax.optimization_barrier((other, results))
    term = plus(term, other)
    halves = lax.all_gather(term, "dm")
    copies = [jnp.broadcast_to(t[None], (pair,) + t.shape).reshape((peers,) + t.shape[1:]) for t in halves]
    back = swap(jnp.concatenate([results, *copies], axis=1), ("pl", "x", "y"))
    outs = outputs(back, query, key, value, grad)
    return tuple(out[None] for out in outs[:4]) + (outs[4],)


def solution(mesh):
    dp, chan, seq = (mesh.shape[name] for name in ("dp", "chan", "seq"))
    split_mesh = Mesh(
        mesh.devices.reshape(dp // 4, 2, 2, chan, seq // SIDE, SIDE),
        ("dh", "dm", "pl", "chan", "y", "x"),
    )
    rows = P(("dh", "dm", "pl"), ("y", "x"), "chan")
    taps = P(("y", "x"), "chan")
    return jax.shard_map(
        on_device,
        mesh=split_mesh,
        in_specs=(rows, rows, rows, taps, P("chan"), rows),
        out_specs=(rows, rows, rows, rows, taps),
        check_vma=False,
    )
```

```python
import functools
import math

import jax
import jax.numpy as jnp
import numpy as np
from jax import lax
from jax.experimental import pallas as pl
from jax.experimental.pallas import tpu as pltpu
from jax.sharding import Mesh
from jax.sharding import PartitionSpec as P

F32 = jnp.float32
BF16 = jnp.bfloat16
LANES = 128
ROWS = 16
SIDE = 4
FREQS = 2 * ROWS
HALF = ROWS + 1
CHUNK = 16
GROUPS = 2


def unit(numer, denom):
    angle = 2.0 * math.pi * numer / denom
    return (math.cos(angle), math.sin(angle))


def times_unit(value, numer, denom):
    re, im = value
    numer = numer % denom
    if 4 * numer % denom == 0:
        return ((re, im), (-im, re), (-re, -im), (im, -re))[4 * numer // denom]
    if 8 * numer % denom == 0:
        root = math.sqrt(0.5)
        summed, apart = (re + im) * root, (re - im) * root
        return {1: (apart, summed), 3: (-summed, apart), 5: (-apart, -summed), 7: (summed, -apart)}[
            8 * numer // denom
        ]
    cos, sin = unit(numer, denom)
    return (re * cos - im * sin, re * sin + im * cos)


def add(a, b):
    return (a[0] + b[0], a[1] + b[1])


def sub(a, b):
    return (a[0] - b[0], a[1] - b[1])


def conj(a):
    return (a[0], -a[1])


def complex_dft(values, sign):
    count = len(values)
    if count == 1:
        return list(values)
    even = complex_dft(values[0::2], sign)
    odd = complex_dft(values[1::2], sign)
    turned = [times_unit(v, sign * j, count) for j, v in enumerate(odd)]
    return [add(e, t) for e, t in zip(even, turned)] + [sub(e, t) for e, t in zip(even, turned)]


def odd_freqs(first, second, count):
    turned = [
        times_unit((a, -b), -r, count) for r, (a, b) in enumerate(zip(first, second))
    ]
    return {4 * j + 1: v for j, v in enumerate(complex_dft(turned, -1))}


def real_dft(values, count):
    half, quarter = count // 2, count // 4
    if count == 2:
        return [(values[0] + values[1], None), (values[0] - values[1], None)]
    if len(values) == half:
        folded, apart = values, values
    else:
        folded = [values[r] + values[r + half] for r in range(half)]
        apart = [values[r] - values[r + half] for r in range(half)]
    out = [None] * (half + 1)
    out[0::2] = real_dft(folded, half)
    for freq, value in odd_freqs(apart[:quarter], apart[quarter:], count).items():
        if freq <= half:
            out[freq] = value
        else:
            out[count - freq] = conj(value)
    return out


def real_inverse(freqs, count, keep_half):
    half, quarter = count // 2, count // 4
    if count == 2:
        first, last = freqs[0][0], freqs[1][0]
        return [first + last, first - last]
    even = real_inverse(freqs[0::2], half, False)
    picked = [
        freqs[4 * j + 1] if 4 * j + 1 <= half else conj(freqs[count - 4 * j - 1])
        for j in range(quarter)
    ]
    turned = [times_unit(v, r, count) for r, v in enumerate(complex_dft(picked, 1))]
    odd = [re for re, _ in turned] + [-im for _, im in turned]
    low = [e + o for e, o in zip(even, odd)]
    if keep_half:
        return low
    return low + [e - o for e, o in zip(even, odd)]


def split_table(table):
    high = table.astype(np.float32).astype(BF16)
    low = (table - high.astype(np.float64)).astype(BF16)
    return np.stack([high, low])


def lane_tables():
    idx = np.arange(LANES)
    angle = 2.0 * np.pi / LANES * (idx[:, None] * idx[None, :] % LANES)
    cos, sin = np.cos(angle), np.sin(angle)
    forward = np.block([[cos, -sin], [sin, cos]])
    inverse = np.block([[cos, sin], [-sin, cos]])
    return split_table(forward), split_table(inverse)


def twist_tables(factor):
    padded = FREQS * LANES
    angle = 2.0 * np.pi / padded * (np.arange(HALF)[:, None] * np.arange(LANES)[None, :])
    weight = np.full((HALF, 1), 2.0)
    weight[0] = weight[-1] = 1.0
    weight = weight / padded * factor
    cos, sin = np.cos(angle), np.sin(angle)
    return np.stack([cos, sin, cos * weight, sin * weight], axis=1).astype(np.float32)


def split_value(value):
    high = value.astype(BF16)
    return high, (value - high.astype(F32)).astype(BF16)


def start_copies(pairs, sems):
    copies = [pltpu.make_async_copy(a, b, sems.at[i]) for i, (a, b) in enumerate(pairs)]
    for copy in copies:
        copy.start()
    return copies


def gate_kernel(query, key, value, grad, taps, out, *scratch):
    held, sems = scratch[:5], scratch[5]
    key_v, value_v, grad_v, query_v, taps_v = held
    peers = out.shape[0]
    own = taps.shape[1] // peers
    share = out.shape[1] - 2 * own
    pieces = LANES // own
    width = taps.shape[1] // GROUPS
    begin = lax.axis_index("pl") * share
    arrivals = []
    for group in range(GROUPS):
        cols = pl.ds(group * width, width)
        pairs = [(a.at[:, cols], b.at[:, cols]) for a, b in zip((key, value, grad, query, taps), held)]
        arrivals.append(start_copies(pairs, sems.at[group]))
    for group, copies in enumerate(arrivals):
        for copy in copies:
            copy.wait()
        tiles = width // LANES
        for tile in range(group * tiles, (group + 1) * tiles):
            cols = pl.ds(tile * LANES, LANES)
            mixed = (key_v[:, cols].astype(F32) * value_v[:, cols].astype(F32)).astype(BF16)
            state = (grad_v[:, cols].astype(F32) * query_v[:, cols].astype(F32)).astype(BF16)
            for place, block in enumerate((mixed, state)):
                turned = block.T
                for i in range(pieces):
                    rows = pl.ds(place * own, own)
                    out[tile * pieces + i, rows, :] = turned[i * own : (i + 1) * own]
            turned = taps_v[:, cols].T
            for i in range(pieces):
                low = turned[i * own : i * own + share]
                high = turned[i * own + share : (i + 1) * own]
                rows = pl.ds(2 * own, share)
                out[tile * pieces + i, rows, :] = jnp.where(begin == 0, low, high)


def spectrum(get_row, twist_ref, lane_ref):
    freqs = real_dft([get_row(r) for r in range(ROWS)], FREQS)
    rows = []
    for k, (re, im) in enumerate(freqs):
        cos, sin = twist_ref[k, 0:1, :], twist_ref[k, 1:2, :]
        if im is None:
            rows.append(jnp.concatenate([re * cos, -re * sin], axis=1))
        else:
            rows.append(jnp.concatenate([re * cos + im * sin, im * cos - re * sin], axis=1))
    return lane_product(jnp.concatenate(rows, axis=0), lane_ref)


def lane_product(value, table_ref):
    high, low = split_value(value)
    out = jnp.dot(high, table_ref[0], preferred_element_type=F32)
    out += jnp.dot(low, table_ref[0], preferred_element_type=F32)
    return out + jnp.dot(high, table_ref[1], preferred_element_type=F32)


def conj_product(first, second):
    are, aim = first[:, :LANES], first[:, LANES:]
    bre, bim = second[:, :LANES], second[:, LANES:]
    return jnp.concatenate([are * bre + aim * bim, are * bim - aim * bre], axis=1)


def plain_product(first, second):
    are, aim = first[:, :LANES], first[:, LANES:]
    bre, bim = second[:, :LANES], second[:, LANES:]
    return jnp.concatenate([are * bre - aim * bim, are * bim + aim * bre], axis=1)


def signal_rows(spec, twist_ref, back_lane_ref):
    back = lane_product(spec, back_lane_ref)
    freqs = []
    for k in range(HALF):
        re = back[k * CHUNK : (k + 1) * CHUNK, :LANES]
        im = back[k * CHUNK : (k + 1) * CHUNK, LANES:]
        cos, sin = twist_ref[k, 2:3, :], twist_ref[k, 3:4, :]
        if k in (0, ROWS):
            freqs.append((re * cos - im * sin, None))
        else:
            freqs.append((re * cos - im * sin, im * cos + re * sin))
    return real_inverse(freqs, FREQS, True)


def slot(row):
    return row % SIDE * SIDE + row // SIDE


def half_start(kept):
    mine = lax.axis_index("dm")
    return pl.multiple_of((mine if kept else 1 - mine) * CHUNK, CHUNK)


def taps_grad_kernel(kept, signals, lane_ref, back_lane_ref, twist_ref, spec_ref, out):
    first = half_start(kept)
    batch = signals.shape[0] // ROWS
    chans = 2 * (signals.shape[1] // 5)
    rows = {}
    for which in range(2):
        place = pl.ds(pl.multiple_of(which * chans + first, CHUNK), CHUNK)
        for b in range(batch):
            rows[which, b] = spectrum(
                lambda r: signals[b * ROWS + slot(r), place, :].astype(F32), twist_ref, lane_ref
            )
            spec_ref[which * batch + b] = rows[which, b]
    product = conj_product(rows[0, 0], rows[1, 0])
    for b in range(1, batch):
        product = product + conj_product(rows[0, b], rows[1, b])
    for r, row in enumerate(signal_rows(product, twist_ref, back_lane_ref)):
        out[slot(r)] = row.astype(BF16)


def state_kernel(signals, gain_ref, lane_ref, back_lane_ref, twist_ref, *refs):
    *specs, out, skip_ref = refs
    batch = signals.shape[0] // ROWS
    chans = out.shape[1] // 2
    share = signals.shape[1] - 2 * chans
    place = (lax.axis_index("pl") * SIDE + lax.axis_index("x")) * SIDE + lax.axis_index("y")
    pieces = LANES // chans
    gains = jnp.broadcast_to(gain_ref[pl.ds(place // pieces, 1), :], (LANES, LANES))
    skip_ref[...] = gains.T
    begin = pl.multiple_of(place % pieces * chans, chans)
    for kept, spec_ref in enumerate(specs):
        first = half_start(kept)
        source = first // share
        taps = spectrum(
            lambda r: signals[source * ROWS + slot(r), pl.ds(2 * chans, CHUNK), :].astype(F32),
            twist_ref,
            lane_ref,
        )
        skip = skip_ref[pl.ds(pl.multiple_of(begin + first, CHUNK), CHUNK), :]
        for which, product in enumerate((plain_product, conj_product)):
            place = pl.ds(pl.multiple_of(which * chans + first, CHUNK), CHUNK)
            for b in range(batch):
                spec = product(taps, spec_ref[which * batch + b])
                for r, row in enumerate(signal_rows(spec, twist_ref, back_lane_ref)):
                    own = signals[b * ROWS + slot(r), place, :].astype(F32)
                    out[b * ROWS + slot(r), place, :] = (row + skip * own).astype(BF16)


def output_kernel(back, query, key, value, grad, *refs):
    outs, held, sems = refs[:5], refs[5:10], refs[10]
    own = back.shape[1] // 3
    pieces = LANES // own
    width = query.shape[1] // GROUPS
    sent = []
    for group in range(GROUPS):
        for tile in range(group * width // LANES, (group + 1) * width // LANES):
            cols = pl.ds(tile * LANES, LANES)
            blocks = [tile * pieces + i for i in range(pieces)]
            state, dmixed, term = (
                jnp.concatenate([back[i, pl.ds(which * own, own), :] for i in blocks], axis=0).T
                for which in range(3)
            )
            state, dmixed = state.astype(F32), dmixed.astype(F32)
            held[0][:, cols] = (query[:, cols].astype(F32) * state).astype(BF16)
            held[1][:, cols] = (grad[:, cols].astype(F32) * state).astype(BF16)
            held[2][:, cols] = (dmixed * value[:, cols].astype(F32)).astype(BF16)
            held[3][:, cols] = (dmixed * key[:, cols].astype(F32)).astype(BF16)
            held[4][:, cols] = term
        cols = pl.ds(group * width, width)
        pairs = [(a.at[:, cols], b.at[:, cols]) for a, b in zip(held, outs)]
        sent += start_copies(pairs, sems.at[group])
    for copy in sent:
        copy.wait()


def call(kernel, shapes, args, scratch=(), in_hbm=False, out_hbm=False, flops=0, moved=2 << 20, limit=24):
    place = lambda hbm: pl.BlockSpec(memory_space=pltpu.HBM if hbm else pltpu.VMEM)
    return pl.pallas_call(
        kernel,
        out_shape=shapes,
        in_specs=[place(in_hbm)] * len(args),
        out_specs=jax.tree.map(lambda _: place(out_hbm), shapes),
        scratch_shapes=list(scratch),
        compiler_params=pltpu.CompilerParams(vmem_limit_bytes=limit << 20),
        cost_estimate=pl.CostEstimate(flops=flops, bytes_accessed=moved, transcendentals=0),
    )(*[pltpu.with_memory_space_constraint(a, pltpu.HBM) for a in args] if in_hbm else args)


def gate(query, key, value, grad, taps, peers):
    rows_dev, chan_dev = query.shape
    own = chan_dev // peers
    out_shape = (peers, 2 * own + own // 2, rows_dev)
    return call(
        gate_kernel,
        jax.ShapeDtypeStruct(out_shape, BF16),
        (query, key, value, grad, taps),
        [pltpu.VMEM((rows_dev, chan_dev), BF16)] * 5
        + [
            pltpu.SemaphoreType.DMA((GROUPS, 5)),
        ],
        in_hbm=True,
    )


def taps_grad(signals, kept, factor):
    batch = signals.shape[0] // ROWS
    forward_lane, inverse_lane = lane_tables()
    shape = jax.ShapeDtypeStruct
    return call(
        functools.partial(taps_grad_kernel, kept),
        (
            shape((2 * batch, HALF * CHUNK, 2 * LANES), F32),
            shape((ROWS, CHUNK, LANES), BF16),
        ),
        (signals, forward_lane, inverse_lane, twist_tables(factor)),
        flops=2 * 10**9,
    )


def states(signals, spectra, skip_gain, own):
    batch = signals.shape[0] // ROWS
    forward_lane, inverse_lane = lane_tables()
    return call(
        state_kernel,
        jax.ShapeDtypeStruct((batch * ROWS, 2 * own, LANES), BF16),
        (signals, skip_gain.reshape(-1, LANES), forward_lane, inverse_lane, twist_tables(1.0), *spectra),
        (pltpu.VMEM((LANES, LANES), F32),),
        flops=3 * 10**9,
    )


def outputs(back, query, key, value, grad):
    block = jax.ShapeDtypeStruct(query.shape, BF16)
    return call(
        output_kernel,
        (block,) * 5,
        (back, query, key, value, grad),
        [pltpu.VMEM(query.shape, BF16)] * 5 + [pltpu.SemaphoreType.DMA((GROUPS, 5))],
        out_hbm=True,
    )


def on_device(query_in, key_in, value_in, filter_taps, skip_gain, grad_out):
    seq_count, pair = lax.axis_size("y") * lax.axis_size("x"), lax.axis_size("pl")
    peers = seq_count * pair
    rows_dev, chan_dev = query_in.shape[1:]
    own = chan_dev // peers
    batch = query_in.shape[0] * lax.axis_size("dh") * lax.axis_size("dm") * pair
    factor = 1.0 / math.sqrt(batch * seq_count * rows_dev)
    query, key, value, grad = query_in[0], key_in[0], value_in[0], grad_out[0]

    def swap(values, axes):
        return lax.all_to_all(values, axes, split_axis=0, concat_axis=0, tiled=True)

    signals = swap(gate(query, key, value, grad, filter_taps, peers), ("pl", "x", "y"))

    def plus(a, b):
        return (a.astype(F32) + b.astype(F32)).astype(BF16)

    spectra, (given, term) = zip(*(taps_grad(signals, kept, factor) for kept in range(2)))
    taken = lax.ppermute(given, "dm", [(0, 1), (1, 0)])
    results = states(signals, spectra, skip_gain, own)
    taken, results = lax.optimization_barrier((taken, results))
    term = plus(*lax.all_gather(plus(term, taken), "dh"))
    halves = lax.all_gather(term, "dm")
    copies = [jnp.broadcast_to(t[None], (pair,) + t.shape).reshape((peers,) + t.shape[1:]) for t in halves]
    back = swap(jnp.concatenate([results, *copies], axis=1), ("pl", "x", "y"))
    outs = outputs(back, query, key, value, grad)
    return tuple(out[None] for out in outs[:4]) + (outs[4],)


def solution(mesh):
    dp, chan, seq = (mesh.shape[name] for name in ("dp", "chan", "seq"))
    split_mesh = Mesh(
        mesh.devices.reshape(dp // 4, 2, 2, chan, seq // SIDE, SIDE),
        ("dh", "dm", "pl", "chan", "y", "x"),
    )
    rows = P(("dh", "dm", "pl"), ("y", "x"), "chan")
    taps = P(("y", "x"), "chan")
    return jax.shard_map(
        on_device,
        mesh=split_mesh,
        in_specs=(rows, rows, rows, taps, P("chan"), rows),
        out_specs=(rows, rows, rows, rows, taps),
        check_vma=False,
    )
```

```python
import functools
import math

import jax
import jax.numpy as jnp
import numpy as np
from jax import lax
from jax.experimental import pallas as pl
from jax.experimental.pallas import tpu as pltpu
from jax.sharding import Mesh
from jax.sharding import PartitionSpec as P

F32 = jnp.float32
BF16 = jnp.bfloat16
LANES = 128
ROWS = 16
SIDE = 4
FREQS = 2 * ROWS
HALF = ROWS + 1
CHUNK = 16
GROUPS = 2


def unit(numer, denom):
    angle = 2.0 * math.pi * numer / denom
    return (math.cos(angle), math.sin(angle))


def times_unit(value, numer, denom):
    re, im = value
    numer = numer % denom
    if 4 * numer % denom == 0:
        return ((re, im), (-im, re), (-re, -im), (im, -re))[4 * numer // denom]
    if 8 * numer % denom == 0:
        root = math.sqrt(0.5)
        summed, apart = (re + im) * root, (re - im) * root
        return {1: (apart, summed), 3: (-summed, apart), 5: (-apart, -summed), 7: (summed, -apart)}[
            8 * numer // denom
        ]
    cos, sin = unit(numer, denom)
    return (re * cos - im * sin, re * sin + im * cos)


def add(a, b):
    return (a[0] + b[0], a[1] + b[1])


def sub(a, b):
    return (a[0] - b[0], a[1] - b[1])


def conj(a):
    return (a[0], -a[1])


def complex_dft(values, sign):
    count = len(values)
    if count == 1:
        return list(values)
    even = complex_dft(values[0::2], sign)
    odd = complex_dft(values[1::2], sign)
    turned = [times_unit(v, sign * j, count) for j, v in enumerate(odd)]
    return [add(e, t) for e, t in zip(even, turned)] + [sub(e, t) for e, t in zip(even, turned)]


def odd_freqs(first, second, count):
    turned = [
        times_unit((a, -b), -r, count) for r, (a, b) in enumerate(zip(first, second))
    ]
    return {4 * j + 1: v for j, v in enumerate(complex_dft(turned, -1))}


def real_dft(values, count):
    half, quarter = count // 2, count // 4
    if count == 2:
        return [(values[0] + values[1], None), (values[0] - values[1], None)]
    if len(values) == half:
        folded, apart = values, values
    else:
        folded = [values[r] + values[r + half] for r in range(half)]
        apart = [values[r] - values[r + half] for r in range(half)]
    out = [None] * (half + 1)
    out[0::2] = real_dft(folded, half)
    for freq, value in odd_freqs(apart[:quarter], apart[quarter:], count).items():
        if freq <= half:
            out[freq] = value
        else:
            out[count - freq] = conj(value)
    return out


def real_inverse(freqs, count, keep_half):
    half, quarter = count // 2, count // 4
    if count == 2:
        first, last = freqs[0][0], freqs[1][0]
        return [first + last, first - last]
    even = real_inverse(freqs[0::2], half, False)
    picked = [
        freqs[4 * j + 1] if 4 * j + 1 <= half else conj(freqs[count - 4 * j - 1])
        for j in range(quarter)
    ]
    turned = [times_unit(v, r, count) for r, v in enumerate(complex_dft(picked, 1))]
    odd = [re for re, _ in turned] + [-im for _, im in turned]
    low = [e + o for e, o in zip(even, odd)]
    if keep_half:
        return low
    return low + [e - o for e, o in zip(even, odd)]


def split_table(table):
    high = table.astype(np.float32).astype(BF16)
    low = (table - high.astype(np.float64)).astype(BF16)
    return np.stack([high, low])


def lane_tables():
    idx = np.arange(LANES)
    angle = 2.0 * np.pi / LANES * (idx[:, None] * idx[None, :] % LANES)
    cos, sin = np.cos(angle), np.sin(angle)
    forward = np.block([[cos, -sin], [sin, cos]])
    inverse = np.block([[cos, sin], [-sin, cos]])
    return split_table(forward), split_table(inverse)


def twist_tables(factor):
    padded = FREQS * LANES
    angle = 2.0 * np.pi / padded * (np.arange(HALF)[:, None] * np.arange(LANES)[None, :])
    weight = np.full((HALF, 1), 2.0)
    weight[0] = weight[-1] = 1.0
    weight = weight / padded * factor
    cos, sin = np.cos(angle), np.sin(angle)
    return np.stack([cos, sin, cos * weight, sin * weight], axis=1).astype(np.float32)


def split_value(value):
    high = value.astype(BF16)
    return high, (value - high.astype(F32)).astype(BF16)


def start_copies(pairs, sems):
    copies = [pltpu.make_async_copy(a, b, sems.at[i]) for i, (a, b) in enumerate(pairs)]
    for copy in copies:
        copy.start()
    return copies


def gate_kernel(query, key, value, grad, taps, out, *scratch):
    held, sems = scratch[:5], scratch[5]
    key_v, value_v, grad_v, query_v, taps_v = held
    peers = out.shape[0]
    own = taps.shape[1] // peers
    share = out.shape[1] - 2 * own
    pieces = LANES // own
    width = taps.shape[1] // GROUPS
    begin = lax.axis_index("pl") * share
    arrivals = []
    for group in range(GROUPS):
        cols = pl.ds(group * width, width)
        pairs = [(a.at[:, cols], b.at[:, cols]) for a, b in zip((key, value, grad, query, taps), held)]
        arrivals.append(start_copies(pairs, sems.at[group]))
    for group, copies in enumerate(arrivals):
        for copy in copies:
            copy.wait()
        tiles = width // LANES
        for tile in range(group * tiles, (group + 1) * tiles):
            cols = pl.ds(tile * LANES, LANES)
            mixed = (key_v[:, cols].astype(F32) * value_v[:, cols].astype(F32)).astype(BF16)
            state = (grad_v[:, cols].astype(F32) * query_v[:, cols].astype(F32)).astype(BF16)
            for place, block in enumerate((mixed, state)):
                turned = block.T
                for i in range(pieces):
                    rows = pl.ds(place * own, own)
                    out[tile * pieces + i, rows, :] = turned[i * own : (i + 1) * own]
            turned = taps_v[:, cols].T
            for i in range(pieces):
                low = turned[i * own : i * own + share]
                high = turned[i * own + share : (i + 1) * own]
                rows = pl.ds(2 * own, share)
                out[tile * pieces + i, rows, :] = jnp.where(begin == 0, low, high)


def spectrum(get_row, twist_ref, lane_ref):
    freqs = real_dft([get_row(r) for r in range(ROWS)], FREQS)
    rows = []
    for k, (re, im) in enumerate(freqs):
        cos, sin = twist_ref[k, 0:1, :], twist_ref[k, 1:2, :]
        if im is None:
            rows.append(jnp.concatenate([re * cos, -re * sin], axis=1))
        else:
            rows.append(jnp.concatenate([re * cos + im * sin, im * cos - re * sin], axis=1))
    return lane_product(jnp.concatenate(rows, axis=0), lane_ref)


def lane_product(value, table_ref):
    high, low = split_value(value)
    out = jnp.dot(high, table_ref[0], preferred_element_type=F32)
    out += jnp.dot(low, table_ref[0], preferred_element_type=F32)
    return out + jnp.dot(high, table_ref[1], preferred_element_type=F32)


def conj_product(first, second):
    are, aim = first[:, :LANES], first[:, LANES:]
    bre, bim = second[:, :LANES], second[:, LANES:]
    return jnp.concatenate([are * bre + aim * bim, are * bim - aim * bre], axis=1)


def plain_product(first, second):
    are, aim = first[:, :LANES], first[:, LANES:]
    bre, bim = second[:, :LANES], second[:, LANES:]
    return jnp.concatenate([are * bre - aim * bim, are * bim + aim * bre], axis=1)


def signal_rows(spec, twist_ref, back_lane_ref):
    back = lane_product(spec, back_lane_ref)
    freqs = []
    for k in range(HALF):
        re = back[k * CHUNK : (k + 1) * CHUNK, :LANES]
        im = back[k * CHUNK : (k + 1) * CHUNK, LANES:]
        cos, sin = twist_ref[k, 2:3, :], twist_ref[k, 3:4, :]
        if k in (0, ROWS):
            freqs.append((re * cos - im * sin, None))
        else:
            freqs.append((re * cos - im * sin, im * cos + re * sin))
    return real_inverse(freqs, FREQS, True)


def slot(row):
    return row % SIDE * SIDE + row // SIDE


def half_start(kept):
    mine = lax.axis_index("dm")
    return pl.multiple_of((mine if kept else 1 - mine) * CHUNK, CHUNK)


def taps_grad_kernel(kept, signals, lane_ref, back_lane_ref, twist_ref, spec_ref, out):
    first = half_start(kept)
    batch = signals.shape[0] // ROWS
    chans = 2 * (signals.shape[1] // 5)
    rows = {}
    for which in range(2):
        place = pl.ds(pl.multiple_of(which * chans + first, CHUNK), CHUNK)
        for b in range(batch):
            rows[which, b] = spectrum(
                lambda r: signals[b * ROWS + slot(r), place, :].astype(F32), twist_ref, lane_ref
            )
            spec_ref[which * batch + b] = rows[which, b]
    product = conj_product(rows[0, 0], rows[1, 0])
    for b in range(1, batch):
        product = product + conj_product(rows[0, b], rows[1, b])
    for r, row in enumerate(signal_rows(product, twist_ref, back_lane_ref)):
        out[slot(r)] = row.astype(BF16)


def state_kernel(signals, gain_ref, lane_ref, back_lane_ref, twist_ref, *refs):
    *specs, out, skip_ref = refs
    batch = signals.shape[0] // ROWS
    chans = out.shape[1] // 2
    share = signals.shape[1] - 2 * chans
    place = (lax.axis_index("pl") * SIDE + lax.axis_index("x")) * SIDE + lax.axis_index("y")
    pieces = LANES // chans
    gains = jnp.broadcast_to(gain_ref[pl.ds(place // pieces, 1), :], (LANES, LANES))
    skip_ref[...] = gains.T
    begin = pl.multiple_of(place % pieces * chans, chans)
    for kept, spec_ref in enumerate(specs):
        first = half_start(kept)
        source = first // share
        taps = spectrum(
            lambda r: signals[source * ROWS + slot(r), pl.ds(2 * chans, CHUNK), :].astype(F32),
            twist_ref,
            lane_ref,
        )
        skip = skip_ref[pl.ds(pl.multiple_of(begin + first, CHUNK), CHUNK), :]
        for which, product in enumerate((plain_product, conj_product)):
            place = pl.ds(pl.multiple_of(which * chans + first, CHUNK), CHUNK)
            for b in range(batch):
                spec = product(taps, spec_ref[which * batch + b])
                for r, row in enumerate(signal_rows(spec, twist_ref, back_lane_ref)):
                    own = signals[b * ROWS + slot(r), place, :].astype(F32)
                    out[b * ROWS + slot(r), place, :] = (row + skip * own).astype(BF16)


def output_kernel(back, query, key, value, grad, *refs):
    outs, held, sems = refs[:5], refs[5:10], refs[10]
    own = back.shape[1] // 3
    pieces = LANES // own
    width = query.shape[1] // GROUPS
    sent = []
    for group in range(GROUPS):
        for tile in range(group * width // LANES, (group + 1) * width // LANES):
            cols = pl.ds(tile * LANES, LANES)
            blocks = [tile * pieces + i for i in range(pieces)]
            state, dmixed, term = (
                jnp.concatenate([back[i, pl.ds(which * own, own), :] for i in blocks], axis=0).T
                for which in range(3)
            )
            state, dmixed = state.astype(F32), dmixed.astype(F32)
            held[0][:, cols] = (query[:, cols].astype(F32) * state).astype(BF16)
            held[1][:, cols] = (grad[:, cols].astype(F32) * state).astype(BF16)
            held[2][:, cols] = (dmixed * value[:, cols].astype(F32)).astype(BF16)
            held[3][:, cols] = (dmixed * key[:, cols].astype(F32)).astype(BF16)
            held[4][:, cols] = term
        cols = pl.ds(group * width, width)
        pairs = [(a.at[:, cols], b.at[:, cols]) for a, b in zip(held, outs)]
        sent += start_copies(pairs, sems.at[group])
    for copy in sent:
        copy.wait()


def call(kernel, shapes, args, scratch=(), in_hbm=False, out_hbm=False, flops=0, moved=2 << 20, limit=24):
    place = lambda hbm: pl.BlockSpec(memory_space=pltpu.HBM if hbm else pltpu.VMEM)
    return pl.pallas_call(
        kernel,
        out_shape=shapes,
        in_specs=[place(in_hbm)] * len(args),
        out_specs=jax.tree.map(lambda _: place(out_hbm), shapes),
        scratch_shapes=list(scratch),
        compiler_params=pltpu.CompilerParams(vmem_limit_bytes=limit << 20),
        cost_estimate=pl.CostEstimate(flops=flops, bytes_accessed=moved, transcendentals=0),
    )(*[pltpu.with_memory_space_constraint(a, pltpu.HBM) for a in args] if in_hbm else args)


def gate(query, key, value, grad, taps, peers):
    rows_dev, chan_dev = query.shape
    own = chan_dev // peers
    out_shape = (peers, 2 * own + own // 2, rows_dev)
    return call(
        gate_kernel,
        jax.ShapeDtypeStruct(out_shape, BF16),
        (query, key, value, grad, taps),
        [pltpu.VMEM((rows_dev, chan_dev), BF16)] * 5
        + [
            pltpu.SemaphoreType.DMA((GROUPS, 5)),
        ],
        in_hbm=True,
    )


def taps_grad(signals, kept, factor):
    batch = signals.shape[0] // ROWS
    forward_lane, inverse_lane = lane_tables()
    shape = jax.ShapeDtypeStruct
    return call(
        functools.partial(taps_grad_kernel, kept),
        (
            shape((2 * batch, HALF * CHUNK, 2 * LANES), F32),
            shape((ROWS, CHUNK, LANES), BF16),
        ),
        (signals, forward_lane, inverse_lane, twist_tables(factor)),
        flops=2 * 10**9,
    )


def states(signals, spectra, skip_gain, own):
    batch = signals.shape[0] // ROWS
    forward_lane, inverse_lane = lane_tables()
    return call(
        state_kernel,
        jax.ShapeDtypeStruct((batch * ROWS, 2 * own, LANES), BF16),
        (signals, skip_gain.reshape(-1, LANES), forward_lane, inverse_lane, twist_tables(1.0), *spectra),
        (pltpu.VMEM((LANES, LANES), F32),),
        flops=3 * 10**9,
    )


def outputs(back, query, key, value, grad):
    block = jax.ShapeDtypeStruct(query.shape, BF16)
    return call(
        output_kernel,
        (block,) * 5,
        (back, query, key, value, grad),
        [pltpu.VMEM(query.shape, BF16)] * 5 + [pltpu.SemaphoreType.DMA((GROUPS, 5))],
        out_hbm=True,
    )


def on_device(query_in, key_in, value_in, filter_taps, skip_gain, grad_out):
    seq_count, pair = lax.axis_size("y") * lax.axis_size("x"), lax.axis_size("pl")
    peers = seq_count * pair
    rows_dev, chan_dev = query_in.shape[1:]
    own = chan_dev // peers
    batch = query_in.shape[0] * lax.axis_size("dh") * lax.axis_size("dm") * pair
    factor = 1.0 / math.sqrt(batch * seq_count * rows_dev)
    query, key, value, grad = query_in[0], key_in[0], value_in[0], grad_out[0]

    def swap(values, axes):
        return lax.all_to_all(values, axes, split_axis=0, concat_axis=0, tiled=True)

    signals = swap(gate(query, key, value, grad, filter_taps, peers), ("pl", "x", "y"))

    def plus(a, b):
        return (a.astype(F32) + b.astype(F32)).astype(BF16)

    spectra, (given, term) = zip(*(taps_grad(signals, kept, factor) for kept in range(2)))
    taken = lax.ppermute(given, "dm", [(0, 1), (1, 0)])
    results = states(signals, spectra, skip_gain, own)
    taken, results = lax.optimization_barrier((taken, results))
    term = plus(term, taken)
    term = plus(term, lax.ppermute(term, "dh", [(0, 1), (1, 0)]))
    halves = lax.all_gather(term, "dm")
    copies = [jnp.broadcast_to(t[None], (pair,) + t.shape).reshape((peers,) + t.shape[1:]) for t in halves]
    back = swap(jnp.concatenate([results, *copies], axis=1), ("pl", "x", "y"))
    outs = outputs(back, query, key, value, grad)
    return tuple(out[None] for out in outs[:4]) + (outs[4],)


def solution(mesh):
    dp, chan, seq = (mesh.shape[name] for name in ("dp", "chan", "seq"))
    split_mesh = Mesh(
        mesh.devices.reshape(dp // 4, 2, 2, chan, seq // SIDE, SIDE),
        ("dh", "dm", "pl", "chan", "y", "x"),
    )
    rows = P(("dh", "dm", "pl"), ("y", "x"), "chan")
    taps = P(("y", "x"), "chan")
    return jax.shard_map(
        on_device,
        mesh=split_mesh,
        in_specs=(rows, rows, rows, taps, P("chan"), rows),
        out_specs=(rows, rows, rows, rows, taps),
        check_vma=False,
    )
```

```python
import functools
import math

import jax
import jax.numpy as jnp
import numpy as np
from jax import lax
from jax.experimental import pallas as pl
from jax.experimental.pallas import tpu as pltpu
from jax.sharding import Mesh
from jax.sharding import PartitionSpec as P

F32 = jnp.float32
BF16 = jnp.bfloat16
LANES = 128
ROWS = 16
SIDE = 4
FREQS = 2 * ROWS
HALF = ROWS + 1
CHUNK = 16
GROUPS = 2


def unit(numer, denom):
    angle = 2.0 * math.pi * numer / denom
    return (math.cos(angle), math.sin(angle))


def times_unit(value, numer, denom):
    re, im = value
    numer = numer % denom
    if 4 * numer % denom == 0:
        return ((re, im), (-im, re), (-re, -im), (im, -re))[4 * numer // denom]
    if 8 * numer % denom == 0:
        root = math.sqrt(0.5)
        summed, apart = (re + im) * root, (re - im) * root
        return {1: (apart, summed), 3: (-summed, apart), 5: (-apart, -summed), 7: (summed, -apart)}[
            8 * numer // denom
        ]
    cos, sin = unit(numer, denom)
    return (re * cos - im * sin, re * sin + im * cos)


def add(a, b):
    return (a[0] + b[0], a[1] + b[1])


def sub(a, b):
    return (a[0] - b[0], a[1] - b[1])


def conj(a):
    return (a[0], -a[1])


def complex_dft(values, sign):
    count = len(values)
    if count == 1:
        return list(values)
    even = complex_dft(values[0::2], sign)
    odd = complex_dft(values[1::2], sign)
    turned = [times_unit(v, sign * j, count) for j, v in enumerate(odd)]
    return [add(e, t) for e, t in zip(even, turned)] + [sub(e, t) for e, t in zip(even, turned)]


def odd_freqs(first, second, count):
    turned = [
        times_unit((a, -b), -r, count) for r, (a, b) in enumerate(zip(first, second))
    ]
    return {4 * j + 1: v for j, v in enumerate(complex_dft(turned, -1))}


def real_dft(values, count):
    half, quarter = count // 2, count // 4
    if count == 2:
        return [(values[0] + values[1], None), (values[0] - values[1], None)]
    if len(values) == half:
        folded, apart = values, values
    else:
        folded = [values[r] + values[r + half] for r in range(half)]
        apart = [values[r] - values[r + half] for r in range(half)]
    out = [None] * (half + 1)
    out[0::2] = real_dft(folded, half)
    for freq, value in odd_freqs(apart[:quarter], apart[quarter:], count).items():
        if freq <= half:
            out[freq] = value
        else:
            out[count - freq] = conj(value)
    return out


def real_inverse(freqs, count, keep_half):
    half, quarter = count // 2, count // 4
    if count == 2:
        first, last = freqs[0][0], freqs[1][0]
        return [first + last, first - last]
    even = real_inverse(freqs[0::2], half, False)
    picked = [
        freqs[4 * j + 1] if 4 * j + 1 <= half else conj(freqs[count - 4 * j - 1])
        for j in range(quarter)
    ]
    turned = [times_unit(v, r, count) for r, v in enumerate(complex_dft(picked, 1))]
    odd = [re for re, _ in turned] + [-im for _, im in turned]
    low = [e + o for e, o in zip(even, odd)]
    if keep_half:
        return low
    return low + [e - o for e, o in zip(even, odd)]


def split_table(table):
    high = table.astype(np.float32).astype(BF16)
    low = (table - high.astype(np.float64)).astype(BF16)
    return np.stack([high, low])


def lane_tables():
    idx = np.arange(LANES)
    angle = 2.0 * np.pi / LANES * (idx[:, None] * idx[None, :] % LANES)
    cos, sin = np.cos(angle), np.sin(angle)
    forward = np.block([[cos, -sin], [sin, cos]])
    inverse = np.block([[cos, sin], [-sin, cos]])
    return split_table(forward), split_table(inverse)


def twist_tables(factor):
    padded = FREQS * LANES
    angle = 2.0 * np.pi / padded * (np.arange(HALF)[:, None] * np.arange(LANES)[None, :])
    weight = np.full((HALF, 1), 2.0)
    weight[0] = weight[-1] = 1.0
    weight = weight / padded * factor
    cos, sin = np.cos(angle), np.sin(angle)
    return np.stack([cos, sin, cos * weight, sin * weight], axis=1).astype(np.float32)


def split_value(value):
    high = value.astype(BF16)
    return high, (value - high.astype(F32)).astype(BF16)


def start_copies(pairs, sems):
    copies = [pltpu.make_async_copy(a, b, sems.at[i]) for i, (a, b) in enumerate(pairs)]
    for copy in copies:
        copy.start()
    return copies


def gate_kernel(query, key, value, grad, taps, out, *scratch):
    held, sems = scratch[:5], scratch[5]
    key_v, value_v, grad_v, query_v, taps_v = held
    peers = out.shape[0]
    own = taps.shape[1] // peers
    share = out.shape[1] - 2 * own
    pieces = LANES // own
    width = taps.shape[1] // GROUPS
    begin = lax.axis_index("pl") * share
    arrivals = []
    for group in range(GROUPS):
        cols = pl.ds(group * width, width)
        pairs = [(a.at[:, cols], b.at[:, cols]) for a, b in zip((key, value, grad, query, taps), held)]
        arrivals.append(start_copies(pairs, sems.at[group]))
    for group, copies in enumerate(arrivals):
        for copy in copies:
            copy.wait()
        tiles = width // LANES
        for tile in range(group * tiles, (group + 1) * tiles):
            cols = pl.ds(tile * LANES, LANES)
            mixed = (key_v[:, cols].astype(F32) * value_v[:, cols].astype(F32)).astype(BF16)
            state = (grad_v[:, cols].astype(F32) * query_v[:, cols].astype(F32)).astype(BF16)
            for place, block in enumerate((mixed, state)):
                turned = block.T
                for i in range(pieces):
                    rows = pl.ds(place * own, own)
                    out[tile * pieces + i, rows, :] = turned[i * own : (i + 1) * own]
            turned = taps_v[:, cols].T
            for i in range(pieces):
                low = turned[i * own : i * own + share]
                high = turned[i * own + share : (i + 1) * own]
                rows = pl.ds(2 * own, share)
                out[tile * pieces + i, rows, :] = jnp.where(begin == 0, low, high)


def spectrum(get_row, twist_ref, lane_ref):
    freqs = real_dft([get_row(r) for r in range(ROWS)], FREQS)
    rows = []
    for k, (re, im) in enumerate(freqs):
        cos, sin = twist_ref[k, 0:1, :], twist_ref[k, 1:2, :]
        if im is None:
            rows.append(jnp.concatenate([re * cos, -re * sin], axis=1))
        else:
            rows.append(jnp.concatenate([re * cos + im * sin, im * cos - re * sin], axis=1))
    return lane_product(jnp.concatenate(rows, axis=0), lane_ref)


def lane_product(value, table_ref):
    high, low = split_value(value)
    out = jnp.dot(high, table_ref[0], preferred_element_type=F32)
    out += jnp.dot(low, table_ref[0], preferred_element_type=F32)
    return out + jnp.dot(high, table_ref[1], preferred_element_type=F32)


def conj_product(first, second):
    are, aim = first[:, :LANES], first[:, LANES:]
    bre, bim = second[:, :LANES], second[:, LANES:]
    return jnp.concatenate([are * bre + aim * bim, are * bim - aim * bre], axis=1)


def plain_product(first, second):
    are, aim = first[:, :LANES], first[:, LANES:]
    bre, bim = second[:, :LANES], second[:, LANES:]
    return jnp.concatenate([are * bre - aim * bim, are * bim + aim * bre], axis=1)


def signal_rows(spec, twist_ref, back_lane_ref):
    back = lane_product(spec, back_lane_ref)
    freqs = []
    for k in range(HALF):
        re = back[k * CHUNK : (k + 1) * CHUNK, :LANES]
        im = back[k * CHUNK : (k + 1) * CHUNK, LANES:]
        cos, sin = twist_ref[k, 2:3, :], twist_ref[k, 3:4, :]
        if k in (0, ROWS):
            freqs.append((re * cos - im * sin, None))
        else:
            freqs.append((re * cos - im * sin, im * cos + re * sin))
    return real_inverse(freqs, FREQS, True)


def slot(row):
    return row % SIDE * SIDE + row // SIDE


def half_start(kept):
    mine = lax.axis_index("dm")
    return pl.multiple_of((mine if kept else 1 - mine) * CHUNK, CHUNK)


def taps_grad_kernel(kept, signals, lane_ref, back_lane_ref, twist_ref, spec_ref, out):
    first = half_start(kept)
    batch = signals.shape[0] // ROWS
    chans = 2 * (signals.shape[1] // 5)
    rows = {}
    for which in range(2):
        place = pl.ds(pl.multiple_of(which * chans + first, CHUNK), CHUNK)
        for b in range(batch):
            rows[which, b] = spectrum(
                lambda r: signals[b * ROWS + slot(r), place, :].astype(F32), twist_ref, lane_ref
            )
            spec_ref[which * batch + b] = rows[which, b]
    product = conj_product(rows[0, 0], rows[1, 0])
    for b in range(1, batch):
        product = product + conj_product(rows[0, b], rows[1, b])
    for r, row in enumerate(signal_rows(product, twist_ref, back_lane_ref)):
        out[slot(r)] = row.astype(BF16)


def state_kernel(signals, gain_ref, lane_ref, back_lane_ref, twist_ref, *refs):
    *specs, out, skip_ref = refs
    batch = signals.shape[0] // ROWS
    chans = out.shape[1] // 2
    share = signals.shape[1] - 2 * chans
    place = (lax.axis_index("pl") * SIDE + lax.axis_index("x")) * SIDE + lax.axis_index("y")
    pieces = LANES // chans
    gains = jnp.broadcast_to(gain_ref[pl.ds(place // pieces, 1), :], (LANES, LANES))
    skip_ref[...] = gains.T
    begin = pl.multiple_of(place % pieces * chans, chans)
    for kept, spec_ref in enumerate(specs):
        first = half_start(kept)
        source = first // share
        taps = spectrum(
            lambda r: signals[source * ROWS + slot(r), pl.ds(2 * chans, CHUNK), :].astype(F32),
            twist_ref,
            lane_ref,
        )
        skip = skip_ref[pl.ds(pl.multiple_of(begin + first, CHUNK), CHUNK), :]
        for which, product in enumerate((plain_product, conj_product)):
            place = pl.ds(pl.multiple_of(which * chans + first, CHUNK), CHUNK)
            for b in range(batch):
                spec = product(taps, spec_ref[which * batch + b])
                for r, row in enumerate(signal_rows(spec, twist_ref, back_lane_ref)):
                    own = signals[b * ROWS + slot(r), place, :].astype(F32)
                    out[b * ROWS + slot(r), place, :] = (row + skip * own).astype(BF16)


def output_kernel(back, query, key, value, grad, *refs):
    outs, held, sems = refs[:5], refs[5:10], refs[10]
    own = back.shape[1] // 3
    pieces = LANES // own
    width = query.shape[1] // GROUPS
    places = (half_start(1), half_start(0))
    halves = [pl.ds(pl.multiple_of(2 * own + place, CHUNK), CHUNK) for place in places]
    sent = []
    for group in range(GROUPS):
        for tile in range(group * width // LANES, (group + 1) * width // LANES):
            cols = pl.ds(tile * LANES, LANES)
            blocks = [tile * pieces + i for i in range(pieces)]
            state, dmixed = (
                jnp.concatenate([back[i, pl.ds(which * own, own), :] for i in blocks], axis=0).T
                for which in range(2)
            )
            term = jnp.concatenate([back[i, half, :] for i in blocks for half in halves], axis=0).T
            state, dmixed = state.astype(F32), dmixed.astype(F32)
            held[0][:, cols] = (query[:, cols].astype(F32) * state).astype(BF16)
            held[1][:, cols] = (grad[:, cols].astype(F32) * state).astype(BF16)
            held[2][:, cols] = (dmixed * value[:, cols].astype(F32)).astype(BF16)
            held[3][:, cols] = (dmixed * key[:, cols].astype(F32)).astype(BF16)
            held[4][:, cols] = term
        cols = pl.ds(group * width, width)
        pairs = [(a.at[:, cols], b.at[:, cols]) for a, b in zip(held, outs)]
        sent += start_copies(pairs, sems.at[group])
    for copy in sent:
        copy.wait()


def call(kernel, shapes, args, scratch=(), in_hbm=False, out_hbm=False, flops=0, moved=2 << 20, limit=24):
    place = lambda hbm: pl.BlockSpec(memory_space=pltpu.HBM if hbm else pltpu.VMEM)
    return pl.pallas_call(
        kernel,
        out_shape=shapes,
        in_specs=[place(in_hbm)] * len(args),
        out_specs=jax.tree.map(lambda _: place(out_hbm), shapes),
        scratch_shapes=list(scratch),
        compiler_params=pltpu.CompilerParams(vmem_limit_bytes=limit << 20),
        cost_estimate=pl.CostEstimate(flops=flops, bytes_accessed=moved, transcendentals=0),
    )(*[pltpu.with_memory_space_constraint(a, pltpu.HBM) for a in args] if in_hbm else args)


def gate(query, key, value, grad, taps, peers):
    rows_dev, chan_dev = query.shape
    own = chan_dev // peers
    out_shape = (peers, 2 * own + own // 2, rows_dev)
    return call(
        gate_kernel,
        jax.ShapeDtypeStruct(out_shape, BF16),
        (query, key, value, grad, taps),
        [pltpu.VMEM((rows_dev, chan_dev), BF16)] * 5
        + [
            pltpu.SemaphoreType.DMA((GROUPS, 5)),
        ],
        in_hbm=True,
    )


def taps_grad(signals, kept, factor):
    batch = signals.shape[0] // ROWS
    forward_lane, inverse_lane = lane_tables()
    shape = jax.ShapeDtypeStruct
    return call(
        functools.partial(taps_grad_kernel, kept),
        (
            shape((2 * batch, HALF * CHUNK, 2 * LANES), F32),
            shape((ROWS, CHUNK, LANES), BF16),
        ),
        (signals, forward_lane, inverse_lane, twist_tables(factor)),
        flops=2 * 10**9,
    )


def states(signals, spectra, skip_gain, own):
    batch = signals.shape[0] // ROWS
    forward_lane, inverse_lane = lane_tables()
    return call(
        state_kernel,
        jax.ShapeDtypeStruct((batch * ROWS, 2 * own, LANES), BF16),
        (signals, skip_gain.reshape(-1, LANES), forward_lane, inverse_lane, twist_tables(1.0), *spectra),
        (pltpu.VMEM((LANES, LANES), F32),),
        flops=3 * 10**9,
    )


def outputs(back, query, key, value, grad):
    block = jax.ShapeDtypeStruct(query.shape, BF16)
    return call(
        output_kernel,
        (block,) * 5,
        (back, query, key, value, grad),
        [pltpu.VMEM(query.shape, BF16)] * 5 + [pltpu.SemaphoreType.DMA((GROUPS, 5))],
        out_hbm=True,
    )


def on_device(query_in, key_in, value_in, filter_taps, skip_gain, grad_out):
    seq_count, pair = lax.axis_size("y") * lax.axis_size("x"), lax.axis_size("pl")
    peers = seq_count * pair
    rows_dev, chan_dev = query_in.shape[1:]
    own = chan_dev // peers
    batch = query_in.shape[0] * lax.axis_size("dh") * lax.axis_size("dm") * pair
    factor = 1.0 / math.sqrt(batch * seq_count * rows_dev)
    query, key, value, grad = query_in[0], key_in[0], value_in[0], grad_out[0]

    def swap(values, axes):
        return lax.all_to_all(values, axes, split_axis=0, concat_axis=0, tiled=True)

    signals = swap(gate(query, key, value, grad, filter_taps, peers), ("pl", "x", "y"))

    def exchange(values, axis):
        return lax.ppermute(values, axis, [(0, 1), (1, 0)])

    def plus(a, b):
        return (a.astype(F32) + b.astype(F32)).astype(BF16)

    spectra, (given, term) = zip(*(taps_grad(signals, kept, factor) for kept in range(2)))
    term = plus(term, exchange(given, "dm"))
    term = plus(*lax.all_gather(term, "dh"))
    other = exchange(term, "dm")
    spectra, _ = lax.optimization_barrier((spectra, term))
    results = states(signals, spectra, skip_gain, own)
    other, results = lax.optimization_barrier((other, results))
    copies = [jnp.broadcast_to(t[None], (pair,) + t.shape).reshape((peers,) + t.shape[1:]) for t in (term, other)]
    back = swap(jnp.concatenate([results, *copies], axis=1), ("pl", "x", "y"))
    outs = outputs(back, query, key, value, grad)
    return tuple(out[None] for out in outs[:4]) + (outs[4],)


def solution(mesh):
    dp, chan, seq = (mesh.shape[name] for name in ("dp", "chan", "seq"))
    split_mesh = Mesh(
        mesh.devices.reshape(dp // 4, 2, 2, chan, seq // SIDE, SIDE),
        ("dh", "dm", "pl", "chan", "y", "x"),
    )
    rows = P(("dh", "dm", "pl"), ("y", "x"), "chan")
    taps = P(("y", "x"), "chan")
    return jax.shard_map(
        on_device,
        mesh=split_mesh,
        in_specs=(rows, rows, rows, taps, P("chan"), rows),
        out_specs=(rows, rows, rows, rows, taps),
        check_vma=False,
    )
```

```python
import functools
import math

import jax
import jax.numpy as jnp
import numpy as np
from jax import lax
from jax.experimental import pallas as pl
from jax.experimental.pallas import tpu as pltpu
from jax.sharding import Mesh
from jax.sharding import PartitionSpec as P

F32 = jnp.float32
BF16 = jnp.bfloat16
LANES = 128
ROWS = 16
SIDE = 4
FREQS = 2 * ROWS
HALF = ROWS + 1
CHUNK = 16
GROUPS = 2


def unit(numer, denom):
    angle = 2.0 * math.pi * numer / denom
    return (math.cos(angle), math.sin(angle))


def times_unit(value, numer, denom):
    re, im = value
    numer = numer % denom
    if 4 * numer % denom == 0:
        return ((re, im), (-im, re), (-re, -im), (im, -re))[4 * numer // denom]
    if 8 * numer % denom == 0:
        root = math.sqrt(0.5)
        summed, apart = (re + im) * root, (re - im) * root
        return {1: (apart, summed), 3: (-summed, apart), 5: (-apart, -summed), 7: (summed, -apart)}[
            8 * numer // denom
        ]
    cos, sin = unit(numer, denom)
    return (re * cos - im * sin, re * sin + im * cos)


def add(a, b):
    return (a[0] + b[0], a[1] + b[1])


def sub(a, b):
    return (a[0] - b[0], a[1] - b[1])


def conj(a):
    return (a[0], -a[1])


def complex_dft(values, sign):
    count = len(values)
    if count == 1:
        return list(values)
    even = complex_dft(values[0::2], sign)
    odd = complex_dft(values[1::2], sign)
    turned = [times_unit(v, sign * j, count) for j, v in enumerate(odd)]
    return [add(e, t) for e, t in zip(even, turned)] + [sub(e, t) for e, t in zip(even, turned)]


def odd_freqs(first, second, count):
    turned = [
        times_unit((a, -b), -r, count) for r, (a, b) in enumerate(zip(first, second))
    ]
    return {4 * j + 1: v for j, v in enumerate(complex_dft(turned, -1))}


def real_dft(values, count):
    half, quarter = count // 2, count // 4
    if count == 2:
        return [(values[0] + values[1], None), (values[0] - values[1], None)]
    if len(values) == half:
        folded, apart = values, values
    else:
        folded = [values[r] + values[r + half] for r in range(half)]
        apart = [values[r] - values[r + half] for r in range(half)]
    out = [None] * (half + 1)
    out[0::2] = real_dft(folded, half)
    for freq, value in odd_freqs(apart[:quarter], apart[quarter:], count).items():
        if freq <= half:
            out[freq] = value
        else:
            out[count - freq] = conj(value)
    return out


def real_inverse(freqs, count, keep_half):
    half, quarter = count // 2, count // 4
    if count == 2:
        first, last = freqs[0][0], freqs[1][0]
        return [first + last, first - last]
    even = real_inverse(freqs[0::2], half, False)
    picked = [
        freqs[4 * j + 1] if 4 * j + 1 <= half else conj(freqs[count - 4 * j - 1])
        for j in range(quarter)
    ]
    turned = [times_unit(v, r, count) for r, v in enumerate(complex_dft(picked, 1))]
    odd = [re for re, _ in turned] + [-im for _, im in turned]
    low = [e + o for e, o in zip(even, odd)]
    if keep_half:
        return low
    return low + [e - o for e, o in zip(even, odd)]


def split_table(table):
    high = table.astype(np.float32).astype(BF16)
    low = (table - high.astype(np.float64)).astype(BF16)
    return np.stack([high, low])


def lane_tables():
    idx = np.arange(LANES)
    angle = 2.0 * np.pi / LANES * (idx[:, None] * idx[None, :] % LANES)
    cos, sin = np.cos(angle), np.sin(angle)
    forward = np.block([[cos, -sin], [sin, cos]])
    inverse = np.block([[cos, sin], [-sin, cos]])
    return split_table(forward), split_table(inverse)


def twist_tables(factor):
    padded = FREQS * LANES
    angle = 2.0 * np.pi / padded * (np.arange(HALF)[:, None] * np.arange(LANES)[None, :])
    weight = np.full((HALF, 1), 2.0)
    weight[0] = weight[-1] = 1.0
    weight = weight / padded * factor
    cos, sin = np.cos(angle), np.sin(angle)
    return np.stack([cos, sin, cos * weight, sin * weight], axis=1).astype(np.float32)


def split_value(value):
    high = value.astype(BF16)
    return high, (value - high.astype(F32)).astype(BF16)


def start_copies(pairs, sems):
    copies = [pltpu.make_async_copy(a, b, sems.at[i]) for i, (a, b) in enumerate(pairs)]
    for copy in copies:
        copy.start()
    return copies


def gate_kernel(query, key, value, grad, taps, out, *scratch):
    held, sems = scratch[:5], scratch[5]
    key_v, value_v, grad_v, query_v, taps_v = held
    peers = out.shape[0]
    own = taps.shape[1] // peers
    share = out.shape[1] - 2 * own
    pieces = LANES // own
    width = taps.shape[1] // GROUPS
    begin = lax.axis_index("pl") * share
    arrivals = []
    for group in range(GROUPS):
        cols = pl.ds(group * width, width)
        pairs = [(a.at[:, cols], b.at[:, cols]) for a, b in zip((key, value, grad, query, taps), held)]
        arrivals.append(start_copies(pairs, sems.at[group]))
    for group, copies in enumerate(arrivals):
        for copy in copies:
            copy.wait()
        tiles = width // LANES
        for tile in range(group * tiles, (group + 1) * tiles):
            cols = pl.ds(tile * LANES, LANES)
            mixed = (key_v[:, cols].astype(F32) * value_v[:, cols].astype(F32)).astype(BF16)
            state = (grad_v[:, cols].astype(F32) * query_v[:, cols].astype(F32)).astype(BF16)
            for place, block in enumerate((mixed, state)):
                turned = block.T
                for i in range(pieces):
                    rows = pl.ds(place * own, own)
                    out[tile * pieces + i, rows, :] = turned[i * own : (i + 1) * own]
            turned = taps_v[:, cols].T
            for i in range(pieces):
                low = turned[i * own : i * own + share]
                high = turned[i * own + share : (i + 1) * own]
                rows = pl.ds(2 * own, share)
                out[tile * pieces + i, rows, :] = jnp.where(begin == 0, low, high)


def spectrum(get_row, twist_ref, lane_ref):
    freqs = real_dft([get_row(r) for r in range(ROWS)], FREQS)
    rows = []
    for k, (re, im) in enumerate(freqs):
        cos, sin = twist_ref[k, 0:1, :], twist_ref[k, 1:2, :]
        if im is None:
            rows.append(jnp.concatenate([re * cos, -re * sin], axis=1))
        else:
            rows.append(jnp.concatenate([re * cos + im * sin, im * cos - re * sin], axis=1))
    return lane_product(jnp.concatenate(rows, axis=0), lane_ref)


def lane_product(value, table_ref):
    high, low = split_value(value)
    out = jnp.dot(high, table_ref[0], preferred_element_type=F32)
    out += jnp.dot(low, table_ref[0], preferred_element_type=F32)
    return out + jnp.dot(high, table_ref[1], preferred_element_type=F32)


def conj_product(first, second):
    are, aim = first[:, :LANES], first[:, LANES:]
    bre, bim = second[:, :LANES], second[:, LANES:]
    return jnp.concatenate([are * bre + aim * bim, are * bim - aim * bre], axis=1)


def plain_product(first, second):
    are, aim = first[:, :LANES], first[:, LANES:]
    bre, bim = second[:, :LANES], second[:, LANES:]
    return jnp.concatenate([are * bre - aim * bim, are * bim + aim * bre], axis=1)


def signal_rows(spec, twist_ref, back_lane_ref):
    back = lane_product(spec, back_lane_ref)
    freqs = []
    for k in range(HALF):
        re = back[k * CHUNK : (k + 1) * CHUNK, :LANES]
        im = back[k * CHUNK : (k + 1) * CHUNK, LANES:]
        cos, sin = twist_ref[k, 2:3, :], twist_ref[k, 3:4, :]
        if k in (0, ROWS):
            freqs.append((re * cos - im * sin, None))
        else:
            freqs.append((re * cos - im * sin, im * cos + re * sin))
    return real_inverse(freqs, FREQS, True)


def slot(row):
    return row % SIDE * SIDE + row // SIDE


def half_start(kept):
    mine = lax.axis_index("dm")
    return pl.multiple_of((mine if kept else 1 - mine) * CHUNK, CHUNK)


def taps_grad_kernel(kept, signals, lane_ref, back_lane_ref, twist_ref, spec_ref, out):
    first = half_start(kept)
    batch = signals.shape[0] // ROWS
    chans = 2 * (signals.shape[1] // 5)
    rows = {}
    for which in range(2):
        place = pl.ds(pl.multiple_of(which * chans + first, CHUNK), CHUNK)
        for b in range(batch):
            rows[which, b] = spectrum(
                lambda r: signals[b * ROWS + slot(r), place, :].astype(F32), twist_ref, lane_ref
            )
            spec_ref[which * batch + b] = rows[which, b]
    product = conj_product(rows[0, 0], rows[1, 0])
    for b in range(1, batch):
        product = product + conj_product(rows[0, b], rows[1, b])
    for r, row in enumerate(signal_rows(product, twist_ref, back_lane_ref)):
        out[slot(r)] = row.astype(BF16)


def state_kernel(kept, signals, gain_ref, lane_ref, back_lane_ref, twist_ref, spec_ref, out, skip_ref):
    batch = signals.shape[0] // ROWS
    chans = 2 * (signals.shape[1] // 5)
    share = signals.shape[1] - 2 * chans
    place = (lax.axis_index("pl") * SIDE + lax.axis_index("x")) * SIDE + lax.axis_index("y")
    pieces = LANES // chans
    gains = jnp.broadcast_to(gain_ref[pl.ds(place // pieces, 1), :], (LANES, LANES))
    skip_ref[...] = gains.T
    first = half_start(kept)
    begin = place % pieces * chans + first
    skip = skip_ref[pl.ds(pl.multiple_of(begin, CHUNK), CHUNK), :]
    source = first // share
    taps = spectrum(
        lambda r: signals[source * ROWS + slot(r), pl.ds(2 * chans, CHUNK), :].astype(F32),
        twist_ref,
        lane_ref,
    )
    for which, product in enumerate((plain_product, conj_product)):
        rows = pl.ds(pl.multiple_of(which * chans + first, CHUNK), CHUNK)
        for b in range(batch):
            spec = product(taps, spec_ref[which * batch + b])
            for r, row in enumerate(signal_rows(spec, twist_ref, back_lane_ref)):
                own = signals[b * ROWS + slot(r), rows, :].astype(F32)
                result = (row + skip * own).astype(BF16)
                out[b * ROWS + slot(r), pl.ds(which * CHUNK, CHUNK), :] = result


def output_kernel(back, query, key, value, grad, *refs):
    outs, held, sems = refs[:5], refs[5:10], refs[10]
    own = back.shape[1] // 3
    pieces = LANES // own
    width = query.shape[1] // GROUPS
    places = (half_start(0), half_start(1))
    parts = [
        [pl.ds(pl.multiple_of(2 * place + which * CHUNK, CHUNK), CHUNK) for place in places]
        for which in range(2)
    ]
    halves = [pl.ds(pl.multiple_of(2 * own + place, CHUNK), CHUNK) for place in places[::-1]]
    sent = []
    for group in range(GROUPS):
        for tile in range(group * width // LANES, (group + 1) * width // LANES):
            cols = pl.ds(tile * LANES, LANES)
            blocks = [tile * pieces + i for i in range(pieces)]
            state, dmixed = (
                jnp.concatenate([back[i, part, :] for i in blocks for part in parts[which]], axis=0).T
                for which in range(2)
            )
            term = jnp.concatenate([back[i, half, :] for i in blocks for half in halves], axis=0).T
            state, dmixed = state.astype(F32), dmixed.astype(F32)
            held[0][:, cols] = (query[:, cols].astype(F32) * state).astype(BF16)
            held[1][:, cols] = (grad[:, cols].astype(F32) * state).astype(BF16)
            held[2][:, cols] = (dmixed * value[:, cols].astype(F32)).astype(BF16)
            held[3][:, cols] = (dmixed * key[:, cols].astype(F32)).astype(BF16)
            held[4][:, cols] = term
        cols = pl.ds(group * width, width)
        pairs = [(a.at[:, cols], b.at[:, cols]) for a, b in zip(held, outs)]
        sent += start_copies(pairs, sems.at[group])
    for copy in sent:
        copy.wait()


def call(kernel, shapes, args, scratch=(), in_hbm=False, out_hbm=False, flops=0, moved=2 << 20, limit=24):
    place = lambda hbm: pl.BlockSpec(memory_space=pltpu.HBM if hbm else pltpu.VMEM)
    return pl.pallas_call(
        kernel,
        out_shape=shapes,
        in_specs=[place(in_hbm)] * len(args),
        out_specs=jax.tree.map(lambda _: place(out_hbm), shapes),
        scratch_shapes=list(scratch),
        compiler_params=pltpu.CompilerParams(vmem_limit_bytes=limit << 20),
        cost_estimate=pl.CostEstimate(flops=flops, bytes_accessed=moved, transcendentals=0),
    )(*[pltpu.with_memory_space_constraint(a, pltpu.HBM) for a in args] if in_hbm else args)


def gate(query, key, value, grad, taps, peers):
    rows_dev, chan_dev = query.shape
    own = chan_dev // peers
    out_shape = (peers, 2 * own + own // 2, rows_dev)
    return call(
        gate_kernel,
        jax.ShapeDtypeStruct(out_shape, BF16),
        (query, key, value, grad, taps),
        [pltpu.VMEM((rows_dev, chan_dev), BF16)] * 5
        + [
            pltpu.SemaphoreType.DMA((GROUPS, 5)),
        ],
        in_hbm=True,
    )


def taps_grad(signals, kept, factor):
    batch = signals.shape[0] // ROWS
    forward_lane, inverse_lane = lane_tables()
    shape = jax.ShapeDtypeStruct
    return call(
        functools.partial(taps_grad_kernel, kept),
        (
            shape((2 * batch, HALF * CHUNK, 2 * LANES), F32),
            shape((ROWS, CHUNK, LANES), BF16),
        ),
        (signals, forward_lane, inverse_lane, twist_tables(factor)),
        flops=2 * 10**9,
    )


def states(signals, kept, spectra, skip_gain):
    forward_lane, inverse_lane = lane_tables()
    return call(
        functools.partial(state_kernel, kept),
        jax.ShapeDtypeStruct((signals.shape[0], 2 * CHUNK, LANES), BF16),
        (signals, skip_gain.reshape(-1, LANES), forward_lane, inverse_lane, twist_tables(1.0), spectra),
        (pltpu.VMEM((LANES, LANES), F32),),
        flops=2 * 10**9,
    )


def outputs(back, query, key, value, grad):
    block = jax.ShapeDtypeStruct(query.shape, BF16)
    return call(
        output_kernel,
        (block,) * 5,
        (back, query, key, value, grad),
        [pltpu.VMEM(query.shape, BF16)] * 5 + [pltpu.SemaphoreType.DMA((GROUPS, 5))],
        out_hbm=True,
    )


def on_device(query_in, key_in, value_in, filter_taps, skip_gain, grad_out):
    seq_count, pair = lax.axis_size("y") * lax.axis_size("x"), lax.axis_size("pl")
    peers = seq_count * pair
    rows_dev, chan_dev = query_in.shape[1:]
    own = chan_dev // peers
    batch = query_in.shape[0] * lax.axis_size("dh") * lax.axis_size("dm") * pair
    factor = 1.0 / math.sqrt(batch * seq_count * rows_dev)
    query, key, value, grad = query_in[0], key_in[0], value_in[0], grad_out[0]

    def swap(values, axes):
        return lax.all_to_all(values, axes, split_axis=0, concat_axis=0, tiled=True)

    signals = swap(gate(query, key, value, grad, filter_taps, peers), ("pl", "x", "y"))

    def exchange(values, axis):
        return lax.ppermute(values, axis, [(0, 1), (1, 0)])

    def plus(a, b):
        return (a.astype(F32) + b.astype(F32)).astype(BF16)

    (spec_given, spec_kept), (given, term) = zip(*(taps_grad(signals, kept, factor) for kept in range(2)))
    taken = exchange(given, "dm")
    state_given = states(signals, 0, spec_given, skip_gain)
    taken, state_given = lax.optimization_barrier((taken, state_given))
    term = plus(term, taken)
    term = plus(*lax.all_gather(term, "dh"))
    other = exchange(term, "dm")
    spec_kept, _ = lax.optimization_barrier((spec_kept, term))
    state_kept = states(signals, 1, spec_kept, skip_gain)
    other, state_kept = lax.optimization_barrier((other, state_kept))
    copies = [jnp.broadcast_to(t[None], (pair,) + t.shape).reshape((peers,) + t.shape[1:]) for t in (term, other)]
    back = swap(jnp.concatenate([state_given, state_kept, *copies], axis=1), ("pl", "x", "y"))
    outs = outputs(back, query, key, value, grad)
    return tuple(out[None] for out in outs[:4]) + (outs[4],)


def solution(mesh):
    dp, chan, seq = (mesh.shape[name] for name in ("dp", "chan", "seq"))
    split_mesh = Mesh(
        mesh.devices.reshape(dp // 4, 2, 2, chan, seq // SIDE, SIDE),
        ("dh", "dm", "pl", "chan", "y", "x"),
    )
    rows = P(("dh", "dm", "pl"), ("y", "x"), "chan")
    taps = P(("y", "x"), "chan")
    return jax.shard_map(
        on_device,
        mesh=split_mesh,
        in_specs=(rows, rows, rows, taps, P("chan"), rows),
        out_specs=(rows, rows, rows, rows, taps),
        check_vma=False,
    )
```

```python
import functools
import math

import jax
import jax.numpy as jnp
import numpy as np
from jax import lax
from jax.experimental import pallas as pl
from jax.experimental.pallas import tpu as pltpu
from jax.sharding import Mesh
from jax.sharding import PartitionSpec as P

F32 = jnp.float32
BF16 = jnp.bfloat16
LANES = 128
ROWS = 16
SIDE = 4
FREQS = 2 * ROWS
HALF = ROWS + 1
CHUNK = 16
GROUPS = 2


def unit(numer, denom):
    angle = 2.0 * math.pi * numer / denom
    return (math.cos(angle), math.sin(angle))


def times_unit(value, numer, denom):
    re, im = value
    numer = numer % denom
    if 4 * numer % denom == 0:
        return ((re, im), (-im, re), (-re, -im), (im, -re))[4 * numer // denom]
    if 8 * numer % denom == 0:
        root = math.sqrt(0.5)
        summed, apart = (re + im) * root, (re - im) * root
        return {1: (apart, summed), 3: (-summed, apart), 5: (-apart, -summed), 7: (summed, -apart)}[
            8 * numer // denom
        ]
    cos, sin = unit(numer, denom)
    return (re * cos - im * sin, re * sin + im * cos)


def add(a, b):
    return (a[0] + b[0], a[1] + b[1])


def sub(a, b):
    return (a[0] - b[0], a[1] - b[1])


def conj(a):
    return (a[0], -a[1])


def complex_dft(values, sign):
    count = len(values)
    if count == 1:
        return list(values)
    even = complex_dft(values[0::2], sign)
    odd = complex_dft(values[1::2], sign)
    turned = [times_unit(v, sign * j, count) for j, v in enumerate(odd)]
    return [add(e, t) for e, t in zip(even, turned)] + [sub(e, t) for e, t in zip(even, turned)]


def odd_freqs(first, second, count):
    turned = [
        times_unit((a, -b), -r, count) for r, (a, b) in enumerate(zip(first, second))
    ]
    return {4 * j + 1: v for j, v in enumerate(complex_dft(turned, -1))}


def real_dft(values, count):
    half, quarter = count // 2, count // 4
    if count == 2:
        return [(values[0] + values[1], None), (values[0] - values[1], None)]
    if len(values) == half:
        folded, apart = values, values
    else:
        folded = [values[r] + values[r + half] for r in range(half)]
        apart = [values[r] - values[r + half] for r in range(half)]
    out = [None] * (half + 1)
    out[0::2] = real_dft(folded, half)
    for freq, value in odd_freqs(apart[:quarter], apart[quarter:], count).items():
        if freq <= half:
            out[freq] = value
        else:
            out[count - freq] = conj(value)
    return out


def real_inverse(freqs, count, keep_half):
    half, quarter = count // 2, count // 4
    if count == 2:
        first, last = freqs[0][0], freqs[1][0]
        return [first + last, first - last]
    even = real_inverse(freqs[0::2], half, False)
    picked = [
        freqs[4 * j + 1] if 4 * j + 1 <= half else conj(freqs[count - 4 * j - 1])
        for j in range(quarter)
    ]
    turned = [times_unit(v, r, count) for r, v in enumerate(complex_dft(picked, 1))]
    odd = [re for re, _ in turned] + [-im for _, im in turned]
    low = [e + o for e, o in zip(even, odd)]
    if keep_half:
        return low
    return low + [e - o for e, o in zip(even, odd)]


def split_table(table):
    high = table.astype(np.float32).astype(BF16)
    low = (table - high.astype(np.float64)).astype(BF16)
    return np.stack([high, low])


def lane_tables():
    idx = np.arange(LANES)
    angle = 2.0 * np.pi / LANES * (idx[:, None] * idx[None, :] % LANES)
    cos, sin = np.cos(angle), np.sin(angle)
    forward = np.block([[cos, -sin], [sin, cos]])
    inverse = np.block([[cos, sin], [-sin, cos]])
    return split_table(forward), split_table(inverse)


def twist_tables(factor):
    padded = FREQS * LANES
    angle = 2.0 * np.pi / padded * (np.arange(HALF)[:, None] * np.arange(LANES)[None, :])
    weight = np.full((HALF, 1), 2.0)
    weight[0] = weight[-1] = 1.0
    weight = weight / padded * factor
    cos, sin = np.cos(angle), np.sin(angle)
    return np.stack([cos, sin, cos * weight, sin * weight], axis=1).astype(np.float32)


def split_value(value):
    high = value.astype(BF16)
    return high, (value - high.astype(F32)).astype(BF16)


def start_copies(pairs, sems):
    copies = [pltpu.make_async_copy(a, b, sems.at[i]) for i, (a, b) in enumerate(pairs)]
    for copy in copies:
        copy.start()
    return copies


def gate_kernel(query, key, value, grad, taps, out, *scratch):
    held, sems = scratch[:5], scratch[5]
    key_v, value_v, grad_v, query_v, taps_v = held
    peers = out.shape[0]
    own = taps.shape[1] // peers
    share = out.shape[1] - 2 * own
    pieces = LANES // own
    width = taps.shape[1] // GROUPS
    begin = lax.axis_index("pl") * share
    arrivals = []
    for group in range(GROUPS):
        cols = pl.ds(group * width, width)
        pairs = [(a.at[:, cols], b.at[:, cols]) for a, b in zip((key, value, grad, query, taps), held)]
        arrivals.append(start_copies(pairs, sems.at[group]))
    tiles = width // LANES
    for group, copies in enumerate(arrivals):
        span = range(group * tiles, (group + 1) * tiles)
        for place, (one, other) in enumerate(((key_v, value_v), (grad_v, query_v))):
            copies[2 * place].wait()
            copies[2 * place + 1].wait()
            for tile in span:
                cols = pl.ds(tile * LANES, LANES)
                turned = (one[:, cols].astype(F32) * other[:, cols].astype(F32)).astype(BF16).T
                for i in range(pieces):
                    rows = pl.ds(place * own, own)
                    out[tile * pieces + i, rows, :] = turned[i * own : (i + 1) * own]
        copies[4].wait()
        for tile in span:
            turned = taps_v[:, pl.ds(tile * LANES, LANES)].T
            for i in range(pieces):
                low = turned[i * own : i * own + share]
                high = turned[i * own + share : (i + 1) * own]
                out[tile * pieces + i, pl.ds(2 * own, share), :] = jnp.where(begin == 0, low, high)


def spectrum(get_row, twist_ref, lane_ref):
    freqs = real_dft([get_row(r) for r in range(ROWS)], FREQS)
    rows = []
    for k, (re, im) in enumerate(freqs):
        cos, sin = twist_ref[k, 0:1, :], twist_ref[k, 1:2, :]
        if im is None:
            rows.append(jnp.concatenate([re * cos, -re * sin], axis=1))
        else:
            rows.append(jnp.concatenate([re * cos + im * sin, im * cos - re * sin], axis=1))
    return lane_product(jnp.concatenate(rows, axis=0), lane_ref)


def lane_product(value, table_ref):
    high, low = split_value(value)
    out = jnp.dot(high, table_ref[0], preferred_element_type=F32)
    out += jnp.dot(low, table_ref[0], preferred_element_type=F32)
    return out + jnp.dot(high, table_ref[1], preferred_element_type=F32)


def conj_product(first, second):
    are, aim = first[:, :LANES], first[:, LANES:]
    bre, bim = second[:, :LANES], second[:, LANES:]
    return jnp.concatenate([are * bre + aim * bim, are * bim - aim * bre], axis=1)


def plain_product(first, second):
    are, aim = first[:, :LANES], first[:, LANES:]
    bre, bim = second[:, :LANES], second[:, LANES:]
    return jnp.concatenate([are * bre - aim * bim, are * bim + aim * bre], axis=1)


def signal_rows(spec, twist_ref, back_lane_ref):
    back = lane_product(spec, back_lane_ref)
    freqs = []
    for k in range(HALF):
        re = back[k * CHUNK : (k + 1) * CHUNK, :LANES]
        im = back[k * CHUNK : (k + 1) * CHUNK, LANES:]
        cos, sin = twist_ref[k, 2:3, :], twist_ref[k, 3:4, :]
        if k in (0, ROWS):
            freqs.append((re * cos - im * sin, None))
        else:
            freqs.append((re * cos - im * sin, im * cos + re * sin))
    return real_inverse(freqs, FREQS, True)


def slot(row):
    return row % SIDE * SIDE + row // SIDE


def half_start(kept):
    mine = lax.axis_index("dm")
    return pl.multiple_of((mine if kept else 1 - mine) * CHUNK, CHUNK)


def taps_grad_kernel(kept, signals, lane_ref, back_lane_ref, twist_ref, spec_ref, out):
    first = half_start(kept)
    batch = signals.shape[0] // ROWS
    chans = 2 * (signals.shape[1] // 5)
    rows = {}
    for which in range(2):
        place = pl.ds(pl.multiple_of(which * chans + first, CHUNK), CHUNK)
        for b in range(batch):
            rows[which, b] = spectrum(
                lambda r: signals[b * ROWS + slot(r), place, :].astype(F32), twist_ref, lane_ref
            )
            spec_ref[which * batch + b] = rows[which, b]
    product = conj_product(rows[0, 0], rows[1, 0])
    for b in range(1, batch):
        product = product + conj_product(rows[0, b], rows[1, b])
    for r, row in enumerate(signal_rows(product, twist_ref, back_lane_ref)):
        out[slot(r)] = row.astype(BF16)


def state_kernel(signals, gain_ref, lane_ref, back_lane_ref, twist_ref, *refs):
    *specs, out, skip_ref = refs
    batch = signals.shape[0] // ROWS
    chans = out.shape[1] // 2
    share = signals.shape[1] - 2 * chans
    place = (lax.axis_index("pl") * SIDE + lax.axis_index("x")) * SIDE + lax.axis_index("y")
    pieces = LANES // chans
    gains = jnp.broadcast_to(gain_ref[pl.ds(place // pieces, 1), :], (LANES, LANES))
    skip_ref[...] = gains.T
    begin = pl.multiple_of(place % pieces * chans, chans)
    for kept, spec_ref in enumerate(specs):
        first = half_start(kept)
        source = first // share
        taps = spectrum(
            lambda r: signals[source * ROWS + slot(r), pl.ds(2 * chans, CHUNK), :].astype(F32),
            twist_ref,
            lane_ref,
        )
        skip = skip_ref[pl.ds(pl.multiple_of(begin + first, CHUNK), CHUNK), :]
        for which, product in enumerate((plain_product, conj_product)):
            place = pl.ds(pl.multiple_of(which * chans + first, CHUNK), CHUNK)
            for b in range(batch):
                spec = product(taps, spec_ref[which * batch + b])
                for r, row in enumerate(signal_rows(spec, twist_ref, back_lane_ref)):
                    own = signals[b * ROWS + slot(r), place, :].astype(F32)
                    out[b * ROWS + slot(r), place, :] = (row + skip * own).astype(BF16)


def output_kernel(back, query, key, value, grad, *refs):
    outs, held, sems = refs[:5], refs[5:10], refs[10]
    own = back.shape[1] // 3
    pieces = LANES // own
    width = query.shape[1] // GROUPS
    places = (half_start(1), half_start(0))
    halves = [pl.ds(pl.multiple_of(2 * own + place, CHUNK), CHUNK) for place in places]
    sent = []
    for group in range(GROUPS):
        for tile in range(group * width // LANES, (group + 1) * width // LANES):
            cols = pl.ds(tile * LANES, LANES)
            blocks = [tile * pieces + i for i in range(pieces)]
            state, dmixed = (
                jnp.concatenate([back[i, pl.ds(which * own, own), :] for i in blocks], axis=0).T
                for which in range(2)
            )
            term = jnp.concatenate([back[i, half, :] for i in blocks for half in halves], axis=0).T
            state, dmixed = state.astype(F32), dmixed.astype(F32)
            held[0][:, cols] = (query[:, cols].astype(F32) * state).astype(BF16)
            held[1][:, cols] = (grad[:, cols].astype(F32) * state).astype(BF16)
            held[2][:, cols] = (dmixed * value[:, cols].astype(F32)).astype(BF16)
            held[3][:, cols] = (dmixed * key[:, cols].astype(F32)).astype(BF16)
            held[4][:, cols] = term
        cols = pl.ds(group * width, width)
        pairs = [(a.at[:, cols], b.at[:, cols]) for a, b in zip(held, outs)]
        sent += start_copies(pairs, sems.at[group])
    for copy in sent:
        copy.wait()


def call(kernel, shapes, args, scratch=(), in_hbm=False, out_hbm=False, flops=0, moved=2 << 20, limit=24):
    place = lambda hbm: pl.BlockSpec(memory_space=pltpu.HBM if hbm else pltpu.VMEM)
    return pl.pallas_call(
        kernel,
        out_shape=shapes,
        in_specs=[place(in_hbm)] * len(args),
        out_specs=jax.tree.map(lambda _: place(out_hbm), shapes),
        scratch_shapes=list(scratch),
        compiler_params=pltpu.CompilerParams(vmem_limit_bytes=limit << 20),
        cost_estimate=pl.CostEstimate(flops=flops, bytes_accessed=moved, transcendentals=0),
    )(*[pltpu.with_memory_space_constraint(a, pltpu.HBM) for a in args] if in_hbm else args)


def gate(query, key, value, grad, taps, peers):
    rows_dev, chan_dev = query.shape
    own = chan_dev // peers
    out_shape = (peers, 2 * own + own // 2, rows_dev)
    return call(
        gate_kernel,
        jax.ShapeDtypeStruct(out_shape, BF16),
        (query, key, value, grad, taps),
        [pltpu.VMEM((rows_dev, chan_dev), BF16)] * 5
        + [
            pltpu.SemaphoreType.DMA((GROUPS, 5)),
        ],
        in_hbm=True,
    )


def taps_grad(signals, kept, factor):
    batch = signals.shape[0] // ROWS
    forward_lane, inverse_lane = lane_tables()
    shape = jax.ShapeDtypeStruct
    return call(
        functools.partial(taps_grad_kernel, kept),
        (
            shape((2 * batch, HALF * CHUNK, 2 * LANES), F32),
            shape((ROWS, CHUNK, LANES), BF16),
        ),
        (signals, forward_lane, inverse_lane, twist_tables(factor)),
        flops=2 * 10**9,
    )


def states(signals, spectra, skip_gain, own):
    batch = signals.shape[0] // ROWS
    forward_lane, inverse_lane = lane_tables()
    return call(
        state_kernel,
        jax.ShapeDtypeStruct((batch * ROWS, 2 * own, LANES), BF16),
        (signals, skip_gain.reshape(-1, LANES), forward_lane, inverse_lane, twist_tables(1.0), *spectra),
        (pltpu.VMEM((LANES, LANES), F32),),
        flops=3 * 10**9,
    )


def outputs(back, query, key, value, grad):
    block = jax.ShapeDtypeStruct(query.shape, BF16)
    return call(
        output_kernel,
        (block,) * 5,
        (back, query, key, value, grad),
        [pltpu.VMEM(query.shape, BF16)] * 5 + [pltpu.SemaphoreType.DMA((GROUPS, 5))],
        out_hbm=True,
    )


def on_device(query_in, key_in, value_in, filter_taps, skip_gain, grad_out):
    seq_count, pair = lax.axis_size("y") * lax.axis_size("x"), lax.axis_size("pl")
    peers = seq_count * pair
    rows_dev, chan_dev = query_in.shape[1:]
    own = chan_dev // peers
    batch = query_in.shape[0] * lax.axis_size("dh") * lax.axis_size("dm") * pair
    factor = 1.0 / math.sqrt(batch * seq_count * rows_dev)
    query, key, value, grad = query_in[0], key_in[0], value_in[0], grad_out[0]

    def swap(values, axes):
        return lax.all_to_all(values, axes, split_axis=0, concat_axis=0, tiled=True)

    signals = swap(gate(query, key, value, grad, filter_taps, peers), ("pl", "x", "y"))

    def exchange(values, axis):
        return lax.ppermute(values, axis, [(0, 1), (1, 0)])

    def plus(a, b):
        return (a.astype(F32) + b.astype(F32)).astype(BF16)

    spectra, (given, term) = zip(*(taps_grad(signals, kept, factor) for kept in range(2)))
    term = plus(term, exchange(given, "dm"))
    term = plus(*lax.all_gather(term, "dh"))
    other = exchange(term, "dm")
    spectra, _ = lax.optimization_barrier((spectra, term))
    results = states(signals, spectra, skip_gain, own)
    other, results = lax.optimization_barrier((other, results))
    copies = [jnp.broadcast_to(t[None], (pair,) + t.shape).reshape((peers,) + t.shape[1:]) for t in (term, other)]
    back = swap(jnp.concatenate([results, *copies], axis=1), ("pl", "x", "y"))
    outs = outputs(back, query, key, value, grad)
    return tuple(out[None] for out in outs[:4]) + (outs[4],)


def solution(mesh):
    dp, chan, seq = (mesh.shape[name] for name in ("dp", "chan", "seq"))
    split_mesh = Mesh(
        mesh.devices.reshape(dp // 4, 2, 2, chan, seq // SIDE, SIDE),
        ("dh", "dm", "pl", "chan", "y", "x"),
    )
    rows = P(("dh", "dm", "pl"), ("y", "x"), "chan")
    taps = P(("y", "x"), "chan")
    return jax.shard_map(
        on_device,
        mesh=split_mesh,
        in_specs=(rows, rows, rows, taps, P("chan"), rows),
        out_specs=(rows, rows, rows, rows, taps),
        check_vma=False,
    )
```
